128 devices in a mesh: seq: 32 (over y_hi, x, z), dp: 4 (over y_lo, core).
Axes of the slice: x: 4, y: 4 (y_hi: 2, y_lo: 2; y = y_hi * 2 + y_lo), z: 4, core: 2. Of those that a mesh axis runs over, the one named last changes fastest.
Arguments:
- teacher_rows: bfloat16 [8192, 8192], P('seq', 'dp'), may hold values from -6 to 6
- teacher_next: bfloat16 [8192, 8192], P('seq', 'dp'), may hold values from -9 to 9
- state_proj: bfloat16 [8192, 256], replicated, may hold values from -0.015625 to 0.015625
- step_proj: bfloat16 [8192, 64], replicated, may hold values from -0.0625 to 0.0625
- rate_log: float32 [64], replicated, may hold values from -12 to 1.2
- step_bias: float32 [64], replicated, may hold values from -1 to 0
- skip_gain: float32 [64], replicated, may hold values from 0.5 to 1.5
Outputs:
- loss_value: float32 [], replicated
- state_proj_grad: float32 [8192, 256], P('dp')
- step_proj_grad: float32 [8192, 64], P('dp')
- rate_log_grad: float32 [64], replicated
- step_bias_grad: float32 [64], replicated
- skip_gain_grad: float32 [64], replicated
The draws below stay inside these ranges and needn't reach their ends.
All inputs are finite; a program needn't handle non-finite values.
Results may differ from the reference program's by a relative error of at most 0.011.
Values may be sent and summed in bfloat16 or wider, within the bound.
A program may use at most 128 MiB of HBM per device.

```python
import jax
import jax.numpy as jnp
from jax import lax

D = 8192
H = 64
N = 128
BLOCK = 256
LEN_DEV = 256
LEN = 8192


def normal_field(key):
    return jnp.clip(jax.random.normal(key, (LEN, D), jnp.float32), -6.0, 6.0)


def draw_teacher_rows(key, part):
    rows = normal_field(key)
    return rows.astype(jnp.bfloat16)


def draw_teacher_next(key, part):
    rows = normal_field(key)
    key = jax.random.fold_in(key, 5)
    result = rows + 0.5 * normal_field(key)
    return result.astype(jnp.bfloat16)


def draw_rate_log(key, part):
    key = jax.random.fold_in(key, 11)
    pick_key, slow_key, fast_key = jax.random.split(key, 3)
    slow_share = 0.5
    slow_heads = jax.random.uniform(pick_key, (H,)) < slow_share
    slow_log = jnp.log(1.0 / LEN) + jnp.log(3.0) * jax.random.uniform(slow_key, (H,))
    fast_log = jnp.log(0.011) + (jnp.log(0.035) - jnp.log(0.011)) * jax.random.uniform(fast_key, (H,))
    return jnp.where(slow_heads, slow_log, fast_log).astype(jnp.float32)


def bell_draw(own_key, dims, deviation, most, held_as=jnp.bfloat16):
    return jnp.clip(deviation * jax.random.normal(own_key, dims, jnp.float32), -most, most).astype(held_as)


def setup_inputs(seed: int = 0) -> dict:
    seeds = jax.random.split(jax.random.key(seed), 8)
    teacher_rows = draw_teacher_rows(jax.random.fold_in(seeds[7], 71), 0)
    teacher_next = draw_teacher_next(jax.random.fold_in(seeds[7], 71), 0)
    state_proj = bell_draw(seeds[2], (D, 2 * N), (16 * D) ** -0.5, 0.015625)
    step_proj = bell_draw(seeds[3], (D, H), D ** -0.5, 0.0625)
    rate_log = draw_rate_log(jax.random.fold_in(seeds[7], 71), 0)
    step_bias = jnp.clip(jax.random.uniform(seeds[5], (H,), jnp.float32, -1.0, 0.0), -1.0, 0.0)
    skip_gain = jnp.clip(1.0 + 0.1 * jax.random.normal(seeds[6], (H,), jnp.float32), 0.5, 1.5)
    return dict(teacher_rows=teacher_rows, teacher_next=teacher_next, state_proj=state_proj, step_proj=step_proj, rate_log=rate_log, step_bias=step_bias, skip_gain=skip_gain)


def block_terms(bc_block, dt_block, rate_log, step_bias):
    state_width = bc_block.shape[1] // 2
    rounded = bc_block.astype(jnp.bfloat16)
    dt_steps = jax.nn.softplus(dt_block + step_bias)
    log_decay = jnp.cumsum(-jnp.exp(rate_log) * dt_steps, axis=0)
    return (rounded[:, :state_width], rounded[:, state_width:], dt_steps, log_decay)

def block_state(rows_block, b_input, dt_steps, log_decay, head_count):
    block_rows, model_width = rows_block.shape
    decay_total = log_decay[-1]
    weighting = dt_steps * jnp.exp(decay_total - log_decay)
    scaled_rows = (rows_block.reshape(block_rows, head_count, -1) * weighting[:, :, None]).reshape(block_rows, model_width).astype(jnp.bfloat16)
    increment = jnp.dot(scaled_rows.T, b_input, preferred_element_type=jnp.float32)
    return (jnp.exp(decay_total), increment)

def block_output(rows_block, b_input, c_output, dt_steps, log_decay, skip_gain, carry_state, head_count):
    block_rows, model_width = rows_block.shape
    scores = jnp.dot(c_output, b_input.T, preferred_element_type=jnp.float32)
    row_index = jnp.arange(block_rows)[:, None]
    col_index = jnp.arange(block_rows)[None, :]
    causal = (row_index >= col_index)[None]
    log_gap = log_decay.T[:, :, None] - log_decay.T[:, None, :]
    weights = jnp.where(causal, jnp.exp(jnp.where(causal, log_gap, 0.0)), 0.0) * scores[None] * dt_steps.T[:, None, :]
    weights = weights.astype(jnp.bfloat16)
    inputs = rows_block.reshape(block_rows, head_count, -1)
    inner_term = jnp.einsum('hts,shp->thp', weights.astype(jnp.float32), inputs.astype(jnp.float32))
    carried = jnp.dot(c_output.astype(jnp.float32), carry_state.T, precision=lax.Precision.HIGHEST)
    output = inner_term + carried.reshape(inner_term.shape) * jnp.exp(log_decay)[:, :, None] + skip_gain[None, :, None] * inputs
    return output.reshape(block_rows, model_width)

def reference(teacher_rows, teacher_next, state_proj, step_proj, rate_log, step_bias, skip_gain):
    seq_rows, model_width = teacher_rows.shape
    head_count = rate_log.shape[0]
    state_width = state_proj.shape[1] // 2
    block_rows = min(BLOCK, LEN_DEV)
    block_count = seq_rows // block_rows
    proj_bc = jnp.dot(teacher_rows, state_proj, preferred_element_type=jnp.float32)
    proj_dt = jnp.dot(teacher_rows, step_proj, preferred_element_type=jnp.float32)

    def objective(proj_bc, proj_dt, rate_log, step_bias, skip_gain):

        def advance(carry_state, block_items):
            rows_block, target_block, bc_block, dt_block = block_items
            b_input, c_output, dt_steps, log_decay = block_terms(bc_block, dt_block, rate_log, step_bias)
            output = block_output(rows_block, b_input, c_output, dt_steps, log_decay, skip_gain, carry_state, head_count)
            decays, increment = block_state(rows_block, b_input, dt_steps, log_decay, head_count)
            errors = output - target_block.astype(jnp.float32)
            new_state = jnp.repeat(decays, model_width // head_count)[:, None] * carry_state + increment
            return (new_state, jnp.sum(errors * errors))
        advance = jax.checkpoint(advance)
        start_state = jnp.zeros((model_width, state_width), jnp.float32)
        _, block_sums = lax.scan(advance, start_state, (teacher_rows.reshape(block_count, block_rows, model_width), teacher_next.reshape(block_count, block_rows, model_width), proj_bc.reshape(block_count, block_rows, 2 * state_width), proj_dt.reshape(block_count, block_rows, head_count)))
        return jnp.sum(block_sums) / (2.0 * seq_rows)
    value, grads = jax.value_and_grad(objective, argnums=(0, 1, 2, 3, 4))(proj_bc, proj_dt, rate_log, step_bias, skip_gain)
    grad_bc, grad_dt, grad_rate, grad_bias, grad_skip = grads
    proj_grads = jnp.concatenate([grad_bc, grad_dt], axis=1).astype(jnp.bfloat16)
    full_term = lax.dot_general(teacher_rows, proj_grads, (((0,), (0,)), ((), ())), preferred_element_type=jnp.float32)
    return (value / model_width, full_term[:, :2 * state_width], full_term[:, 2 * state_width:], grad_rate, grad_bias, grad_skip)
```

```python
import functools

import jax
import jax.numpy as jnp
from jax import lax
from jax.experimental import pallas as pl
from jax.experimental.pallas import tpu as pltpu
from jax.sharding import PartitionSpec as P

SEQ, DP = 32, 4
T = 256
WIDTH = 2048
HEADS = 64
PAIRS = 8
N = 128
PIECE = 64
MESH = pl.DeviceIdType.MESH
BF, F32 = jnp.bfloat16, jnp.float32
SCALE = 1.0 / 8192.0


def dot(a, b):
    return jnp.dot(a, b, preferred_element_type=F32)


def dot_nt(a, b):
    return lax.dot_general(a, b, (((1,), (1,)), ((), ())), preferred_element_type=F32)


def split3(v):
    hi = v.astype(BF).astype(F32)
    rest = v - hi
    mid = rest.astype(BF).astype(F32)
    return hi, mid, rest - mid


def tri_sum(tri, v):
    return sum(dot(tri, part.astype(BF)) for part in split3(v))


def send(src, dst, send_sem, recv_sem, device):
    pltpu.make_async_remote_copy(
        src_ref=src, dst_ref=dst, send_sem=send_sem, recv_sem=recv_sem,
        device_id=device, device_id_type=MESH,
    ).start()


def wait_for(ref, sem):
    pltpu.make_async_copy(ref, ref, sem).wait()


def loop(count, body):
    lax.fori_loop(0, count, lambda k, c: (body(k), c)[1], 0)


def pack_rows(v):
    return jnp.concatenate([v[:32], v[32:]], axis=1)


def unpack_rows(ref):
    parts = []
    for q in range(DP):
        parts += [ref[q][:, :64], ref[q][:, 64:]]
    return jnp.concatenate(parts, axis=0)


def kernel(
    x_ref, tgt_ref, sp_ref, st_ref, rate_ref, bias_ref, skip_ref,
    out_ref, small_ref,
    w_bc, w_dt, xt_ref,
    p_bc, p_dt, r_bc, r_dt, f_bc, f_dt,
    p2_bc, p2_dt, r2_bc, r2_dt, f2_bc, f2_dt,
    stack_ref, rows_ref, cx_ref, sk_ref, sc_ref, xdt_ref, l_ref, z_ref, err_ref, de_ref,
    sm_ref, dsc_ref, dc_ref, db_ref, k_ref, a_ref, dw_ref, acc_ref,
    es_ref, re_ref, sf_ref, rs_ref, gs_ref, rg_ref, sh_ref, rh_ref, dec_ref,
    ws_ref, rw_ref, sums_ref, sroot_ref, sdp_ref, sfin_ref,
    ssem, rsem, lsem,
):
    me, dq = lax.axis_index("seq"), lax.axis_index("dp")
    head0 = dq * (HEADS // DP)

    def peer(k):
        return lax.rem(me + k, SEQ)

    def member(k):
        return lax.rem(dq + k, DP)

    barrier = pltpu.get_barrier_semaphore()
    loop(SEQ - 1, lambda k: pl.semaphore_signal(
        barrier, inc=1, device_id=(peer(k + 1), dq), device_id_type=MESH))
    loop(DP - 1, lambda k: pl.semaphore_signal(
        barrier, inc=1, device_id=(me, member(k + 1)), device_id_type=MESH))

    own = pl.ds(pl.multiple_of(dq * WIDTH, WIDTH), WIDTH)
    load_bc = pltpu.make_async_copy(sp_ref.at[own], w_bc, lsem.at[0])
    load_dt = pltpu.make_async_copy(st_ref.at[own], w_dt, lsem.at[1])
    load_bc.start()
    load_dt.start()
    load_bc.wait()
    load_dt.wait()

    def dp_sum(bc, dt, p_bc, p_dt, r_bc, r_dt, f_bc, f_dt, sem):
        for q in range(DP):
            p_bc[q] = bc[64 * q : 64 * q + 64].astype(BF)
            p_dt[q] = pack_rows(dt[64 * q : 64 * q + 64])
        if sem == 0:
            pl.semaphore_wait(barrier, SEQ + DP - 2)
        for k in range(1, DP):
            q = member(k)
            send(p_bc.at[q], r_bc.at[dq], ssem.at[sem], rsem.at[sem], (me, q))
            send(p_dt.at[q], r_dt.at[dq], ssem.at[sem + 1], rsem.at[sem + 1], (me, q))
        r_bc[dq] = p_bc[dq]
        r_dt[dq] = p_dt[dq]
        wait_for(r_bc.at[pl.ds(0, DP - 1)], rsem.at[sem])
        wait_for(r_dt.at[pl.ds(0, DP - 1)], rsem.at[sem + 1])
        f_bc[dq] = sum(r_bc[q].astype(F32) for q in range(DP)).astype(BF)
        f_dt[dq] = sum(r_dt[q] for q in range(DP))
        for k in range(1, DP):
            q = member(k)
            send(f_bc.at[dq], f_bc.at[dq], ssem.at[sem + 2], rsem.at[sem + 2], (me, q))
            send(f_dt.at[dq], f_dt.at[dq], ssem.at[sem + 3], rsem.at[sem + 3], (me, q))
        wait_for(f_bc.at[pl.ds(0, DP - 1)], rsem.at[sem + 2])
        wait_for(f_dt.at[pl.ds(0, DP - 1)], rsem.at[sem + 3])

    x_all = x_ref[...]
    dp_sum(dot(x_all, w_bc[...]), dot(x_all, w_dt[...]),
           p_bc, p_dt, r_bc, r_dt, f_bc, f_dt, 0)

    bc = f_bc[...].reshape(T, 2 * N)
    b_in, c_out = bc[:, :N], bc[:, N:]
    b_t = b_in.astype(F32).T.astype(BF)
    c_t = c_out.astype(F32).T.astype(BF)
    pre = unpack_rows(f_dt) + bias_ref[...]
    dt = jnp.maximum(pre, 0.0) + jnp.log1p(jnp.exp(-jnp.abs(pre)))
    rate = jnp.exp(rate_ref[...])
    log_rate = -rate * dt
    row_i = lax.broadcasted_iota(jnp.int32, (T, T), 0)
    col_i = lax.broadcasted_iota(jnp.int32, (T, T), 1)
    tri = jnp.where(row_i >= col_i, 1.0, 0.0).astype(BF)
    cum = tri_sum(tri, log_rate)
    cend = cum[T - 1 : T]
    rows_ref[...] = jnp.concatenate([cum, dt], axis=1).T
    skip8 = jnp.broadcast_to(skip_ref[...], (16, HEADS))
    for at, v in ((0, cum), (T, dt), (2 * T, skip8)):
        stack_ref[at : at + v.shape[0]] = jnp.concatenate(split3(v), axis=1).astype(BF)
    sel_row = lax.rem(lax.broadcasted_iota(jnp.int32, (3 * HEADS, 2 * N), 0), HEADS)
    sel_col = lax.broadcasted_iota(jnp.int32, (3 * HEADS, 2 * N), 1) // N

    def cols(hp):
        return pl.ds(pl.multiple_of(hp * 2 * N, 2 * N), 2 * N)

    def start_pair(k):
        return lax.rem(me // 4 + k, PAIRS)

    def send_pair(hp, src, dst, sem):
        for i in range(4):
            o = 4 * hp + i

            @pl.when(o != me)
            def _():
                send(src.at[o], dst.at[me], ssem.at[sem], rsem.at[sem], (o, dq))

    def put_pair(ref, hp, value):
        for i in range(4):
            half, j = i % 2, i // 2
            ref[4 * hp + i, 0:PIECE] = value[
                half * PIECE : (half + 1) * PIECE, j * N : (j + 1) * N].astype(BF)

    def get_pair(ref, hp):
        v = ref[pl.ds(4 * hp, 4)]
        return jnp.concatenate([v[:2].reshape(N, N), v[2:].reshape(N, N)], axis=1)

    def increments(k):
        hp = start_pair(k)
        sel = jnp.where(sel_row == head0 + 2 * hp + sel_col, 1.0, 0.0).astype(BF)
        wide = dot(stack_ref[...], sel)
        cx, dx = wide[:T], wide[T : 2 * T]
        cx_ref[hp] = cx
        sk_ref[hp] = wide[2 * T : 2 * T + 8]
        xp = x_ref[:, cols(hp)].astype(F32)
        xd = xp * dx
        xdt_ref[hp] = xd.astype(BF)
        last = cx[T - 1 : T]
        sc = (xd * jnp.exp(last - cx)).astype(BF)
        sc_ref[hp] = sc
        put_pair(es_ref, hp, dot(b_t, sc))
        hi = last.astype(BF).astype(F32)
        both = jnp.concatenate(
            [jnp.broadcast_to(hi, (8, 2 * N)), jnp.broadcast_to(last - hi, (8, 2 * N))], axis=0
        ).astype(BF)
        for i in range(4):
            es_ref[4 * hp + i, PIECE : PIECE + 16] = both[:, (i // 2) * N : (i // 2 + 1) * N]
        send_pair(hp, es_ref, re_ref, 4)

    loop(PAIRS, increments)
    re_ref[me] = es_ref[me]

    sm_ref[...] = jnp.where(row_i >= col_i, dot_nt(c_out, b_in), 0.0)

    def in_block(hp):
        parts = []
        for j in range(2):
            cx = cx_ref[hp, :, j * N : (j + 1) * N]
            gap = jnp.concatenate([cx, cx], axis=1) - rows_ref[pl.ds(head0 + 2 * hp + j, 1), :]
            decay = jnp.exp(jnp.minimum(gap, 0.0))
            l_ref[2 * hp + j] = decay.astype(BF)
            w = (decay * sm_ref[...]).astype(BF)
            parts.append(dot(w, xdt_ref[hp, :, j * N : (j + 1) * N]))
        z_ref[hp] = jnp.concatenate(parts, axis=1)

    loop(PAIRS, in_block)

    wait_for(re_ref.at[pl.ds(0, SEQ - 1)], rsem.at[4])

    def forward(j, state):
        sf_ref[j] = state.reshape(PIECE, N).astype(BF)
        tail = re_ref[j, PIECE : PIECE + 16].astype(F32)
        decay = jnp.exp(tail[:8] + tail[8:])
        dec_ref[j] = decay
        return decay[None] * state + re_ref[j, 0:PIECE].astype(F32).reshape(8, 8, N)

    lax.fori_loop(0, SEQ, forward, jnp.zeros((8, 8, N), F32))
    loop(SEQ - 1, lambda k: send(
        sf_ref.at[peer(k + 1)], rs_ref.at[me], ssem.at[5], rsem.at[5], (peer(k + 1), dq)))
    rs_ref[me] = sf_ref[me]

    def turn(i):
        at = pl.ds(pl.multiple_of(i * 2 * N, 2 * N), 2 * N)
        xt_ref[at, :] = x_ref[:, at].astype(F32).T.astype(BF)

    loop(PAIRS, turn)
    acc_ref[...] = jnp.zeros_like(acc_ref)
    wait_for(rs_ref.at[pl.ds(0, SEQ - 1)], rsem.at[5])

    def errors(k):
        hp = start_pair(k)
        at = cols(hp)
        decay = jnp.exp(cx_ref[hp])
        z = z_ref[hp] + dot(c_out, get_pair(rs_ref, hp)) * decay
        z_ref[hp] = z
        err = (z + sk_ref[hp][:1] * x_ref[:, at].astype(F32)) - tgt_ref[:, at].astype(F32)
        err_ref[hp] = err
        de = (err * decay).astype(BF)
        de_ref[hp] = de
        put_pair(gs_ref, hp, dot(c_t, de))
        send_pair(hp, gs_ref, rg_ref, 6)
        acc_ref[0:8] += jnp.sum((err * err).reshape(T // 8, 8, 2 * N), axis=0)

    loop(PAIRS, errors)
    rg_ref[me] = gs_ref[me]

    lane = lax.broadcasted_iota(jnp.int32, (T, HEADS), 1)
    lane1 = lax.broadcasted_iota(jnp.int32, (1, HEADS), 1)
    for ref in (dsc_ref, dc_ref, db_ref, k_ref, a_ref, dw_ref):
        ref[...] = jnp.zeros_like(ref)
    acc_ref[8:16] = jnp.zeros((8, 2 * N), F32)

    def grads_in_block(hp):
        at = cols(hp)
        xp = x_ref[:, at]
        err = err_ref[hp]
        errb = err.astype(BF)
        dc_ref[...] += dot_nt(de_ref[hp], get_pair(rs_ref, hp))
        rowed = err * z_ref[hp]
        skipped = jnp.sum(err * xp.astype(F32), axis=0, keepdims=True)
        for j in range(2):
            head = head0 + 2 * hp + j
            sub = slice(j * N, (j + 1) * N)
            dwd = dot_nt(errb[:, sub], xp[:, sub]) * l_ref[2 * hp + j].astype(F32)
            dsc_ref[...] += dwd * rows_ref[pl.ds(HEADS + head, 1), :]
            k_ref[pl.ds(head, 1), :] = jnp.sum(dwd * sm_ref[...], axis=0, keepdims=True)
            a_ref[...] += jnp.where(
                lane == head, jnp.sum(rowed[:, sub], axis=1, keepdims=True), 0.0)
            acc_ref[8:9, :HEADS] += jnp.where(
                lane1 == head, jnp.sum(skipped[:, sub], axis=1, keepdims=True), 0.0)

    loop(PAIRS, grads_in_block)
    dsc = jnp.where(row_i >= col_i, dsc_ref[...], 0.0)
    dc_ref[...] += dot(dsc.astype(BF), b_in)
    db_ref[...] += dot(dsc.T.astype(BF), c_out)

    wait_for(rg_ref.at[pl.ds(0, SEQ - 1)], rsem.at[6])

    def backward(i, state):
        j = SEQ - 1 - i
        sh_ref[j] = state.reshape(PIECE, N).astype(BF)
        return dec_ref[j][None] * state + rg_ref[j].astype(F32).reshape(8, 8, N)

    lax.fori_loop(0, SEQ, backward, jnp.zeros((8, 8, N), F32))
    loop(SEQ - 1, lambda k: send(
        sh_ref.at[peer(k + 1)], rh_ref.at[me], ssem.at[7], rsem.at[7], (peer(k + 1), dq)))
    rh_ref[me] = sh_ref[me]
    k_cols = k_ref[...].T[:, :HEADS]
    wait_for(rh_ref.at[pl.ds(0, SEQ - 1)], rsem.at[7])

    def grads_of_state(hp):
        after = get_pair(rh_ref, hp)
        db_ref[...] += dot_nt(sc_ref[hp], after)
        weighed = dot(b_in, after) * x_ref[:, cols(hp)].astype(F32)
        decayed = jnp.sum(
            after.astype(F32) * get_pair(rs_ref, hp).astype(F32), axis=0, keepdims=True)
        for j in range(2):
            head = head0 + 2 * hp + j
            sub = slice(j * N, (j + 1) * N)
            dw_ref[...] += jnp.where(
                lane == head, jnp.sum(weighed[:, sub], axis=1, keepdims=True), 0.0)
            acc_ref[9:10, :HEADS] += jnp.where(
                lane1 == head, jnp.sum(decayed[:, sub], axis=1, keepdims=True), 0.0)

    loop(PAIRS, grads_of_state)

    left = jnp.exp(cend - cum)
    d_weight = dw_ref[...] * left
    d_gap = d_weight * dt
    d_end = jnp.sum(d_gap, axis=0, keepdims=True) + jnp.exp(cend) * acc_ref[9:10, :HEADS]
    d_cum = a_ref[...] - k_cols * dt - d_gap
    tri_up = jnp.where(row_i <= col_i, 1.0, 0.0).astype(BF)
    d_log = tri_sum(tri_up, d_cum) + d_end
    d_dt = k_cols + d_weight - rate * d_log
    d_pre = d_dt / (1.0 + jnp.exp(-pre)) * SCALE
    loss = jnp.sum(jnp.sum(acc_ref[0:8], axis=0, keepdims=True), axis=1, keepdims=True)
    zero = jnp.zeros((1, HEADS), F32)
    small = jnp.concatenate([
        jnp.broadcast_to(loss * (SCALE * SCALE * 0.5), (1, HEADS)),
        jnp.sum(d_log * log_rate, axis=0, keepdims=True) * SCALE,
        jnp.sum(d_pre, axis=0, keepdims=True),
        acc_ref[8:9, :HEADS] * SCALE,
        zero, zero, zero, zero], axis=0)
    sums_ref[...] = jnp.concatenate([small, jnp.zeros_like(small)], axis=1)

    @pl.when(me != 0)
    def _():
        send(sums_ref, sroot_ref.at[me], ssem.at[14], rsem.at[14], (0, dq))

    d_bc = jnp.concatenate([db_ref[...], dc_ref[...]], axis=1) * SCALE
    dp_sum(d_bc, d_pre, p2_bc, p2_dt, r2_bc, r2_dt, f2_bc, f2_dt, 8)

    g_bc = f2_bc[...].reshape(T, 2 * N)
    g_dt = unpack_rows(f2_dt)
    none = jnp.zeros_like(g_dt)
    g_at = [
        jnp.concatenate([g_dt if i == k else none for i in range(4)], axis=1).astype(BF)
        for k in range(4)
    ]

    def weight_terms(k):
        g = lax.rem(me // 8 + k, 4)
        part = xt_ref[pl.ds(pl.multiple_of(g * 512, 512), 512), :]
        slots = pl.ds(8 * g, 8)
        ws_ref[slots, 0:PIECE, :] = dot(part, g_bc).astype(BF).reshape(8, PIECE, 2 * N)
        part = part.reshape(8, 4, 16, T)
        packed = sum(dot(part[:, i].reshape(128, T), g_at[i]) for i in range(4))
        ws_ref[slots, PIECE : PIECE + 16, :] = packed.astype(BF).reshape(8, 16, 2 * N)

        def one(i):
            o = 8 * g + lax.rem(me + i, 8)

            @pl.when(o != me)
            def _():
                send(ws_ref.at[o], rw_ref.at[me], ssem.at[12], rsem.at[12], (o, dq))

        loop(8, one)

    loop(4, weight_terms)
    rw_ref[me] = ws_ref[me]

    @pl.when(me == 0)
    def _():
        sroot_ref[0] = sums_ref[...]
        wait_for(sroot_ref.at[pl.ds(0, SEQ - 1)], rsem.at[14])
        sdp_ref[dq] = jnp.sum(sroot_ref[...], axis=0)
        for k in range(1, DP):
            send(sdp_ref.at[dq], sdp_ref.at[dq], ssem.at[15], rsem.at[15], (me, member(k)))

    wait_for(rw_ref.at[pl.ds(0, SEQ - 1)], rsem.at[12])
    total = lax.fori_loop(
        1, SEQ, lambda j, s: s + rw_ref[j].astype(F32), rw_ref[0].astype(F32))
    out_ref[me] = total.astype(BF)
    loop(SEQ - 1, lambda k: send(
        out_ref.at[me], out_ref.at[me], ssem.at[13], rsem.at[13], (peer(k + 1), dq)))

    @pl.when(me == 0)
    def _():
        wait_for(sdp_ref.at[pl.ds(0, DP - 1)], rsem.at[15])
        sfin_ref[...] = jnp.sum(sdp_ref[...], axis=0)
        loop(SEQ - 1, lambda k: send(
            sfin_ref, sfin_ref, ssem.at[16], rsem.at[16], (peer(k + 1), dq)))
        wait_for(sdp_ref.at[pl.ds(0, DP - 1)], ssem.at[15])
        wait_for(sroot_ref.at[pl.ds(0, SEQ - 1)], ssem.at[16])

    @pl.when(me != 0)
    def _():
        wait_for(sums_ref, ssem.at[14])
        wait_for(sfin_ref, rsem.at[16])

    small_ref[...] = sfin_ref[...]
    wait_for(out_ref.at[pl.ds(0, SEQ - 1)], rsem.at[13])

    for sem, ref in ((0, r_bc), (1, r_dt), (2, f_bc), (3, f_dt),
                     (8, r2_bc), (9, r2_dt), (10, f2_bc), (11, f2_dt)):
        wait_for(ref.at[pl.ds(0, DP - 1)], ssem.at[sem])
    for sem, ref in ((4, es_ref), (5, sf_ref), (6, gs_ref), (7, sh_ref), (12, ws_ref), (13, out_ref)):
        wait_for(ref.at[pl.ds(0, SEQ - 1)], ssem.at[sem])


def shards(teacher_rows, teacher_next, state_proj, step_proj, rate_log, step_bias, skip_gain):
    vmem = pl.BlockSpec(memory_space=pltpu.VMEM)
    hbm = pl.BlockSpec(memory_space=pl.ANY)

    def buf(*shape, dtype=BF):
        return pltpu.VMEM(shape, dtype)

    def f32(*shape):
        return pltpu.VMEM(shape, F32)

    dp_bufs = [
        buf(DP, 64, 2 * N), f32(DP, 32, 128), buf(DP, 64, 2 * N), f32(DP, 32, 128),
        buf(DP, 64, 2 * N), f32(DP, 32, 128),
    ]
    scratch = [
        buf(WIDTH, 2 * N), buf(WIDTH, HEADS), buf(WIDTH, T),
        *dp_bufs, *dp_bufs,
        buf(2 * T + 16, 3 * HEADS), f32(2 * HEADS, T),
        f32(PAIRS, T, 2 * N), f32(PAIRS, 8, 2 * N), buf(PAIRS, T, 2 * N), buf(PAIRS, T, 2 * N),
        buf(2 * PAIRS, T, T), f32(PAIRS, T, 2 * N), f32(PAIRS, T, 2 * N), buf(PAIRS, T, 2 * N),
        f32(T, T), f32(T, T), f32(T, N), f32(T, N), f32(2 * HEADS, T), f32(T, HEADS), f32(T, HEADS),
        f32(16, 2 * N),
        buf(SEQ, PIECE + 16, N), buf(SEQ, PIECE + 16, N),
        buf(SEQ, PIECE, N), buf(SEQ, PIECE, N), buf(SEQ, PIECE, N), buf(SEQ, PIECE, N),
        buf(SEQ, PIECE, N), buf(SEQ, PIECE, N), f32(SEQ, 8, N),
        buf(SEQ, PIECE + 16, 2 * N), buf(SEQ, PIECE + 16, 2 * N),
        f32(8, 128), f32(SEQ, 8, 128), f32(DP, 8, 128), f32(8, 128),
        pltpu.SemaphoreType.DMA((17,)), pltpu.SemaphoreType.DMA((17,)),
        pltpu.SemaphoreType.DMA((2,)),
    ]
    out, small = pl.pallas_call(
        kernel,
        out_shape=(
            jax.ShapeDtypeStruct((SEQ, PIECE + 16, 2 * N), BF),
            jax.ShapeDtypeStruct((8, 128), F32),
        ),
        in_specs=[vmem, vmem, hbm, hbm, vmem, vmem, vmem],
        out_specs=(vmem, vmem),
        scratch_shapes=scratch,
        compiler_params=pltpu.CompilerParams(
            collective_id=0, has_side_effects=True, vmem_limit_bytes=48 * 1024 * 1024),
    )(teacher_rows, teacher_next, state_proj, step_proj,
      rate_log[None], step_bias[None], skip_gain[None])
    state_grad = out[:, :PIECE].reshape(WIDTH, 2 * N).astype(F32)
    step_grad = (
        out[:, PIECE:].reshape(SEQ, 16, 4, HEADS).transpose(0, 2, 1, 3)
        .reshape(WIDTH, HEADS).astype(F32)
    )
    return (small[0, 0], state_grad, step_grad,
            small[1, :HEADS], small[2, :HEADS], small[3, :HEADS])


def solution(mesh):
    placed = (P("seq", "dp"), P("seq", "dp"), P(), P(), P(), P(), P())
    return jax.shard_map(
        shards,
        mesh=mesh,
        in_specs=placed,
        out_specs=(P(), P("dp", None), P("dp", None), P(), P(), P()),
        check_vma=False,
    )
```

```python
import functools

import jax
import jax.numpy as jnp
from jax import lax
from jax.experimental import pallas as pl
from jax.experimental.pallas import tpu as pltpu
from jax.sharding import PartitionSpec as P

SEQ, DP = 32, 4
T = 256
WIDTH = 2048
HEADS = 64
PAIRS = 8
N = 128
PIECE = 64
MESH = pl.DeviceIdType.MESH
BF, F32 = jnp.bfloat16, jnp.float32
SCALE = 1.0 / 8192.0


def dot(a, b):
    return jnp.dot(a, b, preferred_element_type=F32)


def dot_nt(a, b):
    return lax.dot_general(a, b, (((1,), (1,)), ((), ())), preferred_element_type=F32)


def split3(v):
    hi = v.astype(BF).astype(F32)
    rest = v - hi
    mid = rest.astype(BF).astype(F32)
    return hi, mid, rest - mid


def tri_sum(tri, v):
    return sum(dot(tri, part.astype(BF)) for part in split3(v))


def send(src, dst, send_sem, recv_sem, device):
    pltpu.make_async_remote_copy(
        src_ref=src, dst_ref=dst, send_sem=send_sem, recv_sem=recv_sem,
        device_id=device, device_id_type=MESH,
    ).start()


def wait_for(ref, sem):
    pltpu.make_async_copy(ref, ref, sem).wait()


def loop(count, body):
    lax.fori_loop(0, count, lambda k, c: (body(k), c)[1], 0)


def pack_rows(v):
    return jnp.concatenate([v[:64], v[64:]], axis=1)


def unpack_rows(ref):
    return jnp.concatenate([ref[i][:, j : j + 64] for i in range(2) for j in (0, 64)], axis=0)


def kernel(
    x_hbm, tgt_hbm, sp_ref, st_ref, rate_ref, bias_ref, skip_ref,
    wbc_ref, wdt_ref, small_ref,
    x_ref, tgt_ref, w_bc, w_dt, xt_ref,
    m1_tmp, m1_sa, m1_ra, m1_sb, m1_rb, m1_f,
    d1_tmp, d1_sa, d1_ra, d1_sb, d1_rb, d1_f,
    m2_tmp, m2_sa, m2_ra, m2_sb, m2_rb, m2_f,
    m3_tmp, m3_sa, m3_ra, m3_sb, m3_rb, m3_f,
    stack_ref, skips_ref, rows_ref, cx_ref, sk_ref, sc_ref, xdt_ref, l_ref, z_ref, err_ref, de_ref,
    sm_ref, dsc_ref, dc_ref, db_ref, k_ref, a_ref, dw_ref, acc_ref,
    ce_ref, es_ref, re_ref, sf_ref, rs_ref, gs_ref, rg_ref, sh_ref, rh_ref, dec_ref,
    wsc_ref, rwc_ref, wsb_ref, rwb_ref, sums_ref, sroot_ref, sdp_ref, sfin_ref,
    ssem, rsem, s_rsem, h_rsem, lsem, go,
):
    me, dq = lax.axis_index("seq"), lax.axis_index("dp")
    head0 = dq * (HEADS // DP)
    core = lax.rem(dq, 2)
    sibling = dq + 1 - 2 * core
    across = lax.rem(dq + 2, DP)

    def peer(k):
        return lax.rem(me + k, SEQ)

    def offset(dy, dx, dz):
        y, x, z = me // 16, lax.rem(me // 4, 4), lax.rem(me, 4)
        return lax.rem(y + dy, 2) * 16 + lax.rem(x + dx, 4) * 4 + lax.rem(z + dz, 4)

    def signal(sem, device):
        pl.semaphore_signal(sem, inc=1, device_id=device, device_id_type=MESH)

    def to_peers(start):
        def one(k):
            o = offset(1 - k // 16, lax.rem(2 + k // 4, 4), lax.rem(2 + k, 4))

            @pl.when(o != me)
            def _():
                start(o)

        loop(SEQ, one)

    own = pl.ds(pl.multiple_of(dq * WIDTH, WIDTH), WIDTH)
    load_x = pltpu.make_async_copy(x_hbm, x_ref, lsem.at[0])
    load_bc = pltpu.make_async_copy(sp_ref.at[own], w_bc, lsem.at[1])
    load_dt = pltpu.make_async_copy(st_ref.at[:, own], w_dt, lsem.at[2])
    load_tgt = pltpu.make_async_copy(tgt_hbm, tgt_ref, lsem.at[3])
    load_x.start()
    load_bc.start()
    load_dt.start()
    load_tgt.start()
    barrier = pltpu.get_barrier_semaphore()
    z_line = [(0, 0, k) for k in (1, 2, 3)]
    x_line = [(0, k, 0) for k in (1, 2, 3)]
    for k in range(1, DP):
        signal(barrier, (me, lax.rem(dq + k, DP)))
    for at in z_line + x_line + [(1, 0, 0)]:
        signal(barrier, (offset(*at), dq))
    load_x.wait()
    load_bc.wait()
    load_dt.wait()

    class DpSum:
        def __init__(self, sem, tmp, sa, ra, sb, rb, f):
            self.sem, self.tmp, self.sa, self.ra, self.sb, self.rb, self.f = sem, tmp, sa, ra, sb, rb, f

        def send(self, src, dst, step, member):
            send(src, dst, ssem.at[self.sem + step], rsem.at[self.sem + step], (me, member))

        def first(self):
            self.sa[...] = self.tmp[1 - core].astype(self.sa.dtype)
            self.send(self.sa, self.ra, 0, sibling)

        def second(self):
            wait_for(self.ra, rsem.at[self.sem])
            chip = self.tmp[core] + self.ra[...].astype(F32)
            self.tmp[core] = chip
            self.sb[...] = chip.astype(self.sb.dtype)
            self.send(self.sb, self.rb, 1, across)

        def third(self):
            wait_for(self.rb, rsem.at[self.sem + 1])
            self.f[core] = (self.tmp[core] + self.rb[...].astype(F32)).astype(self.f.dtype)
            self.send(self.f.at[core], self.f.at[core], 2, sibling)

        def last(self):
            wait_for(self.f.at[0], rsem.at[self.sem + 2])

        def sent(self):
            for step, ref in enumerate((self.sa, self.sb, self.f.at[0])):
                wait_for(ref, ssem.at[self.sem + step])

    sum_bc = DpSum(0, m1_tmp, m1_sa, m1_ra, m1_sb, m1_rb, m1_f)
    sum_dt = DpSum(3, d1_tmp, d1_sa, d1_ra, d1_sb, d1_rb, d1_f)
    sum_c = DpSum(6, m2_tmp, m2_sa, m2_ra, m2_sb, m2_rb, m2_f)
    sum_b = DpSum(9, m3_tmp, m3_sa, m3_ra, m3_sb, m3_rb, m3_f)

    x_all = x_ref[...]
    part_dt = dot_nt(x_all, w_dt[...])
    part_bc = dot(x_all, w_bc[...])
    for i in range(2):
        half = slice(128 * i, 128 * i + 128)
        d1_tmp[i] = pack_rows(part_dt[half])
        m1_tmp[i, 0:128] = part_bc[half, :N]
        m1_tmp[i, 128:256] = part_bc[half, N:]
    pl.semaphore_wait(barrier, DP - 1 + 7)
    sum_dt.first()
    sum_bc.first()
    for at in x_line:
        signal(go.at[0], (offset(*at), dq))
    sum_dt.second()
    sum_bc.second()
    pl.semaphore_wait(go.at[0], 3)
    signal(go.at[1], (offset(1, 0, 0), dq))
    sum_dt.third()
    sum_bc.third()
    sum_dt.last()
    sum_bc.last()

    b_in = m1_f[:, 0:128].reshape(T, N)
    c_out = m1_f[:, 128:256].reshape(T, N)
    pre = unpack_rows(d1_f) + bias_ref[...]
    dt = jnp.maximum(pre, 0.0) + jnp.log1p(jnp.exp(-jnp.abs(pre)))
    rate = jnp.exp(rate_ref[...])
    log_rate = -rate * dt
    row_i = lax.broadcasted_iota(jnp.int32, (T, T), 0)
    col_i = lax.broadcasted_iota(jnp.int32, (T, T), 1)
    tri = jnp.where(row_i >= col_i, 1.0, 0.0).astype(BF)
    cum = tri_sum(tri, log_rate)
    cend = cum[T - 1 : T]
    b_t = b_in.astype(F32).T.astype(BF)
    stack_ref[0:T] = jnp.concatenate(split3(cum), axis=1).astype(BF)
    stack_ref[T : 2 * T] = jnp.concatenate(split3(dt), axis=1).astype(BF)
    ce_ref[me] = jnp.concatenate([cend, cend], axis=1)
    pl.semaphore_wait(go.at[1], 1)
    loop(SEQ - 1, lambda k: send(
        ce_ref.at[me], ce_ref.at[me], ssem.at[12], rsem.at[12], (peer(k + 1), dq)))
    sel_row = lax.rem(lax.broadcasted_iota(jnp.int32, (3 * HEADS, 2 * N), 0), HEADS)
    sel_col = lax.broadcasted_iota(jnp.int32, (3 * HEADS, 2 * N), 1) // N

    def cols(hp):
        return pl.ds(pl.multiple_of(hp * 2 * N, 2 * N), 2 * N)

    def pick(hp):
        return jnp.where(sel_row == head0 + 2 * hp + sel_col, 1.0, 0.0).astype(BF)

    def send_pair(hp, src, dst, sem):
        for i in range(4):
            o = 4 * hp + i

            @pl.when(o != me)
            def _():
                send(src.at[o], dst.at[me], ssem.at[sem], rsem.at[sem], (o, dq))

    def wait_pair(hp, ref, sems):
        for i in range(4):
            o = 4 * hp + i

            @pl.when(o != me)
            def _():
                wait_for(ref.at[o], sems.at[o])

    def put_pair(ref, hp, value):
        for i in range(4):
            half, j = i % 2, i // 2
            ref[4 * hp + i] = value[
                half * PIECE : (half + 1) * PIECE, j * N : (j + 1) * N].astype(BF)

    def get_pair(ref, hp):
        v = ref[pl.ds(4 * hp, 4)]
        return jnp.concatenate([v[:2].reshape(N, N), v[2:].reshape(N, N)], axis=1)

    def increments(k):
        hp = lax.rem(me // 4 + k, PAIRS)
        wide = dot(stack_ref[...], pick(hp))
        cx, dx = wide[:T], wide[T:]
        cx_ref[hp] = cx
        xd = x_ref[:, cols(hp)].astype(F32) * dx
        xdt_ref[hp] = xd.astype(BF)
        sc = (xd * jnp.exp(cx[T - 1 : T] - cx)).astype(BF)
        sc_ref[hp] = sc
        put_pair(es_ref, hp, dot(b_t, sc))
        send_pair(hp, es_ref, re_ref, 13)

    loop(PAIRS, increments)
    re_ref[me] = es_ref[me]

    rows_ref[...] = jnp.concatenate([cum, dt], axis=1).T
    sm_ref[...] = jnp.where(row_i >= col_i, dot_nt(c_out, b_in), 0.0)
    skips_ref[...] = jnp.concatenate(
        split3(jnp.broadcast_to(skip_ref[...], (16, HEADS))), axis=1).astype(BF)

    def in_block(hp):
        sk_ref[hp] = dot(skips_ref[...], pick(hp))[:8]
        parts = []
        for j in range(2):
            cx = cx_ref[hp, :, j * N : (j + 1) * N]
            gap = jnp.concatenate([cx, cx], axis=1) - rows_ref[pl.ds(head0 + 2 * hp + j, 1), :]
            decay = jnp.exp(jnp.minimum(gap, 0.0))
            l_ref[2 * hp + j] = decay.astype(BF)
            w = (decay * sm_ref[...]).astype(BF)
            parts.append(dot(w, xdt_ref[hp, :, j * N : (j + 1) * N]))
        z_ref[hp] = jnp.concatenate(parts, axis=1)

    loop(PAIRS, in_block)
    load_tgt.wait()
    c_t = c_out.astype(F32).T.astype(BF)

    wait_for(ce_ref.at[pl.ds(0, SEQ - 1)], rsem.at[12])
    ends = jnp.concatenate(split3(ce_ref[...].reshape(SEQ, N)[:, :HEADS]), axis=1).astype(BF)
    sel_own = jnp.where(sel_row[:, :N] == head0 + me // 2, 1.0, 0.0).astype(BF)
    dec_ref[...] = jnp.exp(dot(ends, sel_own))
    wait_for(re_ref.at[pl.ds(0, SEQ - 1)], rsem.at[13])

    def forward(j, state):
        sf_ref[j] = state.astype(BF)
        return dec_ref[pl.ds(j, 1), :] * state + re_ref[j].astype(F32)

    lax.fori_loop(0, SEQ, forward, jnp.zeros((PIECE, N), F32), unroll=4)
    loop(SEQ - 1, lambda k: send(
        sf_ref.at[peer(k + 1)], rs_ref.at[me], ssem.at[14], s_rsem.at[me], (peer(k + 1), dq)))
    rs_ref[me] = sf_ref[me]

    def turn(i):
        at = pl.ds(pl.multiple_of(i * 2 * N, 2 * N), 2 * N)
        xt_ref[at, :] = x_ref[:, at].astype(F32).T.astype(BF)

    loop(PAIRS, turn)
    acc_ref[...] = jnp.zeros_like(acc_ref)

    def errors(k):
        hp = lax.rem(me // 4 + PAIRS - k, PAIRS)
        at = cols(hp)
        wait_pair(hp, rs_ref, s_rsem)
        decay = jnp.exp(cx_ref[hp])
        z = z_ref[hp] + dot(c_out, get_pair(rs_ref, hp)) * decay
        z_ref[hp] = z
        err = (z + sk_ref[hp][:1] * x_ref[:, at].astype(F32)) - tgt_ref[:, at].astype(F32)
        err_ref[hp] = err
        de = (err * decay).astype(BF)
        de_ref[hp] = de
        put_pair(gs_ref, hp, dot(c_t, de))
        send_pair(hp, gs_ref, rg_ref, 15)
        acc_ref[0:8] += jnp.sum((err * err).reshape(T // 8, 8, 2 * N), axis=0)

    loop(PAIRS, errors)
    rg_ref[me] = gs_ref[me]

    lane = lax.broadcasted_iota(jnp.int32, (T, HEADS), 1)
    lane1 = lax.broadcasted_iota(jnp.int32, (1, HEADS), 1)
    for ref in (dsc_ref, dc_ref, db_ref, k_ref, a_ref, dw_ref):
        ref[...] = jnp.zeros_like(ref)

    def grads_in_block(hp):
        at = cols(hp)
        xp = x_ref[:, at]
        err = err_ref[hp]
        errb = err.astype(BF)
        dc_ref[...] += dot_nt(de_ref[hp], get_pair(rs_ref, hp))
        rowed = err * z_ref[hp]
        skipped = jnp.sum(err * xp.astype(F32), axis=0, keepdims=True)
        for j in range(2):
            head = head0 + 2 * hp + j
            sub = slice(j * N, (j + 1) * N)
            dwd = dot_nt(errb[:, sub], xp[:, sub]) * l_ref[2 * hp + j].astype(F32)
            dsc_ref[...] += dwd * rows_ref[pl.ds(HEADS + head, 1), :]
            k_ref[pl.ds(head, 1), :] = jnp.sum(dwd * sm_ref[...], axis=0, keepdims=True)
            a_ref[...] += jnp.where(
                lane == head, jnp.sum(rowed[:, sub], axis=1, keepdims=True), 0.0)
            acc_ref[8:9, :HEADS] += jnp.where(
                lane1 == head, jnp.sum(skipped[:, sub], axis=1, keepdims=True), 0.0)

    loop(PAIRS, grads_in_block)
    dsc = jnp.where(row_i >= col_i, dsc_ref[...], 0.0)
    m2_tmp[...] = ((dc_ref[...] + dot(dsc.astype(BF), b_in)) * SCALE).reshape(2, 128, N)
    sum_c.first()
    db_ref[...] = dot(dsc.T.astype(BF), c_out)
    sum_c.second()
    k_cols = k_ref[...].T[:, :HEADS]
    sum_c.third()
    sum_c.last()

    wait_for(rg_ref.at[pl.ds(0, SEQ - 1)], rsem.at[15])

    def backward(i, state):
        j = SEQ - 1 - i
        sh_ref[j] = state.astype(BF)
        return dec_ref[pl.ds(j, 1), :] * state + rg_ref[j].astype(F32)

    lax.fori_loop(0, SEQ, backward, jnp.zeros((PIECE, N), F32), unroll=4)
    loop(SEQ - 1, lambda k: send(
        sh_ref.at[peer(k + 1)], rh_ref.at[me], ssem.at[16], h_rsem.at[me], (peer(k + 1), dq)))
    rh_ref[me] = sh_ref[me]

    g_c = m2_f[...].reshape(T, N)

    def terms_c(g):
        part = xt_ref[pl.ds(pl.multiple_of(g * 512, 512), 512), :]
        wsc_ref[pl.ds(8 * g, 8)] = dot(part, g_c).astype(BF).reshape(8, PIECE, N)

    loop(4, terms_c)
    to_peers(lambda o: send(wsc_ref.at[o], rwc_ref.at[me], ssem.at[17], rsem.at[17], (o, dq)))
    rwc_ref[me] = wsc_ref[me]

    def grads_of_state(k):
        hp = lax.rem(me // 4 + PAIRS - k, PAIRS)
        wait_pair(hp, rh_ref, h_rsem)
        after = get_pair(rh_ref, hp)
        db_ref[...] += dot_nt(sc_ref[hp], after)
        weighed = dot(b_in, after) * x_ref[:, cols(hp)].astype(F32)
        decayed = jnp.sum(
            after.astype(F32) * get_pair(rs_ref, hp).astype(F32), axis=0, keepdims=True)
        for j in range(2):
            head = head0 + 2 * hp + j
            sub = slice(j * N, (j + 1) * N)
            dw_ref[...] += jnp.where(
                lane == head, jnp.sum(weighed[:, sub], axis=1, keepdims=True), 0.0)
            acc_ref[9:10, :HEADS] += jnp.where(
                lane1 == head, jnp.sum(decayed[:, sub], axis=1, keepdims=True), 0.0)

    loop(PAIRS, grads_of_state)

    left = jnp.exp(cend - cum)
    d_weight = dw_ref[...] * left
    d_gap = d_weight * dt
    d_end = jnp.sum(d_gap, axis=0, keepdims=True) + jnp.exp(cend) * acc_ref[9:10, :HEADS]
    d_cum = a_ref[...] - k_cols * dt - d_gap
    tri_up = jnp.where(row_i <= col_i, 1.0, 0.0).astype(BF)
    d_log = tri_sum(tri_up, d_cum) + d_end
    d_dt = k_cols + d_weight - rate * d_log
    d_pre = d_dt / (1.0 + jnp.exp(-pre)) * SCALE
    for i in range(2):
        half = slice(128 * i, 128 * i + 128)
        m3_tmp[i, 0:128] = db_ref[half] * SCALE
        m3_tmp[i, 128:192] = pack_rows(d_pre[half])
    sum_b.first()
    loss = jnp.sum(jnp.sum(acc_ref[0:8], axis=0, keepdims=True), axis=1, keepdims=True)
    zero = jnp.zeros((1, HEADS), F32)
    small = jnp.concatenate([
        jnp.broadcast_to(loss * (SCALE * SCALE * 0.5), (1, HEADS)),
        jnp.sum(d_log * log_rate, axis=0, keepdims=True) * SCALE,
        jnp.sum(d_pre, axis=0, keepdims=True),
        acc_ref[8:9, :HEADS] * SCALE,
        zero, zero, zero, zero], axis=0)
    sums_ref[...] = jnp.concatenate([small, jnp.zeros_like(small)], axis=1)
    sum_b.second()

    @pl.when(me != 0)
    def _():
        send(sums_ref, sroot_ref.at[me], ssem.at[21], rsem.at[21], (0, dq))

    def total_of(ref):
        return lax.fori_loop(
            1, SEQ, lambda j, s: s + ref[j].astype(F32), ref[0].astype(F32), unroll=4).astype(BF)

    wait_for(rwc_ref.at[pl.ds(0, SEQ - 1)], rsem.at[17])
    wbc_ref[me, :, N:] = total_of(rwc_ref)
    own_c = wbc_ref.at[me, :, pl.ds(N, N)]
    to_peers(lambda o: send(own_c, own_c, ssem.at[18], rsem.at[18], (o, dq)))

    sum_b.third()
    sum_b.last()

    g_b = m3_f[:, 0:128].reshape(T, N)
    g_dt = unpack_rows(m3_f.at[:, pl.ds(128, 64)]).astype(F32).T.astype(BF)

    def terms_b(g):
        part = xt_ref[pl.ds(pl.multiple_of(g * 512, 512), 512), :]
        wsb_ref[pl.ds(8 * g, 8), 0:PIECE] = dot(part, g_b).astype(BF).reshape(8, PIECE, N)
        wide = dot(g_dt, x_ref[:, pl.ds(pl.multiple_of(g * 512, 512), 512)]).astype(BF)
        for i in range(4):
            for j in range(2):
                wsb_ref[4 * g + i + 16 * j, PIECE : PIECE + 32] = wide[
                    32 * j : 32 * j + 32, N * i : N * i + N]

    loop(4, terms_b)
    to_peers(lambda o: send(wsb_ref.at[o], rwb_ref.at[me], ssem.at[19], rsem.at[19], (o, dq)))
    rwb_ref[me] = wsb_ref[me]

    @pl.when(me == 0)
    def _():
        sroot_ref[0] = sums_ref[...]
        wait_for(sroot_ref.at[pl.ds(0, SEQ - 1)], rsem.at[21])
        sdp_ref[dq] = jnp.sum(sroot_ref[...], axis=0)
        for k in range(1, DP):
            send(sdp_ref.at[dq], sdp_ref.at[dq], ssem.at[22], rsem.at[22],
                 (me, lax.rem(dq + k, DP)))

    wait_for(rwb_ref.at[pl.ds(0, SEQ - 1)], rsem.at[19])
    total = total_of(rwb_ref)
    wbc_ref[me, :, :N] = total[:PIECE]
    own_b = wbc_ref.at[me, :, pl.ds(0, N)]
    own_dt = wdt_ref.at[pl.ds(pl.multiple_of(32 * (me // 16), 32), 32),
                        pl.ds(pl.multiple_of(N * lax.rem(me, 16), N), N)]
    own_dt[...] = total[PIECE:]

    def last_sends(o):
        send(own_b, own_b, ssem.at[20], rsem.at[20], (o, dq))
        send(own_dt, own_dt, ssem.at[24], rsem.at[24], (o, dq))

    to_peers(last_sends)

    @pl.when(me == 0)
    def _():
        wait_for(sdp_ref.at[pl.ds(0, DP - 1)], rsem.at[22])
        sfin_ref[...] = jnp.sum(sdp_ref[...], axis=0)
        loop(SEQ - 1, lambda k: send(
            sfin_ref, sfin_ref, ssem.at[23], rsem.at[23], (peer(k + 1), dq)))
        wait_for(sdp_ref.at[pl.ds(0, DP - 1)], ssem.at[22])
        wait_for(sroot_ref.at[pl.ds(0, SEQ - 1)], ssem.at[23])

    @pl.when(me != 0)
    def _():
        wait_for(sums_ref, ssem.at[21])
        wait_for(sfin_ref, rsem.at[23])

    small_ref[...] = sfin_ref[...]

    for one in (sum_bc, sum_dt, sum_c, sum_b):
        one.sent()
    pieces = pl.ds(0, SEQ - 1)
    for sem, ref in ((12, ce_ref), (13, es_ref), (14, sf_ref), (15, gs_ref), (16, sh_ref),
                     (17, wsc_ref), (18, wsc_ref), (19, wsb_ref), (20, wsc_ref)):
        wait_for(ref.at[pieces], ssem.at[sem])
    wait_for(wsb_ref.at[pieces, pl.ds(0, 32)], ssem.at[24])
    wait_for(wbc_ref.at[pieces, :, pl.ds(N, N)], rsem.at[18])
    wait_for(wbc_ref.at[pieces, :, pl.ds(0, N)], rsem.at[20])
    wait_for(rwb_ref.at[pieces, pl.ds(0, 32)], rsem.at[24])


def shards(teacher_rows, teacher_next, state_proj, step_proj, rate_log, step_bias, skip_gain):
    vmem = pl.BlockSpec(memory_space=pltpu.VMEM)
    hbm = pl.BlockSpec(memory_space=pl.ANY)

    def buf(*shape):
        return pltpu.VMEM(shape, BF)

    def f32(*shape):
        return pltpu.VMEM(shape, F32)

    def dp_bufs(rows, kind):
        return [f32(2, rows, N), *[kind(rows, N) for _ in range(4)], kind(2, rows, N)]

    scratch = [
        buf(T, WIDTH), buf(T, WIDTH), buf(WIDTH, 2 * N), buf(HEADS, WIDTH), buf(WIDTH, T),
        *dp_bufs(256, buf), *dp_bufs(64, f32), *dp_bufs(128, buf), *dp_bufs(192, buf),
        buf(2 * T, 3 * HEADS), buf(16, 3 * HEADS), f32(2 * HEADS, T),
        f32(PAIRS, T, 2 * N), f32(PAIRS, 8, 2 * N), buf(PAIRS, T, 2 * N), buf(PAIRS, T, 2 * N),
        buf(2 * PAIRS, T, T), f32(PAIRS, T, 2 * N), f32(PAIRS, T, 2 * N), buf(PAIRS, T, 2 * N),
        f32(T, T), f32(T, T), f32(T, N), f32(T, N), f32(2 * HEADS, T), f32(T, HEADS), f32(T, HEADS),
        f32(16, 2 * N),
        f32(SEQ, 1, N), *[buf(SEQ, PIECE, N) for _ in range(8)], f32(SEQ, N),
        buf(SEQ, PIECE, N), buf(SEQ, PIECE, N), buf(SEQ, PIECE + 32, N), buf(SEQ, PIECE + 32, N),
        f32(8, 128), f32(SEQ, 8, 128), f32(DP, 8, 128), f32(8, 128),
        pltpu.SemaphoreType.DMA((25,)), pltpu.SemaphoreType.DMA((25,)),
        pltpu.SemaphoreType.DMA((SEQ,)), pltpu.SemaphoreType.DMA((SEQ,)),
        pltpu.SemaphoreType.DMA((4,)), pltpu.SemaphoreType.REGULAR((2,)),
    ]
    state_grad, step_grad, small = pl.pallas_call(
        kernel,
        out_shape=(
            jax.ShapeDtypeStruct((SEQ, PIECE, 2 * N), BF),
            jax.ShapeDtypeStruct((HEADS, WIDTH), BF),
            jax.ShapeDtypeStruct((8, 128), F32),
        ),
        in_specs=[hbm, hbm, hbm, hbm, vmem, vmem, vmem],
        out_specs=(vmem, vmem, vmem),
        scratch_shapes=scratch,
        compiler_params=pltpu.CompilerParams(
            collective_id=0, has_side_effects=True, vmem_limit_bytes=52 * 1024 * 1024),
    )(teacher_rows, teacher_next, state_proj, step_proj.T,
      rate_log[None], step_bias[None], skip_gain[None])
    return (small[0, 0], state_grad.reshape(WIDTH, 2 * N).astype(F32), step_grad.astype(F32).T,
            small[1, :HEADS], small[2, :HEADS], small[3, :HEADS])


def solution(mesh):
    placed = (P("seq", "dp"), P("seq", "dp"), P(), P(), P(), P(), P())
    return jax.shard_map(
        shards,
        mesh=mesh,
        in_specs=placed,
        out_specs=(P(), P("dp", None), P("dp", None), P(), P(), P()),
        check_vma=False,
    )
```

```python
import functools

import jax
import jax.numpy as jnp
from jax import lax
from jax.experimental import pallas as pl
from jax.experimental.pallas import tpu as pltpu
from jax.sharding import PartitionSpec as P

SEQ, DP = 32, 4
T = 256
WIDTH = 2048
HEADS = 64
PAIRS = 8
N = 128
PIECE = 64
MESH = pl.DeviceIdType.MESH
BF, F32 = jnp.bfloat16, jnp.float32
SCALE = 1.0 / 8192.0


def dot(a, b):
    return jnp.dot(a, b, preferred_element_type=F32)


def dot_nt(a, b):
    return lax.dot_general(a, b, (((1,), (1,)), ((), ())), preferred_element_type=F32)


def split3(v):
    hi = v.astype(BF).astype(F32)
    rest = v - hi
    mid = rest.astype(BF).astype(F32)
    return hi, mid, rest - mid


def tri_sum(tri, v):
    return sum(dot(tri, part.astype(BF)) for part in split3(v))


def send(src, dst, send_sem, recv_sem, device):
    pltpu.make_async_remote_copy(
        src_ref=src, dst_ref=dst, send_sem=send_sem, recv_sem=recv_sem,
        device_id=device, device_id_type=MESH,
    ).start()


def wait_for(ref, sem):
    pltpu.make_async_copy(ref, ref, sem).wait()


def loop(count, body):
    lax.fori_loop(0, count, lambda k, c: (body(k), c)[1], 0)


def pack_rows(v):
    return jnp.concatenate([v[:64], v[64:]], axis=1)


def unpack_rows(ref):
    return jnp.concatenate([ref[i][:, j : j + 64] for i in range(2) for j in (0, 64)], axis=0)


def kernel(
    x_hbm, tgt_hbm, sp_ref, st_ref, heads_ref,
    wbc_ref, wdt_ref, small_ref,
    x_ref, tgt_ref, w_bc, w_dt, xt_ref,
    m0_tmp, m0_sa, m0_ra, m0_sb, m0_rb, m0_f,
    m1_tmp, m1_sa, m1_ra, m1_sb, m1_rb, m1_f,
    d1_tmp, d1_sa, d1_ra, d1_sb, d1_rb, d1_f,
    m2_tmp, m2_sa, m2_ra, m2_sb, m2_rb, m2_f,
    m3_tmp, m3_sa, m3_ra, m3_sb, m3_rb, m3_f,
    weight_ref, stack_ref, skips_ref, rows_ref, cx_ref, sk_ref, sc_ref, l_ref, z_ref, err_ref, de_ref,
    sm_ref, dsc_ref, dc_ref, db_ref, k_ref, a_ref, dw_ref, acc_ref,
    ce_ref, es_ref, re_ref, sf_ref, rs_ref, gs_ref, rg_ref, sh_ref, rh_ref, dec_ref,
    z1_s, z1_r, x1_s, x1_r, z2_s, z2_r, x2_s, x2_r, wsb_ref, rwb_ref, sums_ref, sroot_ref, sdp_ref, sfin_ref,
    ssem, rsem, s_rsem, h_rsem, w_rsem, lsem, go,
):
    me, dq = lax.axis_index("seq"), lax.axis_index("dp")
    head0 = dq * (HEADS // DP)
    core = lax.rem(dq, 2)
    sibling = dq + 1 - 2 * core
    across = lax.rem(dq + 2, DP)

    def peer(k):
        return lax.rem(me + k, SEQ)

    def offset(dy, dx, dz):
        y, x, z = me // 16, lax.rem(me // 4, 4), lax.rem(me, 4)
        return lax.rem(y + dy, 2) * 16 + lax.rem(x + dx, 4) * 4 + lax.rem(z + dz, 4)

    def signal(sem, device):
        pl.semaphore_signal(sem, inc=1, device_id=device, device_id_type=MESH)

    def to_peers(start):
        def one(k):
            o = offset(1 - k // 16, lax.rem(2 + k // 4, 4), lax.rem(2 + k, 4))

            @pl.when(o != me)
            def _():
                start(o)

        loop(SEQ, one)

    barrier = pltpu.get_barrier_semaphore()
    z_line = [(0, 0, k) for k in (1, 2, 3)]
    x_line = [(0, k, 0) for k in (1, 2, 3)]
    for k in range(1, DP):
        signal(barrier, (me, lax.rem(dq + k, DP)))
    for at in z_line + x_line + [(1, 0, 0)]:
        signal(barrier, (offset(*at), dq))
    own = pl.ds(pl.multiple_of(dq * WIDTH, WIDTH), WIDTH)
    load_x = pltpu.make_async_copy(x_hbm, x_ref, lsem.at[0])
    load_bc = pltpu.make_async_copy(sp_ref.at[own], w_bc, lsem.at[1])
    load_dt = pltpu.make_async_copy(st_ref.at[:, own], w_dt, lsem.at[2])
    load_tgt = pltpu.make_async_copy(tgt_hbm, tgt_ref, lsem.at[3])
    load_x.start()
    load_bc.start()
    load_dt.start()
    load_tgt.start()
    load_x.wait()
    load_bc.wait()
    load_dt.wait()

    class DpSum:
        def __init__(self, sem, tmp, sa, ra, sb, rb, f):
            self.sem, self.tmp, self.sa, self.ra, self.sb, self.rb, self.f = sem, tmp, sa, ra, sb, rb, f

        def send(self, src, dst, step, member):
            send(src, dst, ssem.at[self.sem + step], rsem.at[self.sem + step], (me, member))

        def first(self):
            self.sa[...] = self.tmp[1 - core].astype(self.sa.dtype)
            self.send(self.sa, self.ra, 0, sibling)

        def second(self):
            wait_for(self.ra, rsem.at[self.sem])
            chip = self.tmp[core] + self.ra[...].astype(F32)
            self.tmp[core] = chip
            self.sb[...] = chip.astype(self.sb.dtype)
            self.send(self.sb, self.rb, 1, across)

        def third(self):
            wait_for(self.rb, rsem.at[self.sem + 1])
            self.f[core] = (self.tmp[core] + self.rb[...].astype(F32)).astype(self.f.dtype)
            self.send(self.f.at[core], self.f.at[core], 2, sibling)

        def last(self):
            wait_for(self.f.at[0], rsem.at[self.sem + 2])

        def sent(self):
            for step, ref in enumerate((self.sa, self.sb, self.f.at[0])):
                wait_for(ref, ssem.at[self.sem + step])

    sum_b1 = DpSum(0, m0_tmp, m0_sa, m0_ra, m0_sb, m0_rb, m0_f)
    sum_c1 = DpSum(25, m1_tmp, m1_sa, m1_ra, m1_sb, m1_rb, m1_f)
    sum_dt = DpSum(3, d1_tmp, d1_sa, d1_ra, d1_sb, d1_rb, d1_f)
    sum_c = DpSum(6, m2_tmp, m2_sa, m2_ra, m2_sb, m2_rb, m2_f)
    sum_b = DpSum(9, m3_tmp, m3_sa, m3_ra, m3_sb, m3_rb, m3_f)

    x_all = x_ref[...]
    part_dt = dot_nt(x_all, w_dt[...])
    part_bc = dot(x_all, w_bc[...])
    for i in range(2):
        half = slice(128 * i, 128 * i + 128)
        d1_tmp[i] = pack_rows(part_dt[half])
        m0_tmp[i] = part_bc[half, :N]
        m1_tmp[i] = part_bc[half, N:]
    pl.semaphore_wait(barrier, DP - 1 + 7)
    sum_dt.first()
    sum_b1.first()
    sum_c1.first()
    for at in x_line:
        signal(go.at[0], (offset(*at), dq))
    sum_dt.second()
    sum_b1.second()
    sum_c1.second()
    pl.semaphore_wait(go.at[0], 3)
    signal(go.at[1], (offset(1, 0, 0), dq))
    sum_dt.third()
    sum_b1.third()
    sum_dt.last()
    sum_b1.last()

    b_in = m0_f[...].reshape(T, N)
    pre = unpack_rows(d1_f) + heads_ref[1:2]
    dt = jnp.maximum(pre, 0.0) + jnp.log1p(jnp.exp(-jnp.abs(pre)))
    rate = jnp.exp(heads_ref[0:1])
    log_rate = -rate * dt
    row_i = lax.broadcasted_iota(jnp.int32, (T, T), 0)
    col_i = lax.broadcasted_iota(jnp.int32, (T, T), 1)
    tri = jnp.where(row_i >= col_i, 1.0, 0.0).astype(BF)
    cum = tri_sum(tri, log_rate)
    cend = cum[T - 1 : T]
    b_t = b_in.astype(F32).T.astype(BF)
    weight = dt * jnp.exp(cend - cum)
    high = weight.astype(BF).astype(F32)
    weight_ref[...] = jnp.concatenate([high, weight - high], axis=1).astype(BF)
    ce_ref[me] = jnp.concatenate([cend, cend], axis=1)
    pl.semaphore_wait(go.at[1], 1)
    loop(SEQ - 1, lambda k: send(
        ce_ref.at[me], ce_ref.at[me], ssem.at[12], rsem.at[12], (peer(k + 1), dq)))
    sel_row = lax.rem(lax.broadcasted_iota(jnp.int32, (3 * HEADS, 2 * N), 0), HEADS)
    sel_col = lax.broadcasted_iota(jnp.int32, (3 * HEADS, 2 * N), 1) // N

    def cols(hp):
        return pl.ds(pl.multiple_of(hp * 2 * N, 2 * N), 2 * N)

    def pick(hp):
        return jnp.where(sel_row == head0 + 2 * hp + sel_col, 1.0, 0.0).astype(BF)

    def send_pair(hp, src, dst, sem):
        for i in range(4):
            o = 4 * hp + i

            @pl.when(o != me)
            def _():
                send(src.at[o], dst.at[me], ssem.at[sem], rsem.at[sem], (o, dq))

    def wait_pair(hp, ref, sems):
        for i in range(4):
            o = 4 * hp + i

            @pl.when(o != me)
            def _():
                wait_for(ref.at[o], sems.at[o])

    def put_pair(ref, hp, value):
        for i in range(4):
            half, j = i % 2, i // 2
            ref[4 * hp + i] = value[
                half * PIECE : (half + 1) * PIECE, j * N : (j + 1) * N].astype(BF)

    def get_pair(ref, hp):
        v = ref[pl.ds(4 * hp, 4)]
        return jnp.concatenate([v[:2].reshape(N, N), v[2:].reshape(N, N)], axis=1)

    def increments(k):
        hp = lax.rem(me // 4 + k, PAIRS)
        wide = dot(weight_ref[...], pick(hp)[: 2 * HEADS])
        sc = (x_ref[:, cols(hp)].astype(F32) * wide).astype(BF)
        sc_ref[hp] = sc
        put_pair(es_ref, hp, dot(b_t, sc))
        send_pair(hp, es_ref, re_ref, 13)

    loop(PAIRS, increments)
    re_ref[me] = es_ref[me]

    sum_c1.third()
    stack_ref[0:T] = jnp.concatenate(split3(cum), axis=1).astype(BF)
    stack_ref[T : 2 * T] = jnp.concatenate(split3(dt), axis=1).astype(BF)
    rows_ref[...] = jnp.concatenate([cum, dt], axis=1).T
    sum_c1.last()
    c_out = m1_f[...].reshape(T, N)
    sm_ref[...] = jnp.where(row_i >= col_i, dot_nt(c_out, b_in), 0.0)
    skips_ref[...] = jnp.concatenate(
        split3(jnp.broadcast_to(heads_ref[2:3], (16, HEADS))), axis=1).astype(BF)

    def in_block(hp):
        sk_ref[hp] = dot(skips_ref[...], pick(hp))[:8]
        wide = dot(stack_ref[...], pick(hp))
        cx_ref[hp] = wide[:T]
        xd = (x_ref[:, cols(hp)].astype(F32) * wide[T:]).astype(BF)
        parts = []
        for j in range(2):
            cx = wide[:T, j * N : (j + 1) * N]
            gap = jnp.concatenate([cx, cx], axis=1) - rows_ref[pl.ds(head0 + 2 * hp + j, 1), :]
            decay = jnp.exp(jnp.minimum(gap, 0.0))
            l_ref[2 * hp + j] = decay.astype(BF)
            w = (decay * sm_ref[...]).astype(BF)
            parts.append(dot(w, xd[:, j * N : (j + 1) * N]))
        z_ref[hp] = jnp.concatenate(parts, axis=1)

    loop(PAIRS, in_block)
    load_tgt.wait()
    c_t = c_out.astype(F32).T.astype(BF)

    wait_for(ce_ref.at[pl.ds(0, SEQ - 1)], rsem.at[12])
    ends = jnp.concatenate(split3(ce_ref[...].reshape(SEQ, N)[:, :HEADS]), axis=1).astype(BF)
    sel_own = jnp.where(sel_row[:, :N] == head0 + me // 2, 1.0, 0.0).astype(BF)
    dec_ref[...] = jnp.exp(dot(ends, sel_own))
    wait_for(re_ref.at[pl.ds(0, SEQ - 1)], rsem.at[13])

    def forward(j, state):
        sf_ref[j] = state.astype(BF)
        return dec_ref[pl.ds(j, 1), :] * state + re_ref[j].astype(F32)

    lax.fori_loop(0, SEQ, forward, jnp.zeros((PIECE, N), F32), unroll=4)
    loop(SEQ - 1, lambda k: send(
        sf_ref.at[peer(k + 1)], rs_ref.at[me], ssem.at[14], s_rsem.at[me], (peer(k + 1), dq)))
    rs_ref[me] = sf_ref[me]

    def turn(i):
        at = pl.ds(pl.multiple_of(i * 2 * N, 2 * N), 2 * N)
        xt_ref[at, :] = x_ref[:, at].astype(F32).T.astype(BF)

    loop(PAIRS, turn)
    acc_ref[...] = jnp.zeros_like(acc_ref)

    def errors(k):
        hp = lax.rem(me // 4 + PAIRS - k, PAIRS)
        at = cols(hp)
        wait_pair(hp, rs_ref, s_rsem)
        decay = jnp.exp(cx_ref[hp])
        z = z_ref[hp] + dot(c_out, get_pair(rs_ref, hp)) * decay
        z_ref[hp] = z
        err = (z + sk_ref[hp][:1] * x_ref[:, at].astype(F32)) - tgt_ref[:, at].astype(F32)
        err_ref[hp] = err
        de = (err * decay).astype(BF)
        de_ref[hp] = de
        put_pair(gs_ref, hp, dot(c_t, de))
        send_pair(hp, gs_ref, rg_ref, 15)
        acc_ref[0:8] += jnp.sum((err * err).reshape(T // 8, 8, 2 * N), axis=0)

    loop(PAIRS, errors)
    rg_ref[me] = gs_ref[me]

    lane = lax.broadcasted_iota(jnp.int32, (T, HEADS), 1)
    lane1 = lax.broadcasted_iota(jnp.int32, (1, HEADS), 1)
    for ref in (dsc_ref, dc_ref, db_ref, k_ref, a_ref, dw_ref):
        ref[...] = jnp.zeros_like(ref)

    def grads_in_block(hp):
        at = cols(hp)
        xp = x_ref[:, at]
        err = err_ref[hp]
        errb = err.astype(BF)
        dc_ref[...] += dot_nt(de_ref[hp], get_pair(rs_ref, hp))
        rowed = err * z_ref[hp]
        skipped = jnp.sum(err * xp.astype(F32), axis=0, keepdims=True)
        for j in range(2):
            head = head0 + 2 * hp + j
            sub = slice(j * N, (j + 1) * N)
            dwd = dot_nt(errb[:, sub], xp[:, sub]) * l_ref[2 * hp + j].astype(F32)
            dsc_ref[...] += dwd * rows_ref[pl.ds(HEADS + head, 1), :]
            k_ref[pl.ds(head, 1), :] = jnp.sum(dwd * sm_ref[...], axis=0, keepdims=True)
            a_ref[...] += jnp.where(
                lane == head, jnp.sum(rowed[:, sub], axis=1, keepdims=True), 0.0)
            acc_ref[8:9, :HEADS] += jnp.where(
                lane1 == head, jnp.sum(skipped[:, sub], axis=1, keepdims=True), 0.0)

    loop(PAIRS, grads_in_block)
    dsc = jnp.where(row_i >= col_i, dsc_ref[...], 0.0)
    m2_tmp[...] = ((dc_ref[...] + dot(dsc.astype(BF), b_in)) * SCALE).reshape(2, 128, N)
    sum_c.first()
    db_ref[...] = dot(dsc.T.astype(BF), c_out)
    sum_c.second()
    k_cols = k_ref[...].T[:, :HEADS]
    wait_for(rg_ref.at[pl.ds(0, SEQ - 1)], rsem.at[15])

    def backward(i, state):
        j = SEQ - 1 - i
        sh_ref[j] = state.astype(BF)
        return dec_ref[pl.ds(j, 1), :] * state + rg_ref[j].astype(F32)

    lax.fori_loop(0, SEQ, backward, jnp.zeros((PIECE, N), F32), unroll=4)
    loop(SEQ - 1, lambda k: send(
        sh_ref.at[peer(k + 1)], rh_ref.at[me], ssem.at[16], h_rsem.at[me], (peer(k + 1), dq)))
    rh_ref[me] = sh_ref[me]

    sum_c.third()
    sum_c.last()

    my_y, my_x, my_z = me // 16, lax.rem(me // 4, 4), lax.rem(me, 4)
    g_c = m2_f[...].reshape(T, N)
    for g in range(4):
        term = dot(xt_ref[512 * g : 512 * g + 512, :], g_c).astype(BF).reshape(8, PIECE, N)
        for i in range(8):
            y, x, z = g // 2, 2 * (g % 2) + i // 4, i % 4
            z1_s[z, 4 * y + x] = term[i, :32]
            x1_s[x, 4 * y + z] = term[i, 32:]
    for k in range(1, 4):
        to = lax.rem(my_z + k, 4)
        send(z1_s.at[to], z1_r.at[my_z], ssem.at[17], rsem.at[17], (offset(0, 0, k), dq))
        to = lax.rem(my_x + k, 4)
        send(x1_s.at[to], x1_r.at[my_x], ssem.at[18], rsem.at[18], (offset(0, k, 0), dq))
    z1_r[my_z] = z1_s[my_z]
    x1_r[my_x] = x1_s[my_x]
    planes = [(dy, d) for dy in (1, 0) for d in (2, 1, 3, 0)][:7]

    def on_plane(dy, mine, d):
        return 4 * lax.rem(my_y + dy, 2) + lax.rem(mine + d, 4)

    def lines_to_planes():
        wait_for(z1_r.at[pl.ds(0, 3)], rsem.at[17])
        z2_s[...] = sum(z1_r[i].astype(F32) for i in range(4)).astype(BF)
        wait_for(x1_r.at[pl.ds(0, 3)], rsem.at[18])
        x2_s[...] = sum(x1_r[i].astype(F32) for i in range(4)).astype(BF)
        at_z, at_x = on_plane(0, my_x, 0), on_plane(0, my_z, 0)
        for dy, d in planes:
            send(z2_s.at[on_plane(dy, my_x, d)], z2_r.at[at_z],
                 ssem.at[28], rsem.at[28], (offset(dy, d, 0), dq))
            send(x2_s.at[on_plane(dy, my_z, d)], x2_r.at[at_x],
                 ssem.at[29], rsem.at[29], (offset(dy, 0, d), dq))
        z2_r[at_z] = z2_s[at_z]
        x2_r[at_x] = x2_s[at_x]

    def half_of(piece, i):
        return wbc_ref.at[piece, pl.ds(32 * i, 32), pl.ds(N, N)]

    def planes_back():
        wait_for(z2_r.at[pl.ds(0, 7)], rsem.at[28])
        wait_for(x2_r.at[pl.ds(0, 7)], rsem.at[29])
        wbc_ref[me, 0:32, N:] = sum(z2_r[i].astype(F32) for i in range(8)).astype(BF)
        wbc_ref[me, 32:64, N:] = sum(x2_r[i].astype(F32) for i in range(8)).astype(BF)
        for dy, d in planes:
            send(half_of(me, 0), half_of(me, 0), ssem.at[30], rsem.at[30], (offset(dy, d, 0), dq))
            send(half_of(me, 1), half_of(me, 1), ssem.at[31], rsem.at[31], (offset(dy, 0, d), dq))

    def lines_back():
        wait_for(wbc_ref.at[pl.ds(0, 7), pl.ds(0, 32), pl.ds(N, N)], rsem.at[30])
        wait_for(wbc_ref.at[pl.ds(0, 7), pl.ds(0, 32), pl.ds(N, N)], rsem.at[31])

        def one(i):
            y, other = i // 4, lax.rem(i, 4)
            for k in range(1, 4):
                piece = half_of(16 * y + 4 * other + my_z, 0)
                send(piece, piece, ssem.at[32], rsem.at[32], (offset(0, 0, k), dq))
                piece = half_of(16 * y + 4 * my_x + other, 1)
                send(piece, piece, ssem.at[33], rsem.at[33], (offset(0, k, 0), dq))

        loop(8, one)

    def grads_of_state(k):
        hp = lax.rem(me // 4 + PAIRS - k, PAIRS)
        wait_pair(hp, rh_ref, h_rsem)
        after = get_pair(rh_ref, hp)
        db_ref[...] += dot_nt(sc_ref[hp], after)
        weighed = dot(b_in, after) * x_ref[:, cols(hp)].astype(F32)
        decayed = jnp.sum(
            after.astype(F32) * get_pair(rs_ref, hp).astype(F32), axis=0, keepdims=True)
        for j in range(2):
            head = head0 + 2 * hp + j
            sub = slice(j * N, (j + 1) * N)
            dw_ref[...] += jnp.where(
                lane == head, jnp.sum(weighed[:, sub], axis=1, keepdims=True), 0.0)
            acc_ref[9:10, :HEADS] += jnp.where(
                lane1 == head, jnp.sum(decayed[:, sub], axis=1, keepdims=True), 0.0)

    loop(PAIRS, grads_of_state)

    left = jnp.exp(cend - cum)
    d_weight = dw_ref[...] * left
    d_gap = d_weight * dt
    d_end = jnp.sum(d_gap, axis=0, keepdims=True) + jnp.exp(cend) * acc_ref[9:10, :HEADS]
    d_cum = a_ref[...] - k_cols * dt - d_gap
    tri_up = jnp.where(row_i <= col_i, 1.0, 0.0).astype(BF)
    d_log = tri_sum(tri_up, d_cum) + d_end
    d_dt = k_cols + d_weight - rate * d_log
    d_pre = d_dt / (1.0 + jnp.exp(-pre)) * SCALE
    for i in range(2):
        half = slice(128 * i, 128 * i + 128)
        m3_tmp[i, 0:128] = db_ref[half] * SCALE
        m3_tmp[i, 128:192] = pack_rows(d_pre[half])
    sum_b.first()
    loss = jnp.sum(jnp.sum(acc_ref[0:8], axis=0, keepdims=True), axis=1, keepdims=True)
    zero = jnp.zeros((1, HEADS), F32)
    small = jnp.concatenate([
        jnp.broadcast_to(loss * (SCALE * SCALE * 0.5), (1, HEADS)),
        jnp.sum(d_log * log_rate, axis=0, keepdims=True) * SCALE,
        jnp.sum(d_pre, axis=0, keepdims=True),
        acc_ref[8:9, :HEADS] * SCALE,
        zero, zero, zero, zero], axis=0)
    sums_ref[...] = jnp.concatenate([small, jnp.zeros_like(small)], axis=1)
    sum_b.second()

    @pl.when(me != 0)
    def _():
        send(sums_ref, sroot_ref.at[me], ssem.at[21], rsem.at[21], (0, dq))

    lines_to_planes()
    sum_b.third()
    sum_b.last()

    g_b = m3_f[:, 0:128].reshape(T, N)
    g_dt = unpack_rows(m3_f.at[:, pl.ds(128, 64)]).astype(F32).T.astype(BF)

    def terms_b(g):
        part = xt_ref[pl.ds(pl.multiple_of(g * 512, 512), 512), :]
        wsb_ref[pl.ds(8 * g, 8), 0:PIECE] = dot(part, g_b).astype(BF).reshape(8, PIECE, N)
        wide = dot(g_dt, x_ref[:, pl.ds(pl.multiple_of(g * 512, 512), 512)]).astype(BF)
        for i in range(4):
            for j in range(2):
                wsb_ref[4 * g + i + 16 * j, PIECE : PIECE + 32] = wide[
                    32 * j : 32 * j + 32, N * i : N * i + N]

    loop(4, terms_b)
    to_peers(lambda o: send(wsb_ref.at[o], rwb_ref.at[me], ssem.at[19], w_rsem.at[me], (o, dq)))
    rwb_ref[me] = wsb_ref[me]
    planes_back()

    @pl.when(me == 0)
    def _():
        sroot_ref[0] = sums_ref[...]
        wait_for(sroot_ref.at[pl.ds(0, SEQ - 1)], rsem.at[21])
        sdp_ref[dq] = jnp.sum(sroot_ref[...], axis=0)
        for k in range(1, DP):
            send(sdp_ref.at[dq], sdp_ref.at[dq], ssem.at[22], rsem.at[22],
                 (me, lax.rem(dq + k, DP)))

    lines_back()

    def add(k, so_far):
        o = offset(1 + k // 16, lax.rem(2 + 3 * (k // 4), 4), lax.rem(2 + 3 * k, 4))

        @pl.when(o != me)
        def _():
            wait_for(rwb_ref.at[o], w_rsem.at[o])

        return so_far + rwb_ref[o].astype(F32)

    total = lax.fori_loop(0, SEQ, add, jnp.zeros((PIECE + 32, N), F32)).astype(BF)
    wbc_ref[me, :, :N] = total[:PIECE]
    own_b = wbc_ref.at[me, :, pl.ds(0, N)]
    own_dt = wdt_ref.at[pl.ds(pl.multiple_of(32 * (me // 16), 32), 32),
                        pl.ds(pl.multiple_of(N * lax.rem(me, 16), N), N)]
    own_dt[...] = total[PIECE:]

    def last_sends(o):
        send(own_b, own_b, ssem.at[20], rsem.at[20], (o, dq))
        send(own_dt, own_dt, ssem.at[24], rsem.at[24], (o, dq))

    to_peers(last_sends)

    @pl.when(me == 0)
    def _():
        wait_for(sdp_ref.at[pl.ds(0, DP - 1)], rsem.at[22])
        sfin_ref[...] = jnp.sum(sdp_ref[...], axis=0)
        loop(SEQ - 1, lambda k: send(
            sfin_ref, sfin_ref, ssem.at[23], rsem.at[23], (peer(k + 1), dq)))
        wait_for(sdp_ref.at[pl.ds(0, DP - 1)], ssem.at[22])
        wait_for(sroot_ref.at[pl.ds(0, SEQ - 1)], ssem.at[23])

    @pl.when(me != 0)
    def _():
        wait_for(sums_ref, ssem.at[21])
        wait_for(sfin_ref, rsem.at[23])

    small_ref[...] = sfin_ref[...]

    for one in (sum_b1, sum_c1, sum_dt, sum_c, sum_b):
        one.sent()
    pieces = pl.ds(0, SEQ - 1)
    for sem, ref in ((12, ce_ref), (13, es_ref), (14, sf_ref), (15, gs_ref), (16, sh_ref),
                     (19, wsb_ref), (20, sf_ref)):
        wait_for(ref.at[pieces], ssem.at[sem])
    wait_for(wsb_ref.at[pieces, pl.ds(0, 32)], ssem.at[24])
    for i in range(2):
        wait_for(z1_s.at[pl.ds(0, 3)], ssem.at[17 + i])
        wait_for(z2_s.at[pl.ds(0, 7)], ssem.at[28 + i])
        wait_for(z2_s.at[pl.ds(0, 7)], ssem.at[30 + i])
        wait_for(z1_s.at[pl.ds(0, 3)], ssem.at[32 + i])
        wait_for(z1_s.at[pl.ds(0, 3)], rsem.at[32 + i])
    wait_for(wbc_ref.at[pieces, :, pl.ds(0, N)], rsem.at[20])
    wait_for(rwb_ref.at[pieces, pl.ds(0, 32)], rsem.at[24])


def widen(wbc_ref, wdt_ref, small_ref, bc_hbm, dt_hbm, loss_ref, *rest):
    sums, (bc_ref, dt_ref, sem) = rest[:3], rest[3:]
    copies = []
    for i in range(4):
        bc_ref[i] = wbc_ref[8 * i : 8 * i + 8].astype(F32).reshape(512, 2 * N)
        copies.append(pltpu.make_async_copy(
            bc_ref.at[i], bc_hbm.at[pl.ds(512 * i, 512)], sem.at[i]))
        copies[-1].start()
    dt_ref[...] = wdt_ref[...].astype(F32)
    copies.append(pltpu.make_async_copy(dt_ref, dt_hbm, sem.at[4]))
    copies[-1].start()
    loss_ref[...] = small_ref[0:1, 0:1]
    for i, ref in enumerate(sums):
        ref[...] = small_ref[i + 1 : i + 2, :HEADS]
    for one in copies:
        one.wait()


def shards(teacher_rows, teacher_next, state_proj, step_proj, rate_log, step_bias, skip_gain):
    vmem = pl.BlockSpec(memory_space=pltpu.VMEM)
    hbm = pl.BlockSpec(memory_space=pl.ANY)

    def buf(*shape):
        return pltpu.VMEM(shape, BF)

    def f32(*shape):
        return pltpu.VMEM(shape, F32)

    def dp_bufs(rows, kind):
        return [f32(2, rows, N), kind(rows, N), kind(rows, N), buf(rows, N), buf(rows, N),
                kind(2, rows, N)]

    scratch = [
        buf(T, WIDTH), buf(T, WIDTH), buf(WIDTH, 2 * N), buf(HEADS, WIDTH), buf(WIDTH, T),
        *dp_bufs(128, buf), *dp_bufs(128, buf), *dp_bufs(64, f32), *dp_bufs(128, buf), *dp_bufs(192, buf),
        buf(T, 2 * HEADS), buf(2 * T, 3 * HEADS), buf(16, 3 * HEADS), f32(2 * HEADS, T),
        f32(PAIRS, T, 2 * N), f32(PAIRS, 8, 2 * N), buf(PAIRS, T, 2 * N),
        buf(2 * PAIRS, T, T), f32(PAIRS, T, 2 * N), f32(PAIRS, T, 2 * N), buf(PAIRS, T, 2 * N),
        f32(T, T), f32(T, T), f32(T, N), f32(T, N), f32(2 * HEADS, T), f32(T, HEADS), f32(T, HEADS),
        f32(16, 2 * N),
        f32(SEQ, 1, N), *[buf(SEQ, PIECE, N) for _ in range(8)], f32(SEQ, N),
        *[buf(4, 8, 32, N) for _ in range(4)], *[buf(8, 32, N) for _ in range(4)],
        buf(SEQ, PIECE + 32, N), buf(SEQ, PIECE + 32, N),
        f32(8, 128), f32(SEQ, 8, 128), f32(DP, 8, 128), f32(8, 128),
        pltpu.SemaphoreType.DMA((34,)), pltpu.SemaphoreType.DMA((34,)),
        *[pltpu.SemaphoreType.DMA((SEQ,)) for _ in range(3)],
        pltpu.SemaphoreType.DMA((4,)), pltpu.SemaphoreType.REGULAR((2,)),
    ]
    state_grad, step_grad, small = pl.pallas_call(
        kernel,
        out_shape=(
            jax.ShapeDtypeStruct((SEQ, PIECE, 2 * N), BF),
            jax.ShapeDtypeStruct((HEADS, WIDTH), BF),
            jax.ShapeDtypeStruct((8, 128), F32),
        ),
        in_specs=[hbm, hbm, hbm, hbm, vmem],
        out_specs=(vmem, vmem, vmem),
        scratch_shapes=scratch,
        compiler_params=pltpu.CompilerParams(
            collective_id=0, has_side_effects=True, vmem_limit_bytes=52 * 1024 * 1024),
    )(teacher_rows, teacher_next, state_proj, step_proj.T,
      jnp.stack([rate_log, step_bias, skip_gain]))
    heads = jax.ShapeDtypeStruct((1, HEADS), F32)
    state_grad, step_grad, loss, *sums = pl.pallas_call(
        widen,
        out_shape=(
            jax.ShapeDtypeStruct((WIDTH, 2 * N), F32),
            jax.ShapeDtypeStruct((HEADS, WIDTH), F32),
            jax.ShapeDtypeStruct((1, 1), F32), heads, heads, heads,
        ),
        in_specs=[vmem] * 3,
        out_specs=(hbm, hbm, vmem, vmem, vmem, vmem),
        scratch_shapes=[f32(4, 512, 2 * N), f32(HEADS, WIDTH), pltpu.SemaphoreType.DMA((5,))],
        compiler_params=pltpu.CompilerParams(vmem_limit_bytes=16 * 1024 * 1024),
    )(state_grad, step_grad, small)
    return (loss[0, 0], state_grad, step_grad.T, *(v[0] for v in sums))


def solution(mesh):
    placed = (P("seq", "dp"), P("seq", "dp"), P(), P(), P(), P(), P())
    return jax.shard_map(
        shards,
        mesh=mesh,
        in_specs=placed,
        out_specs=(P(), P("dp", None), P("dp", None), P(), P(), P()),
        check_vma=False,
    )
```

```python
import functools

import jax
import jax.numpy as jnp
from jax import lax
from jax.experimental import pallas as pl
from jax.experimental.pallas import tpu as pltpu
from jax.sharding import PartitionSpec as P

SEQ, DP = 32, 4
T = 256
WIDTH = 2048
HEADS = 64
PAIRS = 8
N = 128
PIECE = 64
PART = 32
MESH = pl.DeviceIdType.MESH
BF, F32 = jnp.bfloat16, jnp.float32
SCALE = 1.0 / 8192.0


def dot(a, b):
    return jnp.dot(a, b, preferred_element_type=F32)


def dot_nt(a, b):
    return lax.dot_general(a, b, (((1,), (1,)), ((), ())), preferred_element_type=F32)


def split3(v):
    hi = v.astype(BF).astype(F32)
    rest = v - hi
    mid = rest.astype(BF).astype(F32)
    return hi, mid, rest - mid


def tri_sum(tri, v):
    return sum(dot(tri, part.astype(BF)) for part in split3(v))


def send(src, dst, send_sem, recv_sem, device):
    pltpu.make_async_remote_copy(
        src_ref=src, dst_ref=dst, send_sem=send_sem, recv_sem=recv_sem,
        device_id=device, device_id_type=MESH,
    ).start()


def wait_for(ref, sem):
    pltpu.make_async_copy(ref, ref, sem).wait()


def loop(count, body):
    lax.fori_loop(0, count, lambda k, c: (body(k), c)[1], 0)


def pack_rows(v):
    return jnp.concatenate([v[:64], v[64:]], axis=1)


def unpack_rows(ref):
    return jnp.concatenate([ref[i][:, j : j + 64] for i in range(2) for j in (0, 64)], axis=0)


def kernel(
    x_hbm, tgt_hbm, sp_ref, st_ref, heads_ref,
    wbc_ref, wdt_ref, small_ref,
    x_ref, tgt_ref, w_bc, w_dt, xt_ref,
    m0_tmp, m0_sa, m0_ra, m0_sb, m0_rb, m0_f,
    m1_tmp, m1_sa, m1_ra, m1_sb, m1_rb, m1_f,
    d1_tmp, d1_sa, d1_ra, d1_sb, d1_rb, d1_f,
    m2_tmp, m2_sa, m2_ra, m2_sb, m2_rb, m2_f,
    m3_tmp, m3_sa, m3_ra, m3_sb, m3_rb, m3_f,
    weight_ref, stack_ref, skips_ref, rows_ref, cx_ref, sk_ref, sc_ref, l_ref, z_ref, err_ref, de_ref,
    sm_ref, dsc_ref, dc_ref, db_ref, k_ref, a_ref, dw_ref, acc_ref,
    ce_ref, es_ref, re_ref, sf_ref, rs_ref, gs_ref, rg_ref, sh_ref, rh_ref, dec_ref,
    z1_s, z1_r, x1_s, x1_r, z2_s, z2_r, x2_s, x2_r, wsb_ref, rwb_ref, sums_ref, sroot_ref, sdp_ref, sfin_ref,
    ssem, rsem, g_rsem, s_rsem, h_rsem, w_rsem, lsem, go,
):
    me, dq = lax.axis_index("seq"), lax.axis_index("dp")
    head0 = dq * (HEADS // DP)
    core = lax.rem(dq, 2)
    sibling = dq + 1 - 2 * core
    across = lax.rem(dq + 2, DP)

    def peer(k):
        return lax.rem(me + k, SEQ)

    def offset(dy, dx, dz):
        y, x, z = me // 16, lax.rem(me // 4, 4), lax.rem(me, 4)
        return lax.rem(y + dy, 2) * 16 + lax.rem(x + dx, 4) * 4 + lax.rem(z + dz, 4)

    def signal(sem, device):
        pl.semaphore_signal(sem, inc=1, device_id=device, device_id_type=MESH)

    def to_peers(start):
        def one(k):
            k = k + 1
            start(peer(k))

        loop(SEQ - 1, one)

    barrier = pltpu.get_barrier_semaphore()
    z_line = [(0, 0, k) for k in (1, 2, 3)]
    x_line = [(0, k, 0) for k in (1, 2, 3)]
    for k in range(1, DP):
        signal(barrier, (me, lax.rem(dq + k, DP)))
    for at in z_line + x_line + [(1, 0, 0)]:
        signal(barrier, (offset(*at), dq))
    own = pl.ds(pl.multiple_of(dq * WIDTH, WIDTH), WIDTH)
    load_x = pltpu.make_async_copy(x_hbm, x_ref, lsem.at[0])
    load_bc = pltpu.make_async_copy(sp_ref.at[own], w_bc, lsem.at[1])
    load_dt = pltpu.make_async_copy(st_ref.at[:, own], w_dt, lsem.at[2])
    load_tgt = pltpu.make_async_copy(tgt_hbm, tgt_ref, lsem.at[3])
    load_x.start()
    load_bc.start()
    load_dt.start()
    load_tgt.start()
    load_x.wait()
    load_bc.wait()
    load_dt.wait()

    class DpSum:
        def __init__(self, sem, tmp, sa, ra, sb, rb, f):
            self.sem, self.tmp, self.sa, self.ra, self.sb, self.rb, self.f = sem, tmp, sa, ra, sb, rb, f

        def send(self, src, dst, step, member):
            send(src, dst, ssem.at[self.sem + step], rsem.at[self.sem + step], (me, member))

        def first(self):
            self.sa[...] = self.tmp[1 - core].astype(self.sa.dtype)
            self.send(self.sa, self.ra, 0, sibling)

        def second(self):
            wait_for(self.ra, rsem.at[self.sem])
            chip = self.tmp[core] + self.ra[...].astype(F32)
            self.tmp[core] = chip
            self.sb[...] = chip.astype(self.sb.dtype)
            self.send(self.sb, self.rb, 1, across)

        def third(self):
            wait_for(self.rb, rsem.at[self.sem + 1])
            self.f[core] = (self.tmp[core] + self.rb[...].astype(F32)).astype(self.f.dtype)
            self.send(self.f.at[core], self.f.at[core], 2, sibling)

        def last(self):
            wait_for(self.f.at[0], rsem.at[self.sem + 2])

        def sent(self):
            for step, ref in enumerate((self.sa, self.sb, self.f.at[0])):
                wait_for(ref, ssem.at[self.sem + step])

    sum_b1 = DpSum(0, m0_tmp, m0_sa, m0_ra, m0_sb, m0_rb, m0_f)
    sum_c1 = DpSum(25, m1_tmp, m1_sa, m1_ra, m1_sb, m1_rb, m1_f)
    sum_dt = DpSum(3, d1_tmp, d1_sa, d1_ra, d1_sb, d1_rb, d1_f)
    sum_c = DpSum(6, m2_tmp, m2_sa, m2_ra, m2_sb, m2_rb, m2_f)
    sum_b = DpSum(9, m3_tmp, m3_sa, m3_ra, m3_sb, m3_rb, m3_f)

    x_all = x_ref[...]
    part_dt = dot_nt(x_all, w_dt[...])
    part_bc = dot(x_all, w_bc[...])
    for i in range(2):
        half = slice(128 * i, 128 * i + 128)
        d1_tmp[i] = pack_rows(part_dt[half])
        m0_tmp[i] = part_bc[half, :N]
        m1_tmp[i] = part_bc[half, N:]
    pl.semaphore_wait(barrier, DP - 1 + 7)
    sum_dt.first()
    sum_b1.first()
    sum_c1.first()
    for at in x_line:
        signal(go.at[0], (offset(*at), dq))
    sum_dt.second()
    sum_b1.second()
    sum_c1.second()
    pl.semaphore_wait(go.at[0], 3)
    signal(go.at[1], (offset(1, 0, 0), dq))
    sum_dt.third()
    sum_b1.third()
    sum_dt.last()
    sum_b1.last()

    b_in = m0_f[...].reshape(T, N)
    pre = unpack_rows(d1_f) + heads_ref[1:2]
    dt = jnp.maximum(pre, 0.0) + jnp.log1p(jnp.exp(-jnp.abs(pre)))
    rate = jnp.exp(heads_ref[0:1])
    log_rate = -rate * dt
    row_i = lax.broadcasted_iota(jnp.int32, (T, T), 0)
    col_i = lax.broadcasted_iota(jnp.int32, (T, T), 1)
    tri = jnp.where(row_i >= col_i, 1.0, 0.0).astype(BF)
    cum = tri_sum(tri, log_rate)
    cend = cum[T - 1 : T]
    b_t = b_in.astype(F32).T.astype(BF)
    weight = dt * jnp.exp(cend - cum)
    high = weight.astype(BF).astype(F32)
    weight_ref[...] = jnp.concatenate([high, weight - high], axis=1).astype(BF)
    ce_ref[me] = jnp.concatenate([cend, cend], axis=1)
    pl.semaphore_wait(go.at[1], 1)
    loop(SEQ - 1, lambda k: send(
        ce_ref.at[me], ce_ref.at[me], ssem.at[12], rsem.at[12], (peer(k + 1), dq)))
    sel_row = lax.rem(lax.broadcasted_iota(jnp.int32, (3 * HEADS, 2 * N), 0), HEADS)
    sel_col = lax.broadcasted_iota(jnp.int32, (3 * HEADS, 2 * N), 1) // N

    def cols(hp):
        return pl.ds(pl.multiple_of(hp * 2 * N, 2 * N), 2 * N)

    def pick(hp):
        return jnp.where(sel_row == head0 + 2 * hp + sel_col, 1.0, 0.0).astype(BF)

    def pair_of(group, k):
        return 4 * group + lax.rem(me // 8 + k, 4)

    def each_of(hp, body):
        def one(i):
            at = 8 * hp + lax.rem(me + i, 8)
            o = lax.rem(at, SEQ)

            @pl.when(o != me)
            def _():
                body(at, o)

        loop(8, one)

    def send_pair(hp, src, dst, sem):
        each_of(hp, lambda at, o: send(
            src.at[at], dst.at[SEQ * (hp // 4) + me],
            ssem.at[sem], g_rsem.at[2 * (sem - 13) + hp // 4], (o, dq)))

    def wait_pair(hp, ref, sems):
        mine = (SEQ * (hp // 4) + me) // 8 == hp

        @pl.when(mine)
        def _():
            wait_for(ref.at[pl.ds(8 * hp, 7)], sems.at[hp])

        @pl.when(jnp.logical_not(mine))
        def _():
            wait_for(ref.at[pl.ds(8 * hp, 8)], sems.at[hp])

    def send_all(group, src, dst, sem, sems):
        def one(k):
            o = peer(k + 1)
            send(src.at[SEQ * group + o], dst.at[SEQ * group + me],
                 ssem.at[sem], sems.at[(SEQ * group + me) // 8], (o, dq))

        loop(SEQ - 1, one)
        dst[SEQ * group + me] = src[SEQ * group + me]

    def put_pair(ref, hp, value):
        for i in range(8):
            ref[8 * hp + i] = value[
                (i % 4) * PART : (i % 4 + 1) * PART, (i // 4) * N : (i // 4 + 1) * N].astype(BF)

    def get_pair(ref, hp):
        v = ref[pl.ds(8 * hp, 8)]
        return jnp.concatenate([v[:4].reshape(N, N), v[4:].reshape(N, N)], axis=1)

    def wait_group(group, ref, sem):
        wait_for(ref.at[pl.ds(SEQ * group, SEQ - 1)], g_rsem.at[2 * (sem - 13) + group])

    def increments(hp):
        wide = dot(weight_ref[...], pick(hp)[: 2 * HEADS])
        sc = (x_ref[:, cols(hp)].astype(F32) * wide).astype(BF)
        sc_ref[hp] = sc
        put_pair(es_ref, hp, dot(b_t, sc))
        send_pair(hp, es_ref, re_ref, 13)

    for group in range(2):
        loop(4, lambda k: increments(pair_of(group, k + 2)))
        re_ref[SEQ * group + me] = es_ref[SEQ * group + me]

    sum_c1.third()
    stack_ref[0:T] = jnp.concatenate(split3(cum), axis=1).astype(BF)
    stack_ref[T : 2 * T] = jnp.concatenate(split3(dt), axis=1).astype(BF)
    rows_ref[...] = jnp.concatenate([cum, dt], axis=1).T
    sum_c1.last()
    c_out = m1_f[...].reshape(T, N)
    sm_ref[...] = jnp.where(row_i >= col_i, dot_nt(c_out, b_in), 0.0)
    skips_ref[...] = jnp.concatenate(
        split3(jnp.broadcast_to(heads_ref[2:3], (16, HEADS))), axis=1).astype(BF)

    def in_block(hp):
        sk_ref[hp] = dot(skips_ref[...], pick(hp))[:8]
        wide = dot(stack_ref[...], pick(hp))
        cx_ref[hp] = wide[:T]
        xd = (x_ref[:, cols(hp)].astype(F32) * wide[T:]).astype(BF)
        parts = []
        for j in range(2):
            cx = wide[:T, j * N : (j + 1) * N]
            gap = jnp.concatenate([cx, cx], axis=1) - rows_ref[pl.ds(head0 + 2 * hp + j, 1), :]
            decay = jnp.exp(jnp.minimum(gap, 0.0))
            l_ref[2 * hp + j] = decay.astype(BF)
            w = (decay * sm_ref[...]).astype(BF)
            parts.append(dot(w, xd[:, j * N : (j + 1) * N]))
        z_ref[hp] = jnp.concatenate(parts, axis=1)

    loop(PAIRS, in_block)
    load_tgt.wait()
    c_t = c_out.astype(F32).T.astype(BF)

    wait_for(ce_ref.at[pl.ds(0, SEQ - 1)], rsem.at[12])
    ends = jnp.concatenate(split3(ce_ref[...].reshape(SEQ, N)[:, :HEADS]), axis=1).astype(BF)
    for group in range(2):
        sel_own = jnp.where(
            sel_row[:, :N] == head0 + 8 * group + me // 4, 1.0, 0.0).astype(BF)
        dec_ref[SEQ * group : SEQ * group + SEQ] = jnp.exp(dot(ends, sel_own))

    def forward(at, state):
        sf_ref[at] = state.astype(BF)
        return dec_ref[pl.ds(at, 1), :] * state + re_ref[at].astype(F32)

    for group in range(2):
        wait_group(group, re_ref, 13)
        lax.fori_loop(SEQ * group, SEQ * group + SEQ, forward, jnp.zeros((PART, N), F32), unroll=4)
        send_all(group, sf_ref, rs_ref, 14, s_rsem)

    def turn(i):
        at = pl.ds(pl.multiple_of(i * 2 * N, 2 * N), 2 * N)
        xt_ref[at, :] = x_ref[:, at].astype(F32).T.astype(BF)

    loop(PAIRS, turn)
    acc_ref[...] = jnp.zeros_like(acc_ref)

    def errors(hp):
        at = cols(hp)
        wait_pair(hp, rs_ref, s_rsem)
        decay = jnp.exp(cx_ref[hp])
        z = z_ref[hp] + dot(c_out, get_pair(rs_ref, hp)) * decay
        z_ref[hp] = z
        err = (z + sk_ref[hp][:1] * x_ref[:, at].astype(F32)) - tgt_ref[:, at].astype(F32)
        err_ref[hp] = err
        de = (err * decay).astype(BF)
        de_ref[hp] = de
        put_pair(gs_ref, hp, dot(c_t, de))
        send_pair(hp, gs_ref, rg_ref, 15)
        acc_ref[0:8] += jnp.sum((err * err).reshape(T // 8, 8, 2 * N), axis=0)

    for group in range(2):
        loop(4, lambda k: errors(pair_of(group, 4 - k)))
        rg_ref[SEQ * group + me] = gs_ref[SEQ * group + me]

    lane = lax.broadcasted_iota(jnp.int32, (T, HEADS), 1)
    lane1 = lax.broadcasted_iota(jnp.int32, (1, HEADS), 1)
    for ref in (dsc_ref, dc_ref, db_ref, k_ref, a_ref, dw_ref):
        ref[...] = jnp.zeros_like(ref)

    def grads_in_block(hp):
        at = cols(hp)
        xp = x_ref[:, at]
        err = err_ref[hp]
        errb = err.astype(BF)
        dc_ref[...] += dot_nt(de_ref[hp], get_pair(rs_ref, hp))
        rowed = err * z_ref[hp]
        skipped = jnp.sum(err * xp.astype(F32), axis=0, keepdims=True)
        for j in range(2):
            head = head0 + 2 * hp + j
            sub = slice(j * N, (j + 1) * N)
            dwd = dot_nt(errb[:, sub], xp[:, sub]) * l_ref[2 * hp + j].astype(F32)
            dsc_ref[...] += dwd * rows_ref[pl.ds(HEADS + head, 1), :]
            k_ref[pl.ds(head, 1), :] = jnp.sum(dwd * sm_ref[...], axis=0, keepdims=True)
            a_ref[...] += jnp.where(
                lane == head, jnp.sum(rowed[:, sub], axis=1, keepdims=True), 0.0)
            acc_ref[8:9, :HEADS] += jnp.where(
                lane1 == head, jnp.sum(skipped[:, sub], axis=1, keepdims=True), 0.0)

    loop(PAIRS, grads_in_block)
    dsc = jnp.where(row_i >= col_i, dsc_ref[...], 0.0)
    m2_tmp[...] = ((dc_ref[...] + dot(dsc.astype(BF), b_in)) * SCALE).reshape(2, 128, N)
    sum_c.first()
    db_ref[...] = dot(dsc.T.astype(BF), c_out)
    sum_c.second()
    k_cols = k_ref[...].T[:, :HEADS]
    def backward(i, state, group):
        at = SEQ * group + SEQ - 1 - i
        sh_ref[at] = state.astype(BF)
        return dec_ref[pl.ds(at, 1), :] * state + rg_ref[at].astype(F32)

    for group in range(2):
        wait_group(group, rg_ref, 15)
        lax.fori_loop(0, SEQ, functools.partial(backward, group=group),
                      jnp.zeros((PART, N), F32), unroll=4)
        send_all(group, sh_ref, rh_ref, 16, h_rsem)

    sum_c.third()
    sum_c.last()

    my_y, my_x, my_z = me // 16, lax.rem(me // 4, 4), lax.rem(me, 4)
    g_c = m2_f[...].reshape(T, N)
    for g in range(4):
        term = dot(xt_ref[512 * g : 512 * g + 512, :], g_c).astype(BF).reshape(8, PIECE, N)
        for i in range(8):
            y, x, z = g // 2, 2 * (g % 2) + i // 4, i % 4
            z1_s[z, 4 * y + x] = term[i, :32]
            x1_s[x, 4 * y + z] = term[i, 32:]
    for k in range(1, 4):
        to = lax.rem(my_z + k, 4)
        send(z1_s.at[to], z1_r.at[my_z], ssem.at[17], rsem.at[17], (offset(0, 0, k), dq))
        to = lax.rem(my_x + k, 4)
        send(x1_s.at[to], x1_r.at[my_x], ssem.at[18], rsem.at[18], (offset(0, k, 0), dq))
    z1_r[my_z] = z1_s[my_z]
    x1_r[my_x] = x1_s[my_x]
    planes = [(dy, d) for dy in (1, 0) for d in (2, 1, 3, 0)][:7]

    def on_plane(dy, mine, d):
        return 4 * lax.rem(my_y + dy, 2) + lax.rem(mine + d, 4)

    def lines_to_planes():
        wait_for(z1_r.at[pl.ds(0, 3)], rsem.at[17])
        z2_s[...] = sum(z1_r[i].astype(F32) for i in range(4)).astype(BF)
        wait_for(x1_r.at[pl.ds(0, 3)], rsem.at[18])
        x2_s[...] = sum(x1_r[i].astype(F32) for i in range(4)).astype(BF)
        at_z, at_x = on_plane(0, my_x, 0), on_plane(0, my_z, 0)
        for dy, d in planes:
            send(z2_s.at[on_plane(dy, my_x, d)], z2_r.at[at_z],
                 ssem.at[28], rsem.at[28], (offset(dy, d, 0), dq))
            send(x2_s.at[on_plane(dy, my_z, d)], x2_r.at[at_x],
                 ssem.at[29], rsem.at[29], (offset(dy, 0, d), dq))
        z2_r[at_z] = z2_s[at_z]
        x2_r[at_x] = x2_s[at_x]

    def half_of(piece, i):
        return wbc_ref.at[piece, pl.ds(32 * i, 32), pl.ds(N, N)]

    def planes_back():
        wait_for(z2_r.at[pl.ds(0, 7)], rsem.at[28])
        wait_for(x2_r.at[pl.ds(0, 7)], rsem.at[29])
        wbc_ref[me, 0:32, N:] = sum(z2_r[i].astype(F32) for i in range(8)).astype(BF)
        wbc_ref[me, 32:64, N:] = sum(x2_r[i].astype(F32) for i in range(8)).astype(BF)
        for dy, d in planes:
            send(half_of(me, 0), half_of(me, 0), ssem.at[30], rsem.at[30], (offset(dy, d, 0), dq))
            send(half_of(me, 1), half_of(me, 1), ssem.at[31], rsem.at[31], (offset(dy, 0, d), dq))

    def lines_back():
        wait_for(wbc_ref.at[pl.ds(0, 7), pl.ds(0, 32), pl.ds(N, N)], rsem.at[30])
        wait_for(wbc_ref.at[pl.ds(0, 7), pl.ds(0, 32), pl.ds(N, N)], rsem.at[31])

        def one(i):
            y, other = i // 4, lax.rem(i, 4)
            for k in range(1, 4):
                piece = half_of(16 * y + 4 * other + my_z, 0)
                send(piece, piece, ssem.at[32], rsem.at[32], (offset(0, 0, k), dq))
                piece = half_of(16 * y + 4 * my_x + other, 1)
                send(piece, piece, ssem.at[33], rsem.at[33], (offset(0, k, 0), dq))

        loop(8, one)

    def grads_of_state(hp):
        wait_pair(hp, rh_ref, h_rsem)
        after = get_pair(rh_ref, hp)
        db_ref[...] += dot_nt(sc_ref[hp], after)
        weighed = dot(b_in, after) * x_ref[:, cols(hp)].astype(F32)
        decayed = jnp.sum(
            after.astype(F32) * get_pair(rs_ref, hp).astype(F32), axis=0, keepdims=True)
        for j in range(2):
            head = head0 + 2 * hp + j
            sub = slice(j * N, (j + 1) * N)
            dw_ref[...] += jnp.where(
                lane == head, jnp.sum(weighed[:, sub], axis=1, keepdims=True), 0.0)
            acc_ref[9:10, :HEADS] += jnp.where(
                lane1 == head, jnp.sum(decayed[:, sub], axis=1, keepdims=True), 0.0)

    for group in range(2):
        loop(4, lambda k: grads_of_state(pair_of(group, 4 - k)))

    left = jnp.exp(cend - cum)
    d_weight = dw_ref[...] * left
    d_gap = d_weight * dt
    d_end = jnp.sum(d_gap, axis=0, keepdims=True) + jnp.exp(cend) * acc_ref[9:10, :HEADS]
    d_cum = a_ref[...] - k_cols * dt - d_gap
    tri_up = jnp.where(row_i <= col_i, 1.0, 0.0).astype(BF)
    d_log = tri_sum(tri_up, d_cum) + d_end
    d_dt = k_cols + d_weight - rate * d_log
    d_pre = d_dt / (1.0 + jnp.exp(-pre)) * SCALE
    for i in range(2):
        half = slice(128 * i, 128 * i + 128)
        m3_tmp[i, 0:128] = db_ref[half] * SCALE
        m3_tmp[i, 128:192] = pack_rows(d_pre[half])
    sum_b.first()
    loss = jnp.sum(jnp.sum(acc_ref[0:8], axis=0, keepdims=True), axis=1, keepdims=True)
    zero = jnp.zeros((1, HEADS), F32)
    small = jnp.concatenate([
        jnp.broadcast_to(loss * (SCALE * SCALE * 0.5), (1, HEADS)),
        jnp.sum(d_log * log_rate, axis=0, keepdims=True) * SCALE,
        jnp.sum(d_pre, axis=0, keepdims=True),
        acc_ref[8:9, :HEADS] * SCALE,
        zero, zero, zero, zero], axis=0)
    sums_ref[...] = jnp.concatenate([small, jnp.zeros_like(small)], axis=1)
    sum_b.second()

    @pl.when(me != 0)
    def _():
        send(sums_ref, sroot_ref.at[me], ssem.at[24], rsem.at[24], (0, dq))

    lines_to_planes()
    sum_b.third()
    sum_b.last()

    g_b = m3_f[:, 0:128].reshape(T, N)
    g_dt = unpack_rows(m3_f.at[:, pl.ds(128, 64)]).astype(F32).T.astype(BF)

    def terms_b(g):
        part = xt_ref[pl.ds(pl.multiple_of(g * 512, 512), 512), :]
        term = dot(part, g_b).astype(BF).reshape(8, PIECE, N)
        for i in range(2):
            wsb_ref[i, pl.ds(8 * g, 8)] = term[:, 32 * i : 32 * i + 32]

    def terms_dt(g):
        wide = dot(g_dt, x_ref[:, pl.ds(pl.multiple_of(g * 512, 512), 512)]).astype(BF)
        for i in range(4):
            for j in range(2):
                wsb_ref[2, 4 * g + i + 16 * j] = wide[32 * j : 32 * j + 32, N * i : N * i + N]

    def send_terms(i):
        to_peers(lambda o: send(
            wsb_ref.at[i, o], rwb_ref.at[i, me], ssem.at[19], w_rsem.at[i], (o, dq)))
        rwb_ref[i, me] = wsb_ref[i, me]

    loop(4, terms_b)
    send_terms(0)
    loop(4, terms_dt)
    send_terms(1)
    send_terms(2)
    planes_back()

    @pl.when(me == 0)
    def _():
        sroot_ref[0] = sums_ref[...]
        wait_for(sroot_ref.at[pl.ds(0, SEQ - 1)], rsem.at[24])
        sdp_ref[dq] = jnp.sum(sroot_ref[...], axis=0)
        for k in range(1, DP):
            send(sdp_ref.at[dq], sdp_ref.at[dq], ssem.at[22], rsem.at[22],
                 (me, lax.rem(dq + k, DP)))

    own_parts = [wbc_ref.at[me, pl.ds(32 * i, 32), pl.ds(0, N)] for i in range(2)] + [
        wdt_ref.at[pl.ds(pl.multiple_of(32 * (me // 16), 32), 32),
                   pl.ds(pl.multiple_of(N * lax.rem(me, 16), N), N)]]

    def total_of(i):
        wait_for(rwb_ref.at[i, pl.ds(0, SEQ - 1)], w_rsem.at[i])
        total = lax.fori_loop(
            1, SEQ, lambda j, v: v + rwb_ref[i, j].astype(F32), rwb_ref[i, 0].astype(F32), unroll=4)
        own_parts[i][...] = total.astype(BF)
        to_peers(lambda o: send(
            own_parts[i], own_parts[i], ssem.at[20], rsem.at[19 + i], (o, dq)))

    total_of(0)
    total_of(1)
    total_of(2)
    lines_back()

    @pl.when(me == 0)
    def _():
        wait_for(sdp_ref.at[pl.ds(0, DP - 1)], rsem.at[22])
        sfin_ref[...] = jnp.sum(sdp_ref[...], axis=0)
        loop(SEQ - 1, lambda k: send(
            sfin_ref, sfin_ref, ssem.at[23], rsem.at[23], (peer(k + 1), dq)))
        wait_for(sdp_ref.at[pl.ds(0, DP - 1)], ssem.at[22])
        wait_for(sroot_ref.at[pl.ds(0, SEQ - 1)], ssem.at[23])

    @pl.when(me != 0)
    def _():
        wait_for(sums_ref, ssem.at[24])
        wait_for(sfin_ref, rsem.at[23])

    small_ref[...] = sfin_ref[...]

    for one in (sum_b1, sum_c1, sum_dt, sum_c, sum_b):
        one.sent()
    pieces = pl.ds(0, SEQ - 1)
    both = pl.ds(0, 2 * SEQ - 2)
    wait_for(ce_ref.at[pieces], ssem.at[12])
    for sem, ref in ((13, es_ref), (14, sf_ref), (15, gs_ref), (16, sh_ref)):
        wait_for(ref.at[both], ssem.at[sem])
    for sem in (19, 20):
        for i in range(3):
            wait_for(wsb_ref.at[i, pieces], ssem.at[sem])
    for i in range(3):
        wait_for(wsb_ref.at[i, pieces], rsem.at[19 + i])
    for i in range(2):
        wait_for(z1_s.at[pl.ds(0, 3)], ssem.at[17 + i])
        wait_for(z2_s.at[pl.ds(0, 7)], ssem.at[28 + i])
        wait_for(z2_s.at[pl.ds(0, 7)], ssem.at[30 + i])
        wait_for(z1_s.at[pl.ds(0, 3)], ssem.at[32 + i])
        wait_for(z1_s.at[pl.ds(0, 3)], rsem.at[32 + i])


def widen(wbc_ref, wdt_ref, small_ref, bc_hbm, dt_hbm, loss_ref, *rest):
    sums, (bc_ref, dt_ref, sem) = rest[:3], rest[3:]
    copies = []
    for i in range(4):
        bc_ref[i] = wbc_ref[8 * i : 8 * i + 8].astype(F32).reshape(512, 2 * N)
        copies.append(pltpu.make_async_copy(
            bc_ref.at[i], bc_hbm.at[pl.ds(512 * i, 512)], sem.at[i]))
        copies[-1].start()
    dt_ref[...] = wdt_ref[...].astype(F32)
    copies.append(pltpu.make_async_copy(dt_ref, dt_hbm, sem.at[4]))
    copies[-1].start()
    loss_ref[...] = small_ref[0:1, 0:1]
    for i, ref in enumerate(sums):
        ref[...] = small_ref[i + 1 : i + 2, :HEADS]
    for one in copies:
        one.wait()


def shards(teacher_rows, teacher_next, state_proj, step_proj, rate_log, step_bias, skip_gain):
    vmem = pl.BlockSpec(memory_space=pltpu.VMEM)
    hbm = pl.BlockSpec(memory_space=pl.ANY)

    def buf(*shape):
        return pltpu.VMEM(shape, BF)

    def f32(*shape):
        return pltpu.VMEM(shape, F32)

    def dp_bufs(rows, kind):
        return [f32(2, rows, N), kind(rows, N), kind(rows, N), buf(rows, N), buf(rows, N),
                kind(2, rows, N)]

    scratch = [
        buf(T, WIDTH), buf(T, WIDTH), buf(WIDTH, 2 * N), buf(HEADS, WIDTH), buf(WIDTH, T),
        *dp_bufs(128, buf), *dp_bufs(128, buf), *dp_bufs(64, f32), *dp_bufs(128, buf), *dp_bufs(192, buf),
        buf(T, 2 * HEADS), buf(2 * T, 3 * HEADS), buf(16, 3 * HEADS), f32(2 * HEADS, T),
        f32(PAIRS, T, 2 * N), f32(PAIRS, 8, 2 * N), buf(PAIRS, T, 2 * N),
        buf(2 * PAIRS, T, T), f32(PAIRS, T, 2 * N), f32(PAIRS, T, 2 * N), buf(PAIRS, T, 2 * N),
        f32(T, T), f32(T, T), f32(T, N), f32(T, N), f32(2 * HEADS, T), f32(T, HEADS), f32(T, HEADS),
        f32(16, 2 * N),
        f32(SEQ, 1, N), *[buf(2 * SEQ, PART, N) for _ in range(8)], f32(2 * SEQ, N),
        *[buf(4, 8, 32, N) for _ in range(4)], *[buf(8, 32, N) for _ in range(4)],
        buf(3, SEQ, 32, N), buf(3, SEQ, 32, N),
        f32(8, 128), f32(SEQ, 8, 128), f32(DP, 8, 128), f32(8, 128),
        pltpu.SemaphoreType.DMA((34,)), pltpu.SemaphoreType.DMA((34,)),
        pltpu.SemaphoreType.DMA((6,)), pltpu.SemaphoreType.DMA((PAIRS,)),
        pltpu.SemaphoreType.DMA((PAIRS,)), pltpu.SemaphoreType.DMA((3,)),
        pltpu.SemaphoreType.DMA((4,)), pltpu.SemaphoreType.REGULAR((2,)),
    ]
    state_grad, step_grad, small = pl.pallas_call(
        kernel,
        out_shape=(
            jax.ShapeDtypeStruct((SEQ, PIECE, 2 * N), BF),
            jax.ShapeDtypeStruct((HEADS, WIDTH), BF),
            jax.ShapeDtypeStruct((8, 128), F32),
        ),
        in_specs=[hbm, hbm, hbm, hbm, vmem],
        out_specs=(vmem, vmem, vmem),
        scratch_shapes=scratch,
        compiler_params=pltpu.CompilerParams(
            collective_id=0, has_side_effects=True, vmem_limit_bytes=52 * 1024 * 1024),
    )(teacher_rows, teacher_next, state_proj, step_proj.T,
      jnp.stack([rate_log, step_bias, skip_gain]))
    heads = jax.ShapeDtypeStruct((1, HEADS), F32)
    state_grad, step_grad, loss, *sums = pl.pallas_call(
        widen,
        out_shape=(
            jax.ShapeDtypeStruct((WIDTH, 2 * N), F32),
            jax.ShapeDtypeStruct((HEADS, WIDTH), F32),
            jax.ShapeDtypeStruct((1, 1), F32), heads, heads, heads,
        ),
        in_specs=[vmem] * 3,
        out_specs=(hbm, hbm, vmem, vmem, vmem, vmem),
        scratch_shapes=[f32(4, 512, 2 * N), f32(HEADS, WIDTH), pltpu.SemaphoreType.DMA((5,))],
        compiler_params=pltpu.CompilerParams(vmem_limit_bytes=16 * 1024 * 1024),
    )(state_grad, step_grad, small)
    return (loss[0, 0], state_grad, step_grad.T, *(v[0] for v in sums))


def solution(mesh):
    placed = (P("seq", "dp"), P("seq", "dp"), P(), P(), P(), P(), P())
    return jax.shard_map(
        shards,
        mesh=mesh,
        in_specs=placed,
        out_specs=(P(), P("dp", None), P("dp", None), P(), P(), P()),
        check_vma=False,
    )
```

```python
import functools

import jax
import jax.numpy as jnp
from jax import lax
from jax.experimental import pallas as pl
from jax.experimental.pallas import tpu as pltpu
from jax.sharding import PartitionSpec as P

SEQ, DP = 32, 4
T = 256
WIDTH = 2048
HEADS = 64
PAIRS = 8
N = 128
PIECE = 64
PART = 32
MESH = pl.DeviceIdType.MESH
BF, F32 = jnp.bfloat16, jnp.float32
SCALE = 1.0 / 8192.0


def dot(a, b):
    return jnp.dot(a, b, preferred_element_type=F32)


def dot_nt(a, b):
    return lax.dot_general(a, b, (((1,), (1,)), ((), ())), preferred_element_type=F32)


def split3(v):
    hi = v.astype(BF).astype(F32)
    rest = v - hi
    mid = rest.astype(BF).astype(F32)
    return hi, mid, rest - mid


def tri_sum(tri, v):
    return sum(dot(tri, part.astype(BF)) for part in split3(v))


def send(src, dst, send_sem, recv_sem, device):
    pltpu.make_async_remote_copy(
        src_ref=src, dst_ref=dst, send_sem=send_sem, recv_sem=recv_sem,
        device_id=device, device_id_type=MESH,
    ).start()


def wait_for(ref, sem):
    pltpu.make_async_copy(ref, ref, sem).wait()


def loop(count, body):
    lax.fori_loop(0, count, lambda k, c: (body(k), c)[1], 0)


def pack_rows(v):
    return jnp.concatenate([v[:64], v[64:]], axis=1)


def unpack_rows(ref):
    return jnp.concatenate([ref[i][:, j : j + 64] for i in range(2) for j in (0, 64)], axis=0)


def kernel(
    x_hbm, tgt_hbm, sp_ref, st_ref, heads_ref,
    wbc_ref, wdt_ref, small_ref,
    x_ref, tgt_ref, w_bc, w_dt, xt_ref,
    m0_tmp, m0_sa, m0_ra, m0_sb, m0_rb, m0_f,
    m1_tmp, m1_sa, m1_ra, m1_sb, m1_rb, m1_f,
    d1_tmp, d1_sa, d1_ra, d1_sb, d1_rb, d1_f,
    m2_tmp, m2_sa, m2_ra, m2_sb, m2_rb, m2_f,
    m3_tmp, m3_sa, m3_ra, m3_sb, m3_rb, m3_f,
    weight_ref, stack_ref, skips_ref, rows_ref, cx_ref, sk_ref, sc_ref, l_ref, z_ref, err_ref, de_ref,
    sm_ref, dsc_ref, dc_ref, db_ref, k_ref, a_ref, dw_ref, acc_ref,
    ce_ref, es_ref, re_ref, sf_ref, rs_ref, gs_ref, rg_ref, sh_ref, rh_ref, dec_ref,
    z1_s, z1_r, x1_s, x1_r, z2_s, z2_r, x2_s, x2_r, wsb_ref, rwb_ref, sums_ref, sroot_ref, sdp_ref, sfin_ref,
    ssem, rsem, g_rsem, s_rsem, w_rsem, lsem, go,
):
    me, dq = lax.axis_index("seq"), lax.axis_index("dp")
    head0 = dq * (HEADS // DP)
    core = lax.rem(dq, 2)
    sibling = dq + 1 - 2 * core
    across = lax.rem(dq + 2, DP)

    def peer(k):
        return lax.rem(me + k, SEQ)

    def offset(dy, dx, dz):
        y, x, z = me // 16, lax.rem(me // 4, 4), lax.rem(me, 4)
        return lax.rem(y + dy, 2) * 16 + lax.rem(x + dx, 4) * 4 + lax.rem(z + dz, 4)

    def signal(sem, device):
        pl.semaphore_signal(sem, inc=1, device_id=device, device_id_type=MESH)

    def to_peers(start):
        def one(k):
            k = k + 1
            start(peer(k))

        loop(SEQ - 1, one)

    barrier = pltpu.get_barrier_semaphore()
    z_line = [(0, 0, k) for k in (1, 2, 3)]
    x_line = [(0, k, 0) for k in (1, 2, 3)]
    for k in range(1, DP):
        signal(barrier, (me, lax.rem(dq + k, DP)))
    for at in z_line + x_line + [(1, 0, 0)]:
        signal(barrier, (offset(*at), dq))
    own = pl.ds(pl.multiple_of(dq * WIDTH, WIDTH), WIDTH)
    load_x = pltpu.make_async_copy(x_hbm, x_ref, lsem.at[0])
    load_bc = pltpu.make_async_copy(sp_ref.at[own], w_bc, lsem.at[1])
    load_dt = pltpu.make_async_copy(st_ref.at[:, own], w_dt, lsem.at[2])
    load_tgt = pltpu.make_async_copy(tgt_hbm, tgt_ref, lsem.at[3])
    load_x.start()
    load_bc.start()
    load_dt.start()
    load_tgt.start()
    load_x.wait()
    load_bc.wait()
    load_dt.wait()

    class DpSum:
        def __init__(self, sem, tmp, sa, ra, sb, rb, f):
            self.sem, self.tmp, self.sa, self.ra, self.sb, self.rb, self.f = sem, tmp, sa, ra, sb, rb, f

        def send(self, src, dst, step, member):
            send(src, dst, ssem.at[self.sem + step], rsem.at[self.sem + step], (me, member))

        def first(self):
            self.sa[...] = self.tmp[1 - core].astype(self.sa.dtype)
            self.send(self.sa, self.ra, 0, sibling)

        def second(self):
            wait_for(self.ra, rsem.at[self.sem])
            chip = self.tmp[core] + self.ra[...].astype(F32)
            self.tmp[core] = chip
            self.sb[...] = chip.astype(self.sb.dtype)
            self.send(self.sb, self.rb, 1, across)

        def third(self):
            wait_for(self.rb, rsem.at[self.sem + 1])
            self.f[core] = (self.tmp[core] + self.rb[...].astype(F32)).astype(self.f.dtype)
            self.send(self.f.at[core], self.f.at[core], 2, sibling)

        def last(self):
            wait_for(self.f.at[0], rsem.at[self.sem + 2])

        def sent(self):
            for step, ref in enumerate((self.sa, self.sb, self.f.at[0])):
                wait_for(ref, ssem.at[self.sem + step])

    sum_b1 = DpSum(0, m0_tmp, m0_sa, m0_ra, m0_sb, m0_rb, m0_f)
    sum_c1 = DpSum(25, m1_tmp, m1_sa, m1_ra, m1_sb, m1_rb, m1_f)
    sum_dt = DpSum(3, d1_tmp, d1_sa, d1_ra, d1_sb, d1_rb, d1_f)
    sum_c = DpSum(6, m2_tmp, m2_sa, m2_ra, m2_sb, m2_rb, m2_f)
    sum_b = DpSum(9, m3_tmp, m3_sa, m3_ra, m3_sb, m3_rb, m3_f)

    x_all = x_ref[...]
    part_dt = dot_nt(x_all, w_dt[...])
    part_bc = dot(x_all, w_bc[...])
    for i in range(2):
        half = slice(128 * i, 128 * i + 128)
        d1_tmp[i] = pack_rows(part_dt[half])
        m0_tmp[i] = part_bc[half, :N]
        m1_tmp[i] = part_bc[half, N:]
    pl.semaphore_wait(barrier, DP - 1 + 7)
    sum_dt.first()
    sum_b1.first()
    sum_c1.first()
    for at in x_line:
        signal(go.at[0], (offset(*at), dq))
    sum_dt.second()
    sum_b1.second()
    sum_c1.second()
    pl.semaphore_wait(go.at[0], 3)
    signal(go.at[1], (offset(1, 0, 0), dq))
    sum_dt.third()
    sum_b1.third()
    sum_dt.last()

    pre = unpack_rows(d1_f) + heads_ref[1:2]
    dt = jnp.maximum(pre, 0.0) + jnp.log1p(jnp.exp(-jnp.abs(pre)))
    rate = jnp.exp(heads_ref[0:1])
    log_rate = -rate * dt
    row_i = lax.broadcasted_iota(jnp.int32, (T, T), 0)
    col_i = lax.broadcasted_iota(jnp.int32, (T, T), 1)
    tri = jnp.where(row_i >= col_i, 1.0, 0.0).astype(BF)
    cum = tri_sum(tri, log_rate)
    cend = cum[T - 1 : T]
    weight = dt * jnp.exp(cend - cum)
    high = weight.astype(BF).astype(F32)
    weight_ref[...] = jnp.concatenate([high, weight - high], axis=1).astype(BF)
    ce_ref[me] = jnp.concatenate([cend, cend], axis=1)
    sum_b1.last()
    b_in = m0_f[...].reshape(T, N)
    b_t = b_in.astype(F32).T.astype(BF)
    pl.semaphore_wait(go.at[1], 1)
    loop(SEQ - 1, lambda k: send(
        ce_ref.at[me], ce_ref.at[me], ssem.at[12], rsem.at[12], (peer(k + 1), dq)))
    sel_row = lax.rem(lax.broadcasted_iota(jnp.int32, (3 * HEADS, 2 * N), 0), HEADS)
    sel_col = lax.broadcasted_iota(jnp.int32, (3 * HEADS, 2 * N), 1) // N

    def cols(hp):
        return pl.ds(pl.multiple_of(hp * 2 * N, 2 * N), 2 * N)

    def pick(hp):
        return jnp.where(sel_row == head0 + 2 * hp + sel_col, 1.0, 0.0).astype(BF)

    def pair_of(group, k):
        return 4 * group + lax.rem(me // 8 + k, 4)

    def each_of(hp, body):
        def one(i):
            at = 8 * hp + lax.rem(me + i, 8)
            o = lax.rem(at, SEQ)

            @pl.when(o != me)
            def _():
                body(at, o)

        loop(8, one)

    def send_pair(hp, src, dst, sem):
        each_of(hp, lambda at, o: send(
            src.at[at], dst.at[SEQ * (hp // 4) + me],
            ssem.at[sem], g_rsem.at[2 * (sem - 13) + hp // 4], (o, dq)))

    def wait_pair(hp, ref, sems):
        mine = (SEQ * (hp // 4) + me) // 8 == hp

        @pl.when(mine)
        def _():
            wait_for(ref.at[pl.ds(8 * hp, 7)], sems.at[hp])

        @pl.when(jnp.logical_not(mine))
        def _():
            wait_for(ref.at[pl.ds(8 * hp, 8)], sems.at[hp])

    def send_all(group, src, dst, sem, sems, slot=None):
        def one(k):
            o = peer(k + 1)
            send(src.at[SEQ * group + o], dst.at[SEQ * group + me],
                 ssem.at[sem], sems.at[(SEQ * group + me) // 8 if slot is None else slot], (o, dq))

        loop(SEQ - 1, one)
        dst[SEQ * group + me] = src[SEQ * group + me]

    def put_pair(ref, hp, value):
        for i in range(8):
            ref[8 * hp + i] = value[
                (i % 4) * PART : (i % 4 + 1) * PART, (i // 4) * N : (i // 4 + 1) * N].astype(BF)

    def get_pair(ref, hp):
        v = ref[pl.ds(8 * hp, 8)]
        return jnp.concatenate([v[:4].reshape(N, N), v[4:].reshape(N, N)], axis=1)

    def wait_group(group, ref, sem):
        wait_for(ref.at[pl.ds(SEQ * group, SEQ - 1)], g_rsem.at[2 * (sem - 13) + group])

    wide_row = lax.rem(lax.broadcasted_iota(jnp.int32, (2 * HEADS, 8 * N), 0), HEADS)
    wide_col = lax.broadcasted_iota(jnp.int32, (2 * HEADS, 8 * N), 1) // N
    for group in range(2):
        sel = jnp.where(wide_row == head0 + 8 * group + wide_col, 1.0, 0.0).astype(BF)
        wide = dot(weight_ref[...], sel)
        at = slice(8 * N * group, 8 * N * (group + 1))
        sc = (x_ref[:, at].astype(F32) * wide).astype(BF)
        sc_ref[group] = sc
        term = dot(b_t, sc).astype(BF)
        for i in range(SEQ):
            es_ref[SEQ * group + i] = term[
                (i % 4) * PART : (i % 4 + 1) * PART, (i // 4) * N : (i // 4 + 1) * N]
        send_all(group, es_ref, re_ref, 13, g_rsem, group)

    sum_c1.third()
    stack_ref[0:T] = jnp.concatenate(split3(cum), axis=1).astype(BF)
    stack_ref[T : 2 * T] = jnp.concatenate(split3(dt), axis=1).astype(BF)
    rows_ref[...] = jnp.concatenate([cum, dt], axis=1).T
    sum_c1.last()
    c_out = m1_f[...].reshape(T, N)
    sm_ref[...] = jnp.where(row_i >= col_i, dot_nt(c_out, b_in), 0.0)
    skips_ref[...] = jnp.concatenate(
        split3(jnp.broadcast_to(heads_ref[2:3], (16, HEADS))), axis=1).astype(BF)

    def in_block(hp):
        sk_ref[hp] = dot(skips_ref[...], pick(hp))[:8]
        wide = dot(stack_ref[...], pick(hp))
        cx_ref[hp] = wide[:T]
        xd = (x_ref[:, cols(hp)].astype(F32) * wide[T:]).astype(BF)
        parts = []
        for j in range(2):
            cx = wide[:T, j * N : (j + 1) * N]
            gap = jnp.concatenate([cx, cx], axis=1) - rows_ref[pl.ds(head0 + 2 * hp + j, 1), :]
            decay = jnp.exp(jnp.minimum(gap, 0.0))
            l_ref[2 * hp + j] = decay.astype(BF)
            w = (decay * sm_ref[...]).astype(BF)
            parts.append(dot(w, xd[:, j * N : (j + 1) * N]))
        z_ref[hp] = jnp.concatenate(parts, axis=1)

    loop(PAIRS, in_block)
    load_tgt.wait()
    c_t = c_out.astype(F32).T.astype(BF)

    wait_for(ce_ref.at[pl.ds(0, SEQ - 1)], rsem.at[12])
    ends = jnp.concatenate(split3(ce_ref[...].reshape(SEQ, N)[:, :HEADS]), axis=1).astype(BF)
    for group in range(2):
        sel_own = jnp.where(
            sel_row[:, :N] == head0 + 8 * group + me // 4, 1.0, 0.0).astype(BF)
        dec_ref[SEQ * group : SEQ * group + SEQ] = jnp.exp(dot(ends, sel_own))

    def forward(at, state):
        sf_ref[at] = state.astype(BF)
        return dec_ref[pl.ds(at, 1), :] * state + re_ref[at].astype(F32)

    for group in range(2):
        wait_group(group, re_ref, 13)
        lax.fori_loop(SEQ * group, SEQ * group + SEQ, forward, jnp.zeros((PART, N), F32), unroll=8)
        send_all(group, sf_ref, rs_ref, 14, s_rsem)

    def turn(i):
        at = pl.ds(pl.multiple_of(i * 2 * N, 2 * N), 2 * N)
        xt_ref[at, :] = x_ref[:, at].astype(F32).T.astype(BF)

    loop(PAIRS, turn)
    acc_ref[...] = jnp.zeros_like(acc_ref)

    def errors(hp):
        at = cols(hp)
        wait_pair(hp, rs_ref, s_rsem)
        decay = jnp.exp(cx_ref[hp])
        z = z_ref[hp] + dot(c_out, get_pair(rs_ref, hp)) * decay
        z_ref[hp] = z
        err = (z + sk_ref[hp][:1] * x_ref[:, at].astype(F32)) - tgt_ref[:, at].astype(F32)
        err_ref[hp] = err
        de = (err * decay).astype(BF)
        de_ref[hp] = de
        put_pair(gs_ref, hp, dot(c_t, de))
        acc_ref[0:8] += jnp.sum((err * err).reshape(T // 8, 8, 2 * N), axis=0)

    for group in range(2):
        loop(4, lambda k: errors(pair_of(group, 4 - k)))
        send_all(group, gs_ref, rg_ref, 15, g_rsem, 4 + group)

    lane = lax.broadcasted_iota(jnp.int32, (T, HEADS), 1)
    lane1 = lax.broadcasted_iota(jnp.int32, (1, HEADS), 1)
    for ref in (dsc_ref, dc_ref, db_ref, k_ref, a_ref, dw_ref):
        ref[...] = jnp.zeros_like(ref)

    def grads_in_block(hp):
        at = cols(hp)
        xp = x_ref[:, at]
        err = err_ref[hp]
        errb = err.astype(BF)
        dc_ref[...] += dot_nt(de_ref[hp], get_pair(rs_ref, hp))
        rowed = err * z_ref[hp]
        skipped = jnp.sum(err * xp.astype(F32), axis=0, keepdims=True)
        for j in range(2):
            head = head0 + 2 * hp + j
            sub = slice(j * N, (j + 1) * N)
            dwd = dot_nt(errb[:, sub], xp[:, sub]) * l_ref[2 * hp + j].astype(F32)
            dsc_ref[...] += dwd * rows_ref[pl.ds(HEADS + head, 1), :]
            k_ref[pl.ds(head, 1), :] = jnp.sum(dwd * sm_ref[...], axis=0, keepdims=True)
            a_ref[...] += jnp.where(
                lane == head, jnp.sum(rowed[:, sub], axis=1, keepdims=True), 0.0)
            acc_ref[8:9, :HEADS] += jnp.where(
                lane1 == head, jnp.sum(skipped[:, sub], axis=1, keepdims=True), 0.0)

    loop(PAIRS, grads_in_block)
    dsc = jnp.where(row_i >= col_i, dsc_ref[...], 0.0)
    m2_tmp[...] = ((dc_ref[...] + dot(dsc.astype(BF), b_in)) * SCALE).reshape(2, 128, N)
    sum_c.first()
    db_ref[...] = dot(dsc.T.astype(BF), c_out)
    sum_c.second()
    k_cols = k_ref[...].T[:, :HEADS]
    def backward(i, state, group):
        at = SEQ * group + SEQ - 1 - i
        sh_ref[at] = state.astype(BF)
        return dec_ref[pl.ds(at, 1), :] * state + rg_ref[at].astype(F32)

    for group in range(2):
        wait_group(group, rg_ref, 15)
        lax.fori_loop(0, SEQ, functools.partial(backward, group=group),
                      jnp.zeros((PART, N), F32), unroll=8)
        send_all(group, sh_ref, rh_ref, 16, g_rsem, 6 + group)

    sum_c.third()
    sum_c.last()

    my_y, my_x, my_z = me // 16, lax.rem(me // 4, 4), lax.rem(me, 4)
    g_c = m2_f[...].reshape(T, N)
    for g in range(4):
        term = dot(xt_ref[512 * g : 512 * g + 512, :], g_c).astype(BF).reshape(8, PIECE, N)
        for i in range(8):
            y, x, z = g // 2, 2 * (g % 2) + i // 4, i % 4
            z1_s[z, 4 * y + x] = term[i, :32]
            x1_s[x, 4 * y + z] = term[i, 32:]
    for k in range(1, 4):
        to = lax.rem(my_z + k, 4)
        send(z1_s.at[to], z1_r.at[my_z], ssem.at[17], rsem.at[17], (offset(0, 0, k), dq))
        to = lax.rem(my_x + k, 4)
        send(x1_s.at[to], x1_r.at[my_x], ssem.at[18], rsem.at[18], (offset(0, k, 0), dq))
    z1_r[my_z] = z1_s[my_z]
    x1_r[my_x] = x1_s[my_x]
    planes = [(dy, d) for dy in (1, 0) for d in (2, 1, 3, 0)][:7]

    def on_plane(dy, mine, d):
        return 4 * lax.rem(my_y + dy, 2) + lax.rem(mine + d, 4)

    def lines_to_planes():
        wait_for(z1_r.at[pl.ds(0, 3)], rsem.at[17])
        z2_s[...] = sum(z1_r[i].astype(F32) for i in range(4)).astype(BF)
        wait_for(x1_r.at[pl.ds(0, 3)], rsem.at[18])
        x2_s[...] = sum(x1_r[i].astype(F32) for i in range(4)).astype(BF)
        at_z, at_x = on_plane(0, my_x, 0), on_plane(0, my_z, 0)
        for dy, d in planes:
            send(z2_s.at[on_plane(dy, my_x, d)], z2_r.at[at_z],
                 ssem.at[28], rsem.at[28], (offset(dy, d, 0), dq))
            send(x2_s.at[on_plane(dy, my_z, d)], x2_r.at[at_x],
                 ssem.at[29], rsem.at[29], (offset(dy, 0, d), dq))
        z2_r[at_z] = z2_s[at_z]
        x2_r[at_x] = x2_s[at_x]

    def half_of(piece, i):
        return wbc_ref.at[piece, pl.ds(32 * i, 32), pl.ds(N, N)]

    def planes_back():
        wait_for(z2_r.at[pl.ds(0, 7)], rsem.at[28])
        wait_for(x2_r.at[pl.ds(0, 7)], rsem.at[29])
        wbc_ref[me, 0:32, N:] = sum(z2_r[i].astype(F32) for i in range(8)).astype(BF)
        wbc_ref[me, 32:64, N:] = sum(x2_r[i].astype(F32) for i in range(8)).astype(BF)
        for dy, d in planes:
            send(half_of(me, 0), half_of(me, 0), ssem.at[30], rsem.at[30], (offset(dy, d, 0), dq))
            send(half_of(me, 1), half_of(me, 1), ssem.at[31], rsem.at[31], (offset(dy, 0, d), dq))

    def lines_back():
        wait_for(wbc_ref.at[pl.ds(0, 7), pl.ds(0, 32), pl.ds(N, N)], rsem.at[30])
        wait_for(wbc_ref.at[pl.ds(0, 7), pl.ds(0, 32), pl.ds(N, N)], rsem.at[31])

        def one(i):
            y, other = i // 4, lax.rem(i, 4)
            for k in range(1, 4):
                piece = half_of(16 * y + 4 * other + my_z, 0)
                send(piece, piece, ssem.at[32], rsem.at[32], (offset(0, 0, k), dq))
                piece = half_of(16 * y + 4 * my_x + other, 1)
                send(piece, piece, ssem.at[33], rsem.at[33], (offset(0, k, 0), dq))

        loop(8, one)

    sum_row = lax.broadcasted_iota(jnp.int32, (8 * N, HEADS), 0) // N
    sum_col = lax.broadcasted_iota(jnp.int32, (8 * N, HEADS), 1)
    for group in range(2):
        to_head = jnp.where(sum_col == head0 + 8 * group + sum_row, 1.0, 0.0).astype(BF)

        def by_head(v):
            high = v.astype(BF)
            return dot(high, to_head) + dot((v - high.astype(F32)).astype(BF), to_head)

        wait_group(group, rh_ref, 16)
        pairs = range(4 * group, 4 * group + 4)
        after = jnp.concatenate([get_pair(rh_ref, hp) for hp in pairs], axis=1)
        before = jnp.concatenate([get_pair(rs_ref, hp) for hp in pairs], axis=1)
        at = slice(8 * N * group, 8 * N * (group + 1))
        db_ref[...] += dot_nt(sc_ref[group], after)
        dw_ref[...] += by_head(dot(b_in, after) * x_ref[:, at].astype(F32))
        decayed = after.astype(F32) * before.astype(F32)
        acc_ref[16:24, :HEADS] += by_head(jnp.sum(decayed.reshape(16, 8, 8 * N), axis=0))

    left = jnp.exp(cend - cum)
    d_weight = dw_ref[...] * left
    d_gap = d_weight * dt
    d_end = jnp.sum(d_gap, axis=0, keepdims=True) + jnp.exp(cend) * jnp.sum(acc_ref[16:24, :HEADS], axis=0, keepdims=True)
    d_cum = a_ref[...] - k_cols * dt - d_gap
    tri_up = jnp.where(row_i <= col_i, 1.0, 0.0).astype(BF)
    d_log = tri_sum(tri_up, d_cum) + d_end
    d_dt = k_cols + d_weight - rate * d_log
    d_pre = d_dt / (1.0 + jnp.exp(-pre)) * SCALE
    for i in range(2):
        half = slice(128 * i, 128 * i + 128)
        m3_tmp[i, 0:128] = db_ref[half] * SCALE
        m3_tmp[i, 128:192] = pack_rows(d_pre[half])
    sum_b.first()
    loss = jnp.sum(jnp.sum(acc_ref[0:8], axis=0, keepdims=True), axis=1, keepdims=True)
    zero = jnp.zeros((1, HEADS), F32)
    small = jnp.concatenate([
        jnp.broadcast_to(loss * (SCALE * SCALE * 0.5), (1, HEADS)),
        jnp.sum(d_log * log_rate, axis=0, keepdims=True) * SCALE,
        jnp.sum(d_pre, axis=0, keepdims=True),
        acc_ref[8:9, :HEADS] * SCALE,
        zero, zero, zero, zero], axis=0)
    sums_ref[...] = jnp.concatenate([small, jnp.zeros_like(small)], axis=1)
    sum_b.second()

    @pl.when(me != 0)
    def _():
        send(sums_ref, sroot_ref.at[me], ssem.at[24], rsem.at[24], (0, dq))

    lines_to_planes()
    sum_b.third()
    sum_b.last()

    g_b = m3_f[:, 0:128].reshape(T, N)
    g_dt = unpack_rows(m3_f.at[:, pl.ds(128, 64)]).astype(F32).T.astype(BF)

    def terms_dt(g):
        wide = dot(g_dt, x_ref[:, pl.ds(pl.multiple_of(g * 512, 512), 512)]).astype(BF)
        for i in range(4):
            for j in range(2):
                wsb_ref[2, 4 * g + i + 16 * j] = wide[32 * j : 32 * j + 32, N * i : N * i + N]

    def send_terms(i):
        to_peers(lambda o: send(
            wsb_ref.at[i, o], rwb_ref.at[i, me], ssem.at[19], w_rsem.at[i], (o, dq)))
        rwb_ref[i, me] = wsb_ref[i, me]

    term = dot(xt_ref[...], g_b).astype(BF).reshape(SEQ, PIECE, N)
    for i in range(2):
        wsb_ref[i] = term[:, 32 * i : 32 * i + 32]
    send_terms(0)
    loop(4, terms_dt)
    send_terms(1)
    send_terms(2)
    planes_back()

    @pl.when(me == 0)
    def _():
        sroot_ref[0] = sums_ref[...]
        wait_for(sroot_ref.at[pl.ds(0, SEQ - 1)], rsem.at[24])
        sdp_ref[dq] = jnp.sum(sroot_ref[...], axis=0)
        for k in range(1, DP):
            send(sdp_ref.at[dq], sdp_ref.at[dq], ssem.at[22], rsem.at[22],
                 (me, lax.rem(dq + k, DP)))

    own_parts = [wbc_ref.at[me, pl.ds(32 * i, 32), pl.ds(0, N)] for i in range(2)] + [
        wdt_ref.at[pl.ds(pl.multiple_of(32 * (me // 16), 32), 32),
                   pl.ds(pl.multiple_of(N * lax.rem(me, 16), N), N)]]

    def total_of(i):
        wait_for(rwb_ref.at[i, pl.ds(0, SEQ - 1)], w_rsem.at[i])
        total = lax.fori_loop(
            1, SEQ, lambda j, v: v + rwb_ref[i, j].astype(F32), rwb_ref[i, 0].astype(F32), unroll=4)
        own_parts[i][...] = total.astype(BF)
        to_peers(lambda o: send(
            own_parts[i], own_parts[i], ssem.at[20], rsem.at[19 + i], (o, dq)))

    total_of(0)
    total_of(1)
    total_of(2)
    lines_back()

    @pl.when(me == 0)
    def _():
        wait_for(sdp_ref.at[pl.ds(0, DP - 1)], rsem.at[22])
        sfin_ref[...] = jnp.sum(sdp_ref[...], axis=0)
        loop(SEQ - 1, lambda k: send(
            sfin_ref, sfin_ref, ssem.at[23], rsem.at[23], (peer(k + 1), dq)))
        wait_for(sdp_ref.at[pl.ds(0, DP - 1)], ssem.at[22])
        wait_for(sroot_ref.at[pl.ds(0, SEQ - 1)], ssem.at[23])

    @pl.when(me != 0)
    def _():
        wait_for(sums_ref, ssem.at[24])
        wait_for(sfin_ref, rsem.at[23])

    small_ref[...] = sfin_ref[...]

    for one in (sum_b1, sum_c1, sum_dt, sum_c, sum_b):
        one.sent()
    pieces = pl.ds(0, SEQ - 1)
    both = pl.ds(0, 2 * SEQ - 2)
    wait_for(ce_ref.at[pieces], ssem.at[12])
    for sem, ref in ((13, es_ref), (14, sf_ref), (15, gs_ref), (16, sh_ref)):
        wait_for(ref.at[both], ssem.at[sem])
    for sem in (19, 20):
        for i in range(3):
            wait_for(wsb_ref.at[i, pieces], ssem.at[sem])
    for i in range(3):
        wait_for(wsb_ref.at[i, pieces], rsem.at[19 + i])
    for i in range(2):
        wait_for(z1_s.at[pl.ds(0, 3)], ssem.at[17 + i])
        wait_for(z2_s.at[pl.ds(0, 7)], ssem.at[28 + i])
        wait_for(z2_s.at[pl.ds(0, 7)], ssem.at[30 + i])
        wait_for(z1_s.at[pl.ds(0, 3)], ssem.at[32 + i])
        wait_for(z1_s.at[pl.ds(0, 3)], rsem.at[32 + i])


def widen(wbc_ref, wdt_ref, small_ref, bc_hbm, dt_hbm, *rest):
    outs, (bc_ref, dt_ref, loss_ref, heads_ref, sem) = rest[:4], rest[4:]
    copies = []

    def put(src, dst):
        copies.append(pltpu.make_async_copy(src, dst, sem.at[len(copies)]))
        copies[-1].start()

    loss_ref[...] = small_ref[0:1, 0:1]
    put(loss_ref, outs[0])
    for i in range(3):
        heads_ref[i] = small_ref[i + 1 : i + 2, :HEADS]
        put(heads_ref.at[i], outs[i + 1])
    dt_ref[...] = wdt_ref[...].astype(F32)
    put(dt_ref, dt_hbm)
    for i in range(4):
        bc_ref[i] = wbc_ref[8 * i : 8 * i + 8].astype(F32).reshape(512, 2 * N)
        put(bc_ref.at[i], bc_hbm.at[pl.ds(512 * i, 512)])
    for one in copies:
        one.wait()


def shards(teacher_rows, teacher_next, state_proj, step_proj, rate_log, step_bias, skip_gain):
    vmem = pl.BlockSpec(memory_space=pltpu.VMEM)
    hbm = pl.BlockSpec(memory_space=pl.ANY)

    def buf(*shape):
        return pltpu.VMEM(shape, BF)

    def f32(*shape):
        return pltpu.VMEM(shape, F32)

    def dp_bufs(rows, kind):
        return [f32(2, rows, N), kind(rows, N), kind(rows, N), buf(rows, N), buf(rows, N),
                kind(2, rows, N)]

    scratch = [
        buf(T, WIDTH), buf(T, WIDTH), buf(WIDTH, 2 * N), buf(HEADS, WIDTH), buf(WIDTH, T),
        *dp_bufs(128, buf), *dp_bufs(128, buf), *dp_bufs(64, f32), *dp_bufs(128, buf), *dp_bufs(192, buf),
        buf(T, 2 * HEADS), buf(2 * T, 3 * HEADS), buf(16, 3 * HEADS), f32(2 * HEADS, T),
        f32(PAIRS, T, 2 * N), f32(PAIRS, 8, 2 * N), buf(2, T, 8 * N),
        buf(2 * PAIRS, T, T), f32(PAIRS, T, 2 * N), f32(PAIRS, T, 2 * N), buf(PAIRS, T, 2 * N),
        f32(T, T), f32(T, T), f32(T, N), f32(T, N), f32(2 * HEADS, T), f32(T, HEADS), f32(T, HEADS),
        f32(24, 2 * N),
        f32(SEQ, 1, N), *[buf(2 * SEQ, PART, N) for _ in range(8)], f32(2 * SEQ, N),
        *[buf(4, 8, 32, N) for _ in range(4)], *[buf(8, 32, N) for _ in range(4)],
        buf(3, SEQ, 32, N), buf(3, SEQ, 32, N),
        f32(8, 128), f32(SEQ, 8, 128), f32(DP, 8, 128), f32(8, 128),
        pltpu.SemaphoreType.DMA((34,)), pltpu.SemaphoreType.DMA((34,)),
        pltpu.SemaphoreType.DMA((8,)), pltpu.SemaphoreType.DMA((PAIRS,)), pltpu.SemaphoreType.DMA((3,)),
        pltpu.SemaphoreType.DMA((4,)), pltpu.SemaphoreType.REGULAR((2,)),
    ]
    state_grad, step_grad, small = pl.pallas_call(
        kernel,
        out_shape=(
            jax.ShapeDtypeStruct((SEQ, PIECE, 2 * N), BF),
            jax.ShapeDtypeStruct((HEADS, WIDTH), BF),
            jax.ShapeDtypeStruct((8, 128), F32),
        ),
        in_specs=[hbm, hbm, hbm, hbm, vmem],
        out_specs=(vmem, vmem, vmem),
        scratch_shapes=scratch,
        compiler_params=pltpu.CompilerParams(
            collective_id=0, has_side_effects=True, vmem_limit_bytes=52 * 1024 * 1024),
    )(teacher_rows, teacher_next, state_proj, step_proj.T,
      jnp.stack([rate_log, step_bias, skip_gain]))
    heads = jax.ShapeDtypeStruct((1, HEADS), F32)
    state_grad, step_grad, loss, *sums = pl.pallas_call(
        widen,
        out_shape=(
            jax.ShapeDtypeStruct((WIDTH, 2 * N), F32),
            jax.ShapeDtypeStruct((HEADS, WIDTH), F32),
            jax.ShapeDtypeStruct((1, 1), F32), heads, heads, heads,
        ),
        in_specs=[vmem] * 3,
        out_specs=(hbm,) * 6,
        scratch_shapes=[f32(4, 512, 2 * N), f32(HEADS, WIDTH), f32(1, 1), f32(3, 1, HEADS),
                        pltpu.SemaphoreType.DMA((9,))],
        compiler_params=pltpu.CompilerParams(vmem_limit_bytes=16 * 1024 * 1024),
    )(state_grad, step_grad, small)
    return (loss[0, 0], state_grad, step_grad.T, *(v[0] for v in sums))


def solution(mesh):
    placed = (P("seq", "dp"), P("seq", "dp"), P(), P(), P(), P(), P())
    return jax.shard_map(
        shards,
        mesh=mesh,
        in_specs=placed,
        out_specs=(P(), P("dp", None), P("dp", None), P(), P(), P()),
        check_vma=False,
    )
```

```python
import functools

import jax
import jax.numpy as jnp
from jax import lax
from jax.experimental import pallas as pl
from jax.experimental.pallas import tpu as pltpu
from jax.sharding import PartitionSpec as P

SEQ, DP = 32, 4
T = 256
WIDTH = 2048
HEADS = 64
PAIRS = 8
N = 128
PIECE = 64
PART = 32
MESH = pl.DeviceIdType.MESH
BF, F32 = jnp.bfloat16, jnp.float32
SCALE = 1.0 / 8192.0


def dot(a, b):
    return jnp.dot(a, b, preferred_element_type=F32)


def dot_nt(a, b):
    return lax.dot_general(a, b, (((1,), (1,)), ((), ())), preferred_element_type=F32)


def split3(v):
    hi = v.astype(BF).astype(F32)
    rest = v - hi
    mid = rest.astype(BF).astype(F32)
    return hi, mid, rest - mid


def tri_sum(tri, v):
    return sum(dot(tri, part.astype(BF)) for part in split3(v))


def send(src, dst, send_sem, recv_sem, device):
    pltpu.make_async_remote_copy(
        src_ref=src, dst_ref=dst, send_sem=send_sem, recv_sem=recv_sem,
        device_id=device, device_id_type=MESH,
    ).start()


def wait_for(ref, sem):
    pltpu.make_async_copy(ref, ref, sem).wait()


def loop(count, body):
    lax.fori_loop(0, count, lambda k, c: (body(k), c)[1], 0)


def pack_rows(v):
    return jnp.concatenate([v[:64], v[64:]], axis=1)


def unpack_rows(ref):
    return jnp.concatenate([ref[i][:, j : j + 64] for i in range(2) for j in (0, 64)], axis=0)


def kernel(
    x_hbm, tgt_hbm, sp_ref, st_ref, heads_ref,
    wbc_ref, wdt_ref, small_ref,
    x_ref, tgt_ref, w_bc, w_dt, xt_ref,
    m0_tmp, m0_sa, m0_ra, m0_sb, m0_rb, m0_f,
    m1_tmp, m1_sa, m1_ra, m1_sb, m1_rb, m1_f,
    d1_tmp, d1_sa, d1_ra, d1_sb, d1_rb, d1_f,
    m2_tmp, m2_sa, m2_ra, m2_sb, m2_rb, m2_f,
    m3_tmp, m3_sa, m3_ra, m3_sb, m3_rb, m3_f,
    weight_ref, stack_ref, skips_ref, rows_ref, cx_ref, sk_ref, sc_ref, l_ref, z_ref, err_ref, de_ref,
    sm_ref, dsc_ref, dc_ref, db_ref, k_ref, a_ref, dw_ref, acc_ref,
    ce_ref, es_ref, re_ref, sf_ref, rs_ref, gs_ref, rg_ref, sh_ref, rh_ref, dec_ref,
    z1_s, z1_r, x1_s, x1_r, z2_s, z2_r, x2_s, x2_r, wsb_ref, rwb_ref, sums_ref, sroot_ref, sdp_ref, sfin_ref,
    ssem, rsem, g_rsem, s_rsem, w_rsem, lsem, go,
):
    me, dq = lax.axis_index("seq"), lax.axis_index("dp")
    head0 = dq * (HEADS // DP)
    core = lax.rem(dq, 2)
    sibling = dq + 1 - 2 * core
    across = lax.rem(dq + 2, DP)

    def peer(k):
        return lax.rem(me + k, SEQ)

    def offset(dy, dx, dz):
        y, x, z = me // 16, lax.rem(me // 4, 4), lax.rem(me, 4)
        return lax.rem(y + dy, 2) * 16 + lax.rem(x + dx, 4) * 4 + lax.rem(z + dz, 4)

    def signal(sem, device):
        pl.semaphore_signal(sem, inc=1, device_id=device, device_id_type=MESH)

    def to_peers(start):
        def one(k):
            k = k + 1
            start(peer(k))

        loop(SEQ - 1, one)

    barrier = pltpu.get_barrier_semaphore()
    z_line = [(0, 0, k) for k in (1, 2, 3)]
    x_line = [(0, k, 0) for k in (1, 2, 3)]
    for k in range(1, DP):
        signal(barrier, (me, lax.rem(dq + k, DP)))
    for at in z_line + x_line + [(1, 0, 0)]:
        signal(barrier, (offset(*at), dq))
    own = pl.ds(pl.multiple_of(dq * WIDTH, WIDTH), WIDTH)
    load_x = pltpu.make_async_copy(x_hbm, x_ref, lsem.at[0])
    load_bc = pltpu.make_async_copy(sp_ref.at[own], w_bc, lsem.at[1])
    load_dt = pltpu.make_async_copy(st_ref.at[:, own], w_dt, lsem.at[2])
    load_tgt = pltpu.make_async_copy(tgt_hbm, tgt_ref, lsem.at[3])
    load_x.start()
    load_bc.start()
    load_dt.start()
    load_tgt.start()
    load_x.wait()
    load_bc.wait()
    load_dt.wait()

    class DpSum:
        def __init__(self, sem, tmp, sa, ra, sb, rb, f):
            self.sem, self.tmp, self.sa, self.ra, self.sb, self.rb, self.f = sem, tmp, sa, ra, sb, rb, f

        def send(self, src, dst, step, member):
            send(src, dst, ssem.at[self.sem + step], rsem.at[self.sem + step], (me, member))

        def first(self):
            self.sa[...] = self.tmp[1 - core].astype(self.sa.dtype)
            self.send(self.sa, self.ra, 0, sibling)

        def second(self):
            wait_for(self.ra, rsem.at[self.sem])
            chip = self.tmp[core] + self.ra[...].astype(F32)
            self.tmp[core] = chip
            self.sb[...] = chip.astype(self.sb.dtype)
            self.send(self.sb, self.rb, 1, across)

        def third(self):
            wait_for(self.rb, rsem.at[self.sem + 1])
            self.f[core] = (self.tmp[core] + self.rb[...].astype(F32)).astype(self.f.dtype)
            self.send(self.f.at[core], self.f.at[core], 2, sibling)

        def last(self):
            wait_for(self.f.at[0], rsem.at[self.sem + 2])

        def sent(self):
            for step, ref in enumerate((self.sa, self.sb, self.f.at[0])):
                wait_for(ref, ssem.at[self.sem + step])

    sum_b1 = DpSum(0, m0_tmp, m0_sa, m0_ra, m0_sb, m0_rb, m0_f)
    sum_c1 = DpSum(25, m1_tmp, m1_sa, m1_ra, m1_sb, m1_rb, m1_f)
    sum_dt = DpSum(3, d1_tmp, d1_sa, d1_ra, d1_sb, d1_rb, d1_f)
    sum_c = DpSum(6, m2_tmp, m2_sa, m2_ra, m2_sb, m2_rb, m2_f)
    sum_b = DpSum(9, m3_tmp, m3_sa, m3_ra, m3_sb, m3_rb, m3_f)

    x_all = x_ref[...]
    part_dt = dot_nt(x_all, w_dt[...])
    part_bc = dot(x_all, w_bc[...])
    for i in range(2):
        half = slice(128 * i, 128 * i + 128)
        d1_tmp[i] = pack_rows(part_dt[half])
        m0_tmp[i] = part_bc[half, :N]
        m1_tmp[i] = part_bc[half, N:]
    pl.semaphore_wait(barrier, DP - 1 + 7)
    sum_dt.first()
    sum_b1.first()
    sum_c1.first()
    for at in x_line:
        signal(go.at[0], (offset(*at), dq))
    sum_dt.second()
    sum_b1.second()
    sum_c1.second()
    pl.semaphore_wait(go.at[0], 3)
    signal(go.at[1], (offset(1, 0, 0), dq))
    sum_dt.third()
    sum_b1.third()
    sum_dt.last()

    pre = unpack_rows(d1_f) + heads_ref[1:2]
    dt = jnp.maximum(pre, 0.0) + jnp.log1p(jnp.exp(-jnp.abs(pre)))
    rate = jnp.exp(heads_ref[0:1])
    log_rate = -rate * dt
    row_i = lax.broadcasted_iota(jnp.int32, (T, T), 0)
    col_i = lax.broadcasted_iota(jnp.int32, (T, T), 1)
    tri = jnp.where(row_i >= col_i, 1.0, 0.0).astype(BF)
    cum = tri_sum(tri, log_rate)
    cend = cum[T - 1 : T]
    weight = dt * jnp.exp(cend - cum)
    high = weight.astype(BF).astype(F32)
    weight_ref[...] = jnp.concatenate([high, weight - high], axis=1).astype(BF)
    ce_ref[me] = jnp.concatenate([cend, cend], axis=1)
    sum_b1.last()
    b_in = m0_f[...].reshape(T, N)
    b_t = b_in.astype(F32).T.astype(BF)
    pl.semaphore_wait(go.at[1], 1)
    loop(SEQ - 1, lambda k: send(
        ce_ref.at[me], ce_ref.at[me], ssem.at[12], rsem.at[12], (peer(k + 1), dq)))
    sel_row = lax.rem(lax.broadcasted_iota(jnp.int32, (3 * HEADS, 2 * N), 0), HEADS)
    sel_col = lax.broadcasted_iota(jnp.int32, (3 * HEADS, 2 * N), 1) // N

    def cols(hp):
        return pl.ds(pl.multiple_of(hp * 2 * N, 2 * N), 2 * N)

    def pick(hp):
        return jnp.where(sel_row == head0 + 2 * hp + sel_col, 1.0, 0.0).astype(BF)

    def pair_of(group, k):
        return 4 * group + lax.rem(me // 8 + k, 4)

    def each_of(hp, body):
        def one(i):
            at = 8 * hp + lax.rem(me + i, 8)
            o = lax.rem(at, SEQ)

            @pl.when(o != me)
            def _():
                body(at, o)

        loop(8, one)

    def send_pair(hp, src, dst, sem):
        each_of(hp, lambda at, o: send(
            src.at[at], dst.at[SEQ * (hp // 4) + me],
            ssem.at[sem], g_rsem.at[2 * (sem - 13) + hp // 4], (o, dq)))

    def wait_pair(hp, ref, sems):
        mine = (SEQ * (hp // 4) + me) // 8 == hp

        @pl.when(mine)
        def _():
            wait_for(ref.at[pl.ds(8 * hp, 7)], sems.at[hp])

        @pl.when(jnp.logical_not(mine))
        def _():
            wait_for(ref.at[pl.ds(8 * hp, 8)], sems.at[hp])

    def send_all(group, src, dst, sem, sems, slot=None):
        def one(k):
            o = peer(k + 1)
            send(src.at[SEQ * group + o], dst.at[SEQ * group + me],
                 ssem.at[sem], sems.at[(SEQ * group + me) // 8 if slot is None else slot], (o, dq))

        loop(SEQ - 1, one)
        dst[SEQ * group + me] = src[SEQ * group + me]

    def put_pair(ref, hp, value):
        for i in range(8):
            ref[8 * hp + i] = value[
                (i % 4) * PART : (i % 4 + 1) * PART, (i // 4) * N : (i // 4 + 1) * N].astype(BF)

    def get_pair(ref, hp):
        v = ref[pl.ds(8 * hp, 8)]
        return jnp.concatenate([v[:4].reshape(N, N), v[4:].reshape(N, N)], axis=1)

    def wait_group(group, ref, sem):
        wait_for(ref.at[pl.ds(SEQ * group, SEQ - 1)], g_rsem.at[2 * (sem - 13) + group])

    wide_row = lax.rem(lax.broadcasted_iota(jnp.int32, (2 * HEADS, 8 * N), 0), HEADS)
    wide_col = lax.broadcasted_iota(jnp.int32, (2 * HEADS, 8 * N), 1) // N
    for group in range(2):
        sel = jnp.where(wide_row == head0 + 8 * group + wide_col, 1.0, 0.0).astype(BF)
        wide = dot(weight_ref[...], sel)
        at = slice(8 * N * group, 8 * N * (group + 1))
        sc = (x_ref[:, at].astype(F32) * wide).astype(BF)
        sc_ref[group] = sc
        term = dot(b_t, sc).astype(BF)
        for i in range(SEQ):
            es_ref[SEQ * group + i] = term[
                (i % 4) * PART : (i % 4 + 1) * PART, (i // 4) * N : (i // 4 + 1) * N]
        send_all(group, es_ref, re_ref, 13, g_rsem, group)

    sum_c1.third()
    stack_ref[0:T] = jnp.concatenate(split3(cum), axis=1).astype(BF)
    stack_ref[T : 2 * T] = jnp.concatenate(split3(dt), axis=1).astype(BF)
    rows_ref[...] = jnp.concatenate([cum, dt], axis=1).T
    sum_c1.last()
    c_out = m1_f[...].reshape(T, N)
    sm_ref[...] = jnp.where(row_i >= col_i, dot_nt(c_out, b_in), 0.0)
    skips_ref[...] = jnp.concatenate(
        split3(jnp.broadcast_to(heads_ref[2:3], (16, HEADS))), axis=1).astype(BF)

    def in_block(hp):
        sk_ref[hp] = dot(skips_ref[...], pick(hp))[:8]
        wide = dot(stack_ref[...], pick(hp))
        cx_ref[hp] = wide[:T]
        xd = (x_ref[:, cols(hp)].astype(F32) * wide[T:]).astype(BF)
        parts = []
        for j in range(2):
            cx = wide[:T, j * N : (j + 1) * N]
            gap = jnp.concatenate([cx, cx], axis=1) - rows_ref[pl.ds(head0 + 2 * hp + j, 1), :]
            decay = jnp.exp(jnp.minimum(gap, 0.0))
            l_ref[2 * hp + j] = decay.astype(BF)
            w = (decay * sm_ref[...]).astype(BF)
            parts.append(dot(w, xd[:, j * N : (j + 1) * N]))
        z_ref[hp] = jnp.concatenate(parts, axis=1)

    loop(PAIRS, in_block)
    load_tgt.wait()
    c_t = c_out.astype(F32).T.astype(BF)

    wait_for(ce_ref.at[pl.ds(0, SEQ - 1)], rsem.at[12])
    ends = jnp.concatenate(split3(ce_ref[...].reshape(SEQ, N)[:, :HEADS]), axis=1).astype(BF)
    for group in range(2):
        sel_own = jnp.where(
            sel_row[:, :N] == head0 + 8 * group + me // 4, 1.0, 0.0).astype(BF)
        dec_ref[SEQ * group : SEQ * group + SEQ] = jnp.exp(dot(ends, sel_own))

    def forward(at, state):
        sf_ref[at] = state.astype(BF)
        return dec_ref[pl.ds(at, 1), :] * state + re_ref[at].astype(F32)

    for group in range(2):
        wait_group(group, re_ref, 13)
        lax.fori_loop(SEQ * group, SEQ * group + SEQ, forward, jnp.zeros((PART, N), F32), unroll=8)
        send_all(group, sf_ref, rs_ref, 14, s_rsem)

    def turn(i):
        at = pl.ds(pl.multiple_of(i * 2 * N, 2 * N), 2 * N)
        xt_ref[at, :] = x_ref[:, at].astype(F32).T.astype(BF)

    loop(PAIRS, turn)
    acc_ref[...] = jnp.zeros_like(acc_ref)

    def errors(hp):
        at = cols(hp)
        wait_pair(hp, rs_ref, s_rsem)
        decay = jnp.exp(cx_ref[hp])
        z = z_ref[hp] + dot(c_out, get_pair(rs_ref, hp)) * decay
        z_ref[hp] = z
        err = (z + sk_ref[hp][:1] * x_ref[:, at].astype(F32)) - tgt_ref[:, at].astype(F32)
        err_ref[hp] = err
        de = (err * decay).astype(BF)
        de_ref[hp] = de
        put_pair(gs_ref, hp, dot(c_t, de))
        acc_ref[0:8] += jnp.sum((err * err).reshape(T // 8, 8, 2 * N), axis=0)

    for group in range(2):
        loop(4, lambda k: errors(pair_of(group, 4 - k)))
        send_all(group, gs_ref, rg_ref, 15, g_rsem, 4 + group)

    lane = lax.broadcasted_iota(jnp.int32, (T, HEADS), 1)
    lane1 = lax.broadcasted_iota(jnp.int32, (1, HEADS), 1)
    for ref in (dsc_ref, dc_ref, db_ref, k_ref, a_ref, dw_ref):
        ref[...] = jnp.zeros_like(ref)

    def grads_in_block(hp):
        at = cols(hp)
        xp = x_ref[:, at]
        err = err_ref[hp]
        errb = err.astype(BF)
        dc_ref[...] += dot_nt(de_ref[hp], get_pair(rs_ref, hp))
        rowed = err * z_ref[hp]
        skipped = jnp.sum(err * xp.astype(F32), axis=0, keepdims=True)
        for j in range(2):
            head = head0 + 2 * hp + j
            sub = slice(j * N, (j + 1) * N)
            dwd = dot_nt(errb[:, sub], xp[:, sub]) * l_ref[2 * hp + j].astype(F32)
            dsc_ref[...] += dwd * rows_ref[pl.ds(HEADS + head, 1), :]
            k_ref[pl.ds(head, 1), :] = jnp.sum(dwd * sm_ref[...], axis=0, keepdims=True)
            a_ref[...] += jnp.where(
                lane == head, jnp.sum(rowed[:, sub], axis=1, keepdims=True), 0.0)
            acc_ref[8:9, :HEADS] += jnp.where(
                lane1 == head, jnp.sum(skipped[:, sub], axis=1, keepdims=True), 0.0)

    loop(PAIRS, grads_in_block)
    dsc = jnp.where(row_i >= col_i, dsc_ref[...], 0.0)
    m2_tmp[...] = ((dc_ref[...] + dot(dsc.astype(BF), b_in)) * SCALE).reshape(2, 128, N)
    sum_c.first()
    db_ref[...] = dot(dsc.T.astype(BF), c_out)
    sum_c.second()
    k_cols = k_ref[...].T[:, :HEADS]
    def backward(i, state, group):
        at = SEQ * group + SEQ - 1 - i
        sh_ref[at] = state.astype(BF)
        return dec_ref[pl.ds(at, 1), :] * state + rg_ref[at].astype(F32)

    for group in range(2):
        wait_group(group, rg_ref, 15)
        lax.fori_loop(0, SEQ, functools.partial(backward, group=group),
                      jnp.zeros((PART, N), F32), unroll=8)
        send_all(group, sh_ref, rh_ref, 16, g_rsem, 6 + group)

    sum_c.third()
    sum_c.last()

    my_y, my_x, my_z = me // 16, lax.rem(me // 4, 4), lax.rem(me, 4)
    g_c = m2_f[...].reshape(T, N)
    for g in range(4):
        term = dot(xt_ref[512 * g : 512 * g + 512, :], g_c).astype(BF).reshape(8, PIECE, N)
        for i in range(8):
            y, x, z = g // 2, 2 * (g % 2) + i // 4, i % 4
            z1_s[z, 4 * y + x] = term[i, :32]
            x1_s[x, 4 * y + z] = term[i, 32:]
    for k in range(1, 4):
        to = lax.rem(my_z + k, 4)
        send(z1_s.at[to], z1_r.at[my_z], ssem.at[17], rsem.at[17], (offset(0, 0, k), dq))
        to = lax.rem(my_x + k, 4)
        send(x1_s.at[to], x1_r.at[my_x], ssem.at[18], rsem.at[18], (offset(0, k, 0), dq))
    z1_r[my_z] = z1_s[my_z]
    x1_r[my_x] = x1_s[my_x]
    planes = [(dy, d) for dy in (1, 0) for d in (2, 1, 3, 0)][:7]

    def on_plane(dy, mine, d):
        return 4 * lax.rem(my_y + dy, 2) + lax.rem(mine + d, 4)

    def lines_to_planes():
        wait_for(z1_r.at[pl.ds(0, 3)], rsem.at[17])
        z2_s[...] = sum(z1_r[i].astype(F32) for i in range(4)).astype(BF)
        wait_for(x1_r.at[pl.ds(0, 3)], rsem.at[18])
        x2_s[...] = sum(x1_r[i].astype(F32) for i in range(4)).astype(BF)
        at_z, at_x = on_plane(0, my_x, 0), on_plane(0, my_z, 0)
        for dy, d in planes:
            send(z2_s.at[on_plane(dy, my_x, d)], z2_r.at[at_z],
                 ssem.at[28], rsem.at[28], (offset(dy, d, 0), dq))
            send(x2_s.at[on_plane(dy, my_z, d)], x2_r.at[at_x],
                 ssem.at[29], rsem.at[29], (offset(dy, 0, d), dq))
        z2_r[at_z] = z2_s[at_z]
        x2_r[at_x] = x2_s[at_x]

    def half_of(piece, i):
        return wbc_ref.at[piece, pl.ds(32 * i, 32), pl.ds(N, N)]

    def planes_back():
        wait_for(z2_r.at[pl.ds(0, 7)], rsem.at[28])
        wait_for(x2_r.at[pl.ds(0, 7)], rsem.at[29])
        wbc_ref[me, 0:32, N:] = sum(z2_r[i].astype(F32) for i in range(8)).astype(BF)
        wbc_ref[me, 32:64, N:] = sum(x2_r[i].astype(F32) for i in range(8)).astype(BF)
        for dy, d in planes:
            send(half_of(me, 0), half_of(me, 0), ssem.at[30], rsem.at[30], (offset(dy, d, 0), dq))
            send(half_of(me, 1), half_of(me, 1), ssem.at[31], rsem.at[31], (offset(dy, 0, d), dq))

    def lines_back():
        wait_for(wbc_ref.at[pl.ds(0, 7), pl.ds(0, 32), pl.ds(N, N)], rsem.at[30])
        wait_for(wbc_ref.at[pl.ds(0, 7), pl.ds(0, 32), pl.ds(N, N)], rsem.at[31])

        def one(i):
            y, other = i // 4, lax.rem(i, 4)
            for k in range(1, 4):
                piece = half_of(16 * y + 4 * other + my_z, 0)
                send(piece, piece, ssem.at[32], rsem.at[32], (offset(0, 0, k), dq))
                piece = half_of(16 * y + 4 * my_x + other, 1)
                send(piece, piece, ssem.at[33], rsem.at[33], (offset(0, k, 0), dq))

        loop(8, one)

    sum_row = lax.broadcasted_iota(jnp.int32, (8 * N, HEADS), 0) // N
    sum_col = lax.broadcasted_iota(jnp.int32, (8 * N, HEADS), 1)
    for group in range(2):
        to_head = jnp.where(sum_col == head0 + 8 * group + sum_row, 1.0, 0.0).astype(BF)

        def by_head(v):
            high = v.astype(BF)
            return dot(high, to_head) + dot((v - high.astype(F32)).astype(BF), to_head)

        wait_group(group, rh_ref, 16)
        pairs = range(4 * group, 4 * group + 4)
        after = jnp.concatenate([get_pair(rh_ref, hp) for hp in pairs], axis=1)
        before = jnp.concatenate([get_pair(rs_ref, hp) for hp in pairs], axis=1)
        at = slice(8 * N * group, 8 * N * (group + 1))
        db_ref[...] += dot_nt(sc_ref[group], after)
        dw_ref[...] += by_head(dot(b_in, after) * x_ref[:, at].astype(F32))
        decayed = after.astype(F32) * before.astype(F32)
        acc_ref[16:24, :HEADS] += by_head(jnp.sum(decayed.reshape(16, 8, 8 * N), axis=0))

    left = jnp.exp(cend - cum)
    d_weight = dw_ref[...] * left
    d_gap = d_weight * dt
    d_end = jnp.sum(d_gap, axis=0, keepdims=True) + jnp.exp(cend) * jnp.sum(acc_ref[16:24, :HEADS], axis=0, keepdims=True)
    d_cum = a_ref[...] - k_cols * dt - d_gap
    tri_up = jnp.where(row_i <= col_i, 1.0, 0.0).astype(BF)
    d_log = tri_sum(tri_up, d_cum) + d_end
    d_dt = k_cols + d_weight - rate * d_log
    d_pre = d_dt / (1.0 + jnp.exp(-pre)) * SCALE
    for i in range(2):
        half = slice(128 * i, 128 * i + 128)
        m3_tmp[i, 0:128] = db_ref[half] * SCALE
        m3_tmp[i, 128:192] = pack_rows(d_pre[half])
    sum_b.first()
    loss = jnp.sum(jnp.sum(acc_ref[0:8], axis=0, keepdims=True), axis=1, keepdims=True)
    zero = jnp.zeros((1, HEADS), F32)
    small = jnp.concatenate([
        jnp.broadcast_to(loss * (SCALE * SCALE * 0.5), (1, HEADS)),
        jnp.sum(d_log * log_rate, axis=0, keepdims=True) * SCALE,
        jnp.sum(d_pre, axis=0, keepdims=True),
        acc_ref[8:9, :HEADS] * SCALE,
        zero, zero, zero, zero], axis=0)
    sums_ref[...] = jnp.concatenate([small, jnp.zeros_like(small)], axis=1)
    sum_b.second()

    @pl.when(me != 0)
    def _():
        send(sums_ref, sroot_ref.at[me], ssem.at[24], rsem.at[24], (0, dq))

    lines_to_planes()
    sum_b.third()
    sum_b.last()

    g_b = m3_f[:, 0:128].reshape(T, N)
    g_dt = unpack_rows(m3_f.at[:, pl.ds(128, 64)]).astype(F32).T.astype(BF)

    def terms_dt(g):
        wide = dot(g_dt, x_ref[:, pl.ds(pl.multiple_of(g * 512, 512), 512)]).astype(BF)
        for i in range(4):
            for j in range(2):
                wsb_ref[2, 4 * g + i + 16 * j] = wide[32 * j : 32 * j + 32, N * i : N * i + N]

    def send_terms(i):
        to_peers(lambda o: send(
            wsb_ref.at[i, o], rwb_ref.at[i, me], ssem.at[19], w_rsem.at[i], (o, dq)))
        rwb_ref[i, me] = wsb_ref[i, me]

    term = dot(xt_ref[...], g_b).astype(BF).reshape(SEQ, PIECE, N)
    for i in range(2):
        wsb_ref[i] = term[:, 32 * i : 32 * i + 32]
    send_terms(0)
    loop(4, terms_dt)
    send_terms(1)
    send_terms(2)

    @pl.when(me == 0)
    def _():
        sroot_ref[0] = sums_ref[...]
        wait_for(sroot_ref.at[pl.ds(0, SEQ - 1)], rsem.at[24])
        sdp_ref[dq] = jnp.sum(sroot_ref[...], axis=0)
        for k in range(1, DP):
            send(sdp_ref.at[dq], sdp_ref.at[dq], ssem.at[22], rsem.at[22],
                 (me, lax.rem(dq + k, DP)))

    own_parts = [wbc_ref.at[me, pl.ds(32 * i, 32), pl.ds(0, N)] for i in range(2)] + [
        wdt_ref.at[pl.ds(pl.multiple_of(32 * (me // 16), 32), 32),
                   pl.ds(pl.multiple_of(N * lax.rem(me, 16), N), N)]]

    def total_of(i):
        wait_for(rwb_ref.at[i, pl.ds(0, SEQ - 1)], w_rsem.at[i])
        total = lax.fori_loop(
            1, SEQ, lambda j, v: v + rwb_ref[i, j].astype(F32), rwb_ref[i, 0].astype(F32), unroll=31)
        own_parts[i][...] = total.astype(BF)
        to_peers(lambda o: send(
            own_parts[i], own_parts[i], ssem.at[20], rsem.at[19 + i], (o, dq)))

    total_of(0)
    planes_back()
    total_of(1)
    total_of(2)
    lines_back()

    @pl.when(me == 0)
    def _():
        wait_for(sdp_ref.at[pl.ds(0, DP - 1)], rsem.at[22])
        sfin_ref[...] = jnp.sum(sdp_ref[...], axis=0)
        loop(SEQ - 1, lambda k: send(
            sfin_ref, sfin_ref, ssem.at[23], rsem.at[23], (peer(k + 1), dq)))
        wait_for(sdp_ref.at[pl.ds(0, DP - 1)], ssem.at[22])
        wait_for(sroot_ref.at[pl.ds(0, SEQ - 1)], ssem.at[23])

    @pl.when(me != 0)
    def _():
        wait_for(sums_ref, ssem.at[24])
        wait_for(sfin_ref, rsem.at[23])

    small_ref[...] = sfin_ref[...]

    for one in (sum_b1, sum_c1, sum_dt, sum_c, sum_b):
        one.sent()
    pieces = pl.ds(0, SEQ - 1)
    both = pl.ds(0, 2 * SEQ - 2)
    wait_for(ce_ref.at[pieces], ssem.at[12])
    for sem, ref in ((13, es_ref), (14, sf_ref), (15, gs_ref), (16, sh_ref)):
        wait_for(ref.at[both], ssem.at[sem])
    for sem in (19, 20):
        for i in range(3):
            wait_for(wsb_ref.at[i, pieces], ssem.at[sem])
    for i in range(3):
        wait_for(wsb_ref.at[i, pieces], rsem.at[19 + i])
    for i in range(2):
        wait_for(z1_s.at[pl.ds(0, 3)], ssem.at[17 + i])
        wait_for(z2_s.at[pl.ds(0, 7)], ssem.at[28 + i])
        wait_for(z2_s.at[pl.ds(0, 7)], ssem.at[30 + i])
        wait_for(z1_s.at[pl.ds(0, 3)], ssem.at[32 + i])
        wait_for(z1_s.at[pl.ds(0, 3)], rsem.at[32 + i])


def widen(wbc_ref, wdt_ref, small_ref, bc_hbm, dt_hbm, *rest):
    outs, (bc_ref, dt_ref, loss_ref, heads_ref, sem) = rest[:4], rest[4:]
    copies = []

    def put(src, dst):
        copies.append(pltpu.make_async_copy(src, dst, sem.at[len(copies)]))
        copies[-1].start()

    loss_ref[...] = small_ref[0:1, 0:1]
    put(loss_ref, outs[0])
    for i in range(3):
        heads_ref[i] = small_ref[i + 1 : i + 2, :HEADS]
        put(heads_ref.at[i], outs[i + 1])
    dt_ref[...] = wdt_ref[...].astype(F32)
    put(dt_ref, dt_hbm)
    for i in range(4):
        bc_ref[i] = wbc_ref[8 * i : 8 * i + 8].astype(F32).reshape(512, 2 * N)
        put(bc_ref.at[i], bc_hbm.at[pl.ds(512 * i, 512)])
    for one in copies:
        one.wait()


def shards(teacher_rows, teacher_next, state_proj, step_proj, rate_log, step_bias, skip_gain):
    vmem = pl.BlockSpec(memory_space=pltpu.VMEM)
    hbm = pl.BlockSpec(memory_space=pl.ANY)

    def buf(*shape):
        return pltpu.VMEM(shape, BF)

    def f32(*shape):
        return pltpu.VMEM(shape, F32)

    def dp_bufs(rows, kind):
        return [f32(2, rows, N), kind(rows, N), kind(rows, N), buf(rows, N), buf(rows, N),
                kind(2, rows, N)]

    scratch = [
        buf(T, WIDTH), buf(T, WIDTH), buf(WIDTH, 2 * N), buf(HEADS, WIDTH), buf(WIDTH, T),
        *dp_bufs(128, buf), *dp_bufs(128, buf), *dp_bufs(64, f32), *dp_bufs(128, buf), *dp_bufs(192, buf),
        buf(T, 2 * HEADS), buf(2 * T, 3 * HEADS), buf(16, 3 * HEADS), f32(2 * HEADS, T),
        f32(PAIRS, T, 2 * N), f32(PAIRS, 8, 2 * N), buf(2, T, 8 * N),
        buf(2 * PAIRS, T, T), f32(PAIRS, T, 2 * N), f32(PAIRS, T, 2 * N), buf(PAIRS, T, 2 * N),
        f32(T, T), f32(T, T), f32(T, N), f32(T, N), f32(2 * HEADS, T), f32(T, HEADS), f32(T, HEADS),
        f32(24, 2 * N),
        f32(SEQ, 1, N), *[buf(2 * SEQ, PART, N) for _ in range(8)], f32(2 * SEQ, N),
        *[buf(4, 8, 32, N) for _ in range(4)], *[buf(8, 32, N) for _ in range(4)],
        buf(3, SEQ, 32, N), buf(3, SEQ, 32, N),
        f32(8, 128), f32(SEQ, 8, 128), f32(DP, 8, 128), f32(8, 128),
        pltpu.SemaphoreType.DMA((34,)), pltpu.SemaphoreType.DMA((34,)),
        pltpu.SemaphoreType.DMA((8,)), pltpu.SemaphoreType.DMA((PAIRS,)), pltpu.SemaphoreType.DMA((3,)),
        pltpu.SemaphoreType.DMA((4,)), pltpu.SemaphoreType.REGULAR((2,)),
    ]
    state_grad, step_grad, small = pl.pallas_call(
        kernel,
        out_shape=(
            jax.ShapeDtypeStruct((SEQ, PIECE, 2 * N), BF),
            jax.ShapeDtypeStruct((HEADS, WIDTH), BF),
            jax.ShapeDtypeStruct((8, 128), F32),
        ),
        in_specs=[hbm, hbm, hbm, hbm, vmem],
        out_specs=(vmem, vmem, vmem),
        scratch_shapes=scratch,
        compiler_params=pltpu.CompilerParams(
            collective_id=0, has_side_effects=True, vmem_limit_bytes=52 * 1024 * 1024),
    )(teacher_rows, teacher_next, state_proj, step_proj.T,
      jnp.stack([rate_log, step_bias, skip_gain]))
    heads = jax.ShapeDtypeStruct((1, HEADS), F32)
    state_grad, step_grad, loss, *sums = pl.pallas_call(
        widen,
        out_shape=(
            jax.ShapeDtypeStruct((WIDTH, 2 * N), F32),
            jax.ShapeDtypeStruct((HEADS, WIDTH), F32),
            jax.ShapeDtypeStruct((1, 1), F32), heads, heads, heads,
        ),
        in_specs=[vmem] * 3,
        out_specs=(hbm,) * 6,
        scratch_shapes=[f32(4, 512, 2 * N), f32(HEADS, WIDTH), f32(1, 1), f32(3, 1, HEADS),
                        pltpu.SemaphoreType.DMA((9,))],
        compiler_params=pltpu.CompilerParams(vmem_limit_bytes=16 * 1024 * 1024),
    )(state_grad, step_grad, small)
    return (loss[0, 0], state_grad, step_grad.T, *(v[0] for v in sums))


def solution(mesh):
    placed = (P("seq", "dp"), P("seq", "dp"), P(), P(), P(), P(), P())
    return jax.shard_map(
        shards,
        mesh=mesh,
        in_specs=placed,
        out_specs=(P(), P("dp", None), P("dp", None), P(), P(), P()),
        check_vma=False,
    )
```

```python
import functools

import jax
import jax.numpy as jnp
from jax import lax
from jax.experimental import pallas as pl
from jax.experimental.pallas import tpu as pltpu
from jax.sharding import PartitionSpec as P

SEQ, DP = 32, 4
T = 256
WIDTH = 2048
HEADS = 64
PAIRS = 8
N = 128
PIECE = 64
PART = 32
MESH = pl.DeviceIdType.MESH
BF, F32 = jnp.bfloat16, jnp.float32
SCALE = 1.0 / 8192.0


def dot(a, b):
    return jnp.dot(a, b, preferred_element_type=F32)


def dot_nt(a, b):
    return lax.dot_general(a, b, (((1,), (1,)), ((), ())), preferred_element_type=F32)


def split3(v):
    hi = v.astype(BF).astype(F32)
    rest = v - hi
    mid = rest.astype(BF).astype(F32)
    return hi, mid, rest - mid


def tri_sum(tri, v):
    return sum(dot(tri, part.astype(BF)) for part in split3(v))


def send(src, dst, send_sem, recv_sem, device):
    pltpu.make_async_remote_copy(
        src_ref=src, dst_ref=dst, send_sem=send_sem, recv_sem=recv_sem,
        device_id=device, device_id_type=MESH,
    ).start()


def wait_for(ref, sem):
    pltpu.make_async_copy(ref, ref, sem).wait()


def loop(count, body):
    lax.fori_loop(0, count, lambda k, c: (body(k), c)[1], 0)


def pack_rows(v):
    return jnp.concatenate([v[:64], v[64:]], axis=1)


def unpack_rows(ref):
    return jnp.concatenate([ref[i][:, j : j + 64] for i in range(2) for j in (0, 64)], axis=0)


def kernel(
    x_hbm, tgt_hbm, sp_ref, st_ref, heads_ref,
    wbc_ref, wdt_ref, small_ref,
    x_ref, tgt_ref, w_bc, w_dt, xt_ref,
    m0_tmp, m0_sa, m0_ra, m0_sb, m0_rb, m0_f,
    m1_tmp, m1_sa, m1_ra, m1_sb, m1_rb, m1_f,
    d1_tmp, d1_sa, d1_ra, d1_sb, d1_rb, d1_f,
    m2_tmp, m2_sa, m2_ra, m2_sb, m2_rb, m2_f,
    m3_tmp, m3_sa, m3_ra, m3_sb, m3_rb, m3_f,
    weight_ref, stack_ref, skips_ref, rows_ref, cx_ref, sk_ref, sc_ref, l_ref, z_ref, err_ref, de_ref,
    sm_ref, dsc_ref, dc_ref, db_ref, k_ref, a_ref, dw_ref, acc_ref,
    ce_ref, es_ref, re_ref, sf_ref, rs_ref, gs_ref, rg_ref, sh_ref, rh_ref, dec_ref,
    z1_s, z1_r, x1_s, x1_r, z2_s, z2_r, x2_s, x2_r, wsb_ref, rwb_ref, sums_ref, sroot_ref, sdp_ref, sfin_ref,
    ssem, rsem, g_rsem, s_rsem, w_rsem, lsem, go,
):
    me, dq = lax.axis_index("seq"), lax.axis_index("dp")
    head0 = dq * (HEADS // DP)
    core = lax.rem(dq, 2)
    sibling = dq + 1 - 2 * core
    across = lax.rem(dq + 2, DP)

    def peer(k):
        return lax.rem(me + k, SEQ)

    def offset(dy, dx, dz):
        y, x, z = me // 16, lax.rem(me // 4, 4), lax.rem(me, 4)
        return lax.rem(y + dy, 2) * 16 + lax.rem(x + dx, 4) * 4 + lax.rem(z + dz, 4)

    def signal(sem, device):
        pl.semaphore_signal(sem, inc=1, device_id=device, device_id_type=MESH)

    def to_peers(start):
        def one(k):
            k = k + 1
            start(peer(k))

        loop(SEQ - 1, one)

    barrier = pltpu.get_barrier_semaphore()
    z_line = [(0, 0, k) for k in (1, 2, 3)]
    x_line = [(0, k, 0) for k in (1, 2, 3)]
    for k in range(1, DP):
        signal(barrier, (me, lax.rem(dq + k, DP)))
    for at in z_line + x_line + [(1, 0, 0)]:
        signal(barrier, (offset(*at), dq))
    own = pl.ds(pl.multiple_of(dq * WIDTH, WIDTH), WIDTH)
    load_x = pltpu.make_async_copy(x_hbm, x_ref, lsem.at[0])
    load_bc = pltpu.make_async_copy(sp_ref.at[own], w_bc, lsem.at[1])
    load_dt = pltpu.make_async_copy(st_ref.at[:, own], w_dt, lsem.at[2])
    load_tgt = pltpu.make_async_copy(tgt_hbm, tgt_ref, lsem.at[3])
    load_x.start()
    load_bc.start()
    load_dt.start()
    load_tgt.start()
    load_x.wait()
    load_bc.wait()
    load_dt.wait()

    class DpSum:
        def __init__(self, sem, tmp, sa, ra, sb, rb, f):
            self.slot = 1 if sem == 25 else sem
            self.sem, self.tmp, self.sa, self.ra, self.sb, self.rb, self.f = sem, tmp, sa, ra, sb, rb, f

        def send(self, src, dst, step, member):
            send(src, dst, ssem.at[self.slot], rsem.at[self.sem + step], (me, member))

        def first(self):
            self.sa[...] = self.tmp[1 - core].astype(self.sa.dtype)
            self.send(self.sa, self.ra, 0, sibling)

        def second(self):
            wait_for(self.ra, rsem.at[self.sem])
            chip = self.tmp[core] + self.ra[...].astype(F32)
            self.tmp[core] = chip
            self.sb[...] = chip.astype(self.sb.dtype)
            self.send(self.sb, self.rb, 1, across)

        def third(self):
            wait_for(self.rb, rsem.at[self.sem + 1])
            self.f[core] = (self.tmp[core] + self.rb[...].astype(F32)).astype(self.f.dtype)
            self.send(self.f.at[core], self.f.at[core], 2, sibling)

        def last(self):
            wait_for(self.f.at[0], rsem.at[self.sem + 2])

        def sent(self):
            for step, ref in enumerate((self.sa, self.sb, self.f.at[0])):
                wait_for(ref, ssem.at[self.slot])

    sum_b1 = DpSum(0, m0_tmp, m0_sa, m0_ra, m0_sb, m0_rb, m0_f)
    sum_c1 = DpSum(25, m1_tmp, m1_sa, m1_ra, m1_sb, m1_rb, m1_f)
    sum_dt = DpSum(3, d1_tmp, d1_sa, d1_ra, d1_sb, d1_rb, d1_f)
    sum_c = DpSum(6, m2_tmp, m2_sa, m2_ra, m2_sb, m2_rb, m2_f)
    sum_b = DpSum(9, m3_tmp, m3_sa, m3_ra, m3_sb, m3_rb, m3_f)

    x_all = x_ref[...]
    part_dt = dot_nt(x_all, w_dt[...])
    part_bc = dot(x_all, w_bc[...])
    for i in range(2):
        half = slice(128 * i, 128 * i + 128)
        d1_tmp[i] = pack_rows(part_dt[half])
        m0_tmp[i] = part_bc[half, :N]
        m1_tmp[i] = part_bc[half, N:]
    pl.semaphore_wait(barrier, DP - 1 + 7)
    sum_dt.first()
    sum_b1.first()
    sum_c1.first()
    for at in x_line:
        signal(go.at[0], (offset(*at), dq))
    sum_dt.second()
    sum_b1.second()
    sum_c1.second()
    pl.semaphore_wait(go.at[0], 3)
    signal(go.at[1], (offset(1, 0, 0), dq))
    sum_dt.third()
    sum_b1.third()
    sum_dt.last()

    pre = unpack_rows(d1_f) + heads_ref[1:2]
    dt = jnp.maximum(pre, 0.0) + jnp.log1p(jnp.exp(-jnp.abs(pre)))
    rate = jnp.exp(heads_ref[0:1])
    log_rate = -rate * dt
    row_i = lax.broadcasted_iota(jnp.int32, (T, T), 0)
    col_i = lax.broadcasted_iota(jnp.int32, (T, T), 1)
    tri = jnp.where(row_i >= col_i, 1.0, 0.0).astype(BF)
    cum = tri_sum(tri, log_rate)
    cend = cum[T - 1 : T]
    weight = dt * jnp.exp(cend - cum)
    high = weight.astype(BF).astype(F32)
    weight_ref[...] = jnp.concatenate([high, weight - high], axis=1).astype(BF)
    ce_ref[me] = jnp.concatenate([cend, cend], axis=1)
    sum_b1.last()
    b_in = m0_f[...].reshape(T, N)
    b_t = b_in.astype(F32).T.astype(BF)
    pl.semaphore_wait(go.at[1], 1)
    loop(SEQ - 1, lambda k: send(
        ce_ref.at[me], ce_ref.at[me], ssem.at[12], rsem.at[12], (peer(k + 1), dq)))
    sel_row = lax.rem(lax.broadcasted_iota(jnp.int32, (3 * HEADS, 2 * N), 0), HEADS)
    sel_col = lax.broadcasted_iota(jnp.int32, (3 * HEADS, 2 * N), 1) // N

    def cols(hp):
        return pl.ds(pl.multiple_of(hp * 2 * N, 2 * N), 2 * N)

    def pick(hp):
        return jnp.where(sel_row == head0 + 2 * hp + sel_col, 1.0, 0.0).astype(BF)

    def pair_of(group, k):
        return 4 * group + lax.rem(me // 8 + k, 4)

    def each_of(hp, body):
        def one(i):
            at = 8 * hp + lax.rem(me + i, 8)
            o = lax.rem(at, SEQ)

            @pl.when(o != me)
            def _():
                body(at, o)

        loop(8, one)

    def send_pair(hp, src, dst, sem):
        each_of(hp, lambda at, o: send(
            src.at[at], dst.at[SEQ * (hp // 4) + me],
            ssem.at[sem], g_rsem.at[2 * (sem - 13) + hp // 4], (o, dq)))

    def wait_pair(hp, ref, sems):
        mine = (SEQ * (hp // 4) + me) // 8 == hp

        @pl.when(mine)
        def _():
            wait_for(ref.at[pl.ds(8 * hp, 7)], sems.at[hp])

        @pl.when(jnp.logical_not(mine))
        def _():
            wait_for(ref.at[pl.ds(8 * hp, 8)], sems.at[hp])

    def send_all(group, src, dst, sem, sems, slot=None):
        def one(k):
            o = peer(k + 1)
            send(src.at[SEQ * group + o], dst.at[SEQ * group + me],
                 ssem.at[sem], sems.at[(SEQ * group + me) // 8 if slot is None else slot], (o, dq))

        loop(SEQ - 1, one)
        dst[SEQ * group + me] = src[SEQ * group + me]

    def put_pair(ref, hp, value):
        for i in range(8):
            ref[8 * hp + i] = value[
                (i % 4) * PART : (i % 4 + 1) * PART, (i // 4) * N : (i // 4 + 1) * N].astype(BF)

    def get_pair(ref, hp):
        v = ref[pl.ds(8 * hp, 8)]
        return jnp.concatenate([v[:4].reshape(N, N), v[4:].reshape(N, N)], axis=1)

    def wait_group(group, ref, sem):
        wait_for(ref.at[pl.ds(SEQ * group, SEQ - 1)], g_rsem.at[2 * (sem - 13) + group])

    wide_row = lax.rem(lax.broadcasted_iota(jnp.int32, (2 * HEADS, 8 * N), 0), HEADS)
    wide_col = lax.broadcasted_iota(jnp.int32, (2 * HEADS, 8 * N), 1) // N
    for group in range(2):
        sel = jnp.where(wide_row == head0 + 8 * group + wide_col, 1.0, 0.0).astype(BF)
        wide = dot(weight_ref[...], sel)
        at = slice(8 * N * group, 8 * N * (group + 1))
        sc = (x_ref[:, at].astype(F32) * wide).astype(BF)
        sc_ref[group] = sc
        term = dot(b_t, sc).astype(BF)
        for i in range(SEQ):
            es_ref[SEQ * group + i] = term[
                (i % 4) * PART : (i % 4 + 1) * PART, (i // 4) * N : (i // 4 + 1) * N]
        send_all(group, es_ref, re_ref, 13, g_rsem, group)

    sum_c1.third()
    stack_ref[0:T] = jnp.concatenate(split3(cum), axis=1).astype(BF)
    stack_ref[T : 2 * T] = jnp.concatenate(split3(dt), axis=1).astype(BF)
    rows_ref[...] = jnp.concatenate([cum, dt], axis=1).T
    sum_c1.last()
    c_out = m1_f[...].reshape(T, N)
    sm_ref[...] = jnp.where(row_i >= col_i, dot_nt(c_out, b_in), 0.0)
    skips_ref[...] = jnp.concatenate(
        split3(jnp.broadcast_to(heads_ref[2:3], (16, HEADS))), axis=1).astype(BF)

    def in_block(hp):
        sk_ref[hp] = dot(skips_ref[...], pick(hp))[:8]
        wide = dot(stack_ref[...], pick(hp))
        cx_ref[hp] = wide[:T]
        xd = (x_ref[:, cols(hp)].astype(F32) * wide[T:]).astype(BF)
        parts = []
        for j in range(2):
            cx = wide[:T, j * N : (j + 1) * N]
            gap = jnp.concatenate([cx, cx], axis=1) - rows_ref[pl.ds(head0 + 2 * hp + j, 1), :]
            decay = jnp.exp(jnp.minimum(gap, 0.0))
            l_ref[2 * hp + j] = decay.astype(BF)
            w = (decay * sm_ref[...]).astype(BF)
            parts.append(dot(w, xd[:, j * N : (j + 1) * N]))
        z_ref[hp] = jnp.concatenate(parts, axis=1)

    loop(PAIRS, in_block)
    load_tgt.wait()
    c_t = c_out.astype(F32).T.astype(BF)

    wait_for(ce_ref.at[pl.ds(0, SEQ - 1)], rsem.at[12])
    ends = jnp.concatenate(split3(ce_ref[...].reshape(SEQ, N)[:, :HEADS]), axis=1).astype(BF)
    for group in range(2):
        sel_own = jnp.where(
            sel_row[:, :N] == head0 + 8 * group + me // 4, 1.0, 0.0).astype(BF)
        dec_ref[SEQ * group : SEQ * group + SEQ] = jnp.exp(dot(ends, sel_own))

    def forward(at, state):
        sf_ref[at] = state.astype(BF)
        return dec_ref[pl.ds(at, 1), :] * state + re_ref[at].astype(F32)

    for group in range(2):
        wait_group(group, re_ref, 13)
        lax.fori_loop(SEQ * group, SEQ * group + SEQ, forward, jnp.zeros((PART, N), F32), unroll=8)
        send_all(group, sf_ref, rs_ref, 14, s_rsem)

    def turn(i):
        at = pl.ds(pl.multiple_of(i * 2 * N, 2 * N), 2 * N)
        xt_ref[at, :] = x_ref[:, at].astype(F32).T.astype(BF)

    loop(PAIRS, turn)
    acc_ref[...] = jnp.zeros_like(acc_ref)

    def errors(hp):
        at = cols(hp)
        wait_pair(hp, rs_ref, s_rsem)
        decay = jnp.exp(cx_ref[hp])
        z = z_ref[hp] + dot(c_out, get_pair(rs_ref, hp)) * decay
        z_ref[hp] = z
        err = (z + sk_ref[hp][:1] * x_ref[:, at].astype(F32)) - tgt_ref[:, at].astype(F32)
        err_ref[hp] = err
        de = (err * decay).astype(BF)
        de_ref[hp] = de
        put_pair(gs_ref, hp, dot(c_t, de))
        acc_ref[0:8] += jnp.sum((err * err).reshape(T // 8, 8, 2 * N), axis=0)

    for group in range(2):
        loop(4, lambda k: errors(pair_of(group, 4 - k)))
        send_all(group, gs_ref, rg_ref, 15, g_rsem, 4 + group)

    lane = lax.broadcasted_iota(jnp.int32, (T, HEADS), 1)
    lane1 = lax.broadcasted_iota(jnp.int32, (1, HEADS), 1)
    for ref in (dsc_ref, dc_ref, db_ref, k_ref, a_ref, dw_ref):
        ref[...] = jnp.zeros_like(ref)

    def grads_in_block(hp):
        at = cols(hp)
        xp = x_ref[:, at]
        err = err_ref[hp]
        errb = err.astype(BF)
        dc_ref[...] += dot_nt(de_ref[hp], get_pair(rs_ref, hp))
        rowed = err * z_ref[hp]
        skipped = jnp.sum(err * xp.astype(F32), axis=0, keepdims=True)
        for j in range(2):
            head = head0 + 2 * hp + j
            sub = slice(j * N, (j + 1) * N)
            dwd = dot_nt(errb[:, sub], xp[:, sub]) * l_ref[2 * hp + j].astype(F32)
            dsc_ref[...] += dwd * rows_ref[pl.ds(HEADS + head, 1), :]
            k_ref[pl.ds(head, 1), :] = jnp.sum(dwd * sm_ref[...], axis=0, keepdims=True)
            a_ref[...] += jnp.where(
                lane == head, jnp.sum(rowed[:, sub], axis=1, keepdims=True), 0.0)
            acc_ref[8:9, :HEADS] += jnp.where(
                lane1 == head, jnp.sum(skipped[:, sub], axis=1, keepdims=True), 0.0)

    loop(PAIRS, grads_in_block)
    dsc = jnp.where(row_i >= col_i, dsc_ref[...], 0.0)
    m2_tmp[...] = ((dc_ref[...] + dot(dsc.astype(BF), b_in)) * SCALE).reshape(2, 128, N)
    sum_c.first()
    db_ref[...] = dot(dsc.T.astype(BF), c_out)
    sum_c.second()
    k_cols = k_ref[...].T[:, :HEADS]
    def backward(i, state, group):
        at = SEQ * group + SEQ - 1 - i
        sh_ref[at] = state.astype(BF)
        return dec_ref[pl.ds(at, 1), :] * state + rg_ref[at].astype(F32)

    for group in range(2):
        wait_group(group, rg_ref, 15)
        lax.fori_loop(0, SEQ, functools.partial(backward, group=group),
                      jnp.zeros((PART, N), F32), unroll=8)
        send_all(group, sh_ref, rh_ref, 16, g_rsem, 6 + group)

    sum_c.third()
    sum_c.last()

    my_y, my_x, my_z = me // 16, lax.rem(me // 4, 4), lax.rem(me, 4)
    g_c = m2_f[...].reshape(T, N)
    for g in range(4):
        term = dot(xt_ref[512 * g : 512 * g + 512, :], g_c).astype(BF).reshape(8, PIECE, N)
        for i in range(8):
            y, x, z = g // 2, 2 * (g % 2) + i // 4, i % 4
            z1_s[z, 4 * y + x] = term[i, :32]
            x1_s[x, 4 * y + z] = term[i, 32:]
    for k in range(1, 4):
        to = lax.rem(my_z + k, 4)
        send(z1_s.at[to], z1_r.at[my_z], ssem.at[17], rsem.at[17], (offset(0, 0, k), dq))
        to = lax.rem(my_x + k, 4)
        send(x1_s.at[to], x1_r.at[my_x], ssem.at[17], rsem.at[18], (offset(0, k, 0), dq))
    z1_r[my_z] = z1_s[my_z]
    x1_r[my_x] = x1_s[my_x]
    planes = [(dy, d) for dy in (1, 0) for d in (2, 1, 3, 0)][:7]

    def on_plane(dy, mine, d):
        return 4 * lax.rem(my_y + dy, 2) + lax.rem(mine + d, 4)

    def lines_to_planes():
        wait_for(z1_r.at[pl.ds(0, 3)], rsem.at[17])
        z2_s[...] = sum(z1_r[i].astype(F32) for i in range(4)).astype(BF)
        wait_for(x1_r.at[pl.ds(0, 3)], rsem.at[18])
        x2_s[...] = sum(x1_r[i].astype(F32) for i in range(4)).astype(BF)
        at_z, at_x = on_plane(0, my_x, 0), on_plane(0, my_z, 0)
        for dy, d in planes:
            send(z2_s.at[on_plane(dy, my_x, d)], z2_r.at[at_z],
                 ssem.at[2], rsem.at[28], (offset(dy, d, 0), dq))
            send(x2_s.at[on_plane(dy, my_z, d)], x2_r.at[at_x],
                 ssem.at[2], rsem.at[29], (offset(dy, 0, d), dq))
        z2_r[at_z] = z2_s[at_z]
        x2_r[at_x] = x2_s[at_x]

    def half_of(piece, i):
        return wbc_ref.at[piece, pl.ds(32 * i, 32), pl.ds(N, N)]

    def planes_back():
        wait_for(z2_r.at[pl.ds(0, 7)], rsem.at[28])
        wait_for(x2_r.at[pl.ds(0, 7)], rsem.at[29])
        wbc_ref[me, 0:32, N:] = sum(z2_r[i].astype(F32) for i in range(8)).astype(BF)
        wbc_ref[me, 32:64, N:] = sum(x2_r[i].astype(F32) for i in range(8)).astype(BF)
        for dy, d in planes:
            send(half_of(me, 0), half_of(me, 0), ssem.at[4], rsem.at[13], (offset(dy, d, 0), dq))
            send(half_of(me, 1), half_of(me, 1), ssem.at[4], rsem.at[14], (offset(dy, 0, d), dq))

    def lines_back():
        wait_for(wbc_ref.at[pl.ds(0, 7), pl.ds(0, 32), pl.ds(N, N)], rsem.at[13])
        wait_for(wbc_ref.at[pl.ds(0, 7), pl.ds(0, 32), pl.ds(N, N)], rsem.at[14])

        def one(i):
            y, other = i // 4, lax.rem(i, 4)
            for k in range(1, 4):
                piece = half_of(16 * y + 4 * other + my_z, 0)
                send(piece, piece, ssem.at[5], rsem.at[15], (offset(0, 0, k), dq))
                piece = half_of(16 * y + 4 * my_x + other, 1)
                send(piece, piece, ssem.at[5], rsem.at[16], (offset(0, k, 0), dq))

        loop(8, one)

    sum_row = lax.broadcasted_iota(jnp.int32, (8 * N, HEADS), 0) // N
    sum_col = lax.broadcasted_iota(jnp.int32, (8 * N, HEADS), 1)
    for group in range(2):
        to_head = jnp.where(sum_col == head0 + 8 * group + sum_row, 1.0, 0.0).astype(BF)

        def by_head(v):
            high = v.astype(BF)
            return dot(high, to_head) + dot((v - high.astype(F32)).astype(BF), to_head)

        wait_group(group, rh_ref, 16)
        pairs = range(4 * group, 4 * group + 4)
        after = jnp.concatenate([get_pair(rh_ref, hp) for hp in pairs], axis=1)
        before = jnp.concatenate([get_pair(rs_ref, hp) for hp in pairs], axis=1)
        at = slice(8 * N * group, 8 * N * (group + 1))
        db_ref[...] += dot_nt(sc_ref[group], after)
        dw_ref[...] += by_head(dot(b_in, after) * x_ref[:, at].astype(F32))
        decayed = after.astype(F32) * before.astype(F32)
        acc_ref[16:24, :HEADS] += by_head(jnp.sum(decayed.reshape(16, 8, 8 * N), axis=0))

    left = jnp.exp(cend - cum)
    d_weight = dw_ref[...] * left
    d_gap = d_weight * dt
    d_end = jnp.sum(d_gap, axis=0, keepdims=True) + jnp.exp(cend) * jnp.sum(acc_ref[16:24, :HEADS], axis=0, keepdims=True)
    d_cum = a_ref[...] - k_cols * dt - d_gap
    tri_up = jnp.where(row_i <= col_i, 1.0, 0.0).astype(BF)
    d_log = tri_sum(tri_up, d_cum) + d_end
    d_dt = k_cols + d_weight - rate * d_log
    d_pre = d_dt / (1.0 + jnp.exp(-pre)) * SCALE
    for i in range(2):
        half = slice(128 * i, 128 * i + 128)
        m3_tmp[i, 0:128] = db_ref[half] * SCALE
        m3_tmp[i, 128:192] = pack_rows(d_pre[half])
    sum_b.first()
    loss = jnp.sum(jnp.sum(acc_ref[0:8], axis=0, keepdims=True), axis=1, keepdims=True)
    zero = jnp.zeros((1, HEADS), F32)
    small = jnp.concatenate([
        jnp.broadcast_to(loss * (SCALE * SCALE * 0.5), (1, HEADS)),
        jnp.sum(d_log * log_rate, axis=0, keepdims=True) * SCALE,
        jnp.sum(d_pre, axis=0, keepdims=True),
        acc_ref[8:9, :HEADS] * SCALE,
        zero, zero, zero, zero], axis=0)
    sums_ref[...] = jnp.concatenate([small, jnp.zeros_like(small)], axis=1)
    sum_b.second()

    @pl.when(me != 0)
    def _():
        send(sums_ref, sroot_ref.at[me], ssem.at[7], rsem.at[24], (0, dq))

    lines_to_planes()
    sum_b.third()
    sum_b.last()

    g_b = m3_f[:, 0:128].reshape(T, N)
    g_dt = unpack_rows(m3_f.at[:, pl.ds(128, 64)]).astype(F32).T.astype(BF)

    def terms_dt(g):
        wide = dot(g_dt, x_ref[:, pl.ds(pl.multiple_of(g * 512, 512), 512)]).astype(BF)
        for i in range(4):
            for j in range(2):
                wsb_ref[2, 4 * g + i + 16 * j] = wide[32 * j : 32 * j + 32, N * i : N * i + N]

    def send_terms(i):
        to_peers(lambda o: send(
            wsb_ref.at[i, o], rwb_ref.at[i, me], ssem.at[19], w_rsem.at[i], (o, dq)))
        rwb_ref[i, me] = wsb_ref[i, me]

    term = dot(xt_ref[...], g_b).astype(BF).reshape(SEQ, PIECE, N)
    for i in range(2):
        wsb_ref[i] = term[:, 32 * i : 32 * i + 32]
    send_terms(0)
    loop(4, terms_dt)
    send_terms(1)
    send_terms(2)

    @pl.when(me == 0)
    def _():
        sroot_ref[0] = sums_ref[...]
        wait_for(sroot_ref.at[pl.ds(0, SEQ - 1)], rsem.at[24])
        sdp_ref[dq] = jnp.sum(sroot_ref[...], axis=0)
        for k in range(1, DP):
            send(sdp_ref.at[dq], sdp_ref.at[dq], ssem.at[10], rsem.at[22],
                 (me, lax.rem(dq + k, DP)))

    own_parts = [wbc_ref.at[me, pl.ds(32 * i, 32), pl.ds(0, N)] for i in range(2)] + [
        wdt_ref.at[pl.ds(pl.multiple_of(32 * (me // 16), 32), 32),
                   pl.ds(pl.multiple_of(N * lax.rem(me, 16), N), N)]]

    def total_of(i):
        wait_for(rwb_ref.at[i, pl.ds(0, SEQ - 1)], w_rsem.at[i])
        total = lax.fori_loop(
            1, SEQ, lambda j, v: v + rwb_ref[i, j].astype(F32), rwb_ref[i, 0].astype(F32), unroll=31)
        own_parts[i][...] = total.astype(BF)
        to_peers(lambda o: send(
            own_parts[i], own_parts[i], ssem.at[20], rsem.at[19 + i], (o, dq)))

    total_of(0)
    planes_back()
    total_of(1)
    total_of(2)
    lines_back()

    @pl.when(me == 0)
    def _():
        wait_for(sdp_ref.at[pl.ds(0, DP - 1)], rsem.at[22])
        sfin_ref[...] = jnp.sum(sdp_ref[...], axis=0)
        loop(SEQ - 1, lambda k: send(
            sfin_ref, sfin_ref, ssem.at[8], rsem.at[23], (peer(k + 1), dq)))
        wait_for(sdp_ref.at[pl.ds(0, DP - 1)], ssem.at[10])
        wait_for(sroot_ref.at[pl.ds(0, SEQ - 1)], ssem.at[8])

    @pl.when(me != 0)
    def _():
        wait_for(sums_ref, ssem.at[7])
        wait_for(sfin_ref, rsem.at[23])

    small_ref[...] = sfin_ref[...]

    for one in (sum_b1, sum_c1, sum_dt, sum_c, sum_b):
        one.sent()
    pieces = pl.ds(0, SEQ - 1)
    both = pl.ds(0, 2 * SEQ - 2)
    wait_for(ce_ref.at[pieces], ssem.at[12])
    for sem, ref in ((13, es_ref), (14, sf_ref), (15, gs_ref), (16, sh_ref)):
        wait_for(ref.at[both], ssem.at[sem])
    for sem in (19, 20):
        for i in range(3):
            wait_for(wsb_ref.at[i, pieces], ssem.at[sem])
    for i in range(3):
        wait_for(wsb_ref.at[i, pieces], rsem.at[19 + i])
    for i in range(2):
        wait_for(z1_s.at[pl.ds(0, 3)], ssem.at[17])
        wait_for(z2_s.at[pl.ds(0, 7)], ssem.at[2])
        wait_for(z2_s.at[pl.ds(0, 7)], ssem.at[4])
        wait_for(z1_s.at[pl.ds(0, 3)], ssem.at[5])
        wait_for(z1_s.at[pl.ds(0, 3)], rsem.at[15 + i])


def widen(wbc_ref, wdt_ref, small_ref, bc_hbm, dt_hbm, *rest):
    outs, (bc_ref, dt_ref, loss_ref, heads_ref, sem) = rest[:4], rest[4:]
    copies = []

    def put(src, dst):
        copies.append(pltpu.make_async_copy(src, dst, sem.at[len(copies)]))
        copies[-1].start()

    loss_ref[...] = small_ref[0:1, 0:1]
    put(loss_ref, outs[0])
    for i in range(3):
        heads_ref[i] = small_ref[i + 1 : i + 2, :HEADS]
        put(heads_ref.at[i], outs[i + 1])
    dt_ref[...] = wdt_ref[...].astype(F32)
    put(dt_ref, dt_hbm)
    for i in range(4):
        bc_ref[i] = wbc_ref[8 * i : 8 * i + 8].astype(F32).reshape(512, 2 * N)
        put(bc_ref.at[i], bc_hbm.at[pl.ds(512 * i, 512)])
    for one in copies:
        one.wait()


def shards(teacher_rows, teacher_next, state_proj, step_proj, rate_log, step_bias, skip_gain):
    vmem = pl.BlockSpec(memory_space=pltpu.VMEM)
    hbm = pl.BlockSpec(memory_space=pl.ANY)

    def buf(*shape):
        return pltpu.VMEM(shape, BF)

    def f32(*shape):
        return pltpu.VMEM(shape, F32)

    def dp_bufs(rows, kind):
        return [f32(2, rows, N), kind(rows, N), kind(rows, N), buf(rows, N), buf(rows, N),
                kind(2, rows, N)]

    scratch = [
        buf(T, WIDTH), buf(T, WIDTH), buf(WIDTH, 2 * N), buf(HEADS, WIDTH), buf(WIDTH, T),
        *dp_bufs(128, buf), *dp_bufs(128, buf), *dp_bufs(64, f32), *dp_bufs(128, buf), *dp_bufs(192, buf),
        buf(T, 2 * HEADS), buf(2 * T, 3 * HEADS), buf(16, 3 * HEADS), f32(2 * HEADS, T),
        f32(PAIRS, T, 2 * N), f32(PAIRS, 8, 2 * N), buf(2, T, 8 * N),
        buf(2 * PAIRS, T, T), f32(PAIRS, T, 2 * N), f32(PAIRS, T, 2 * N), buf(PAIRS, T, 2 * N),
        f32(T, T), f32(T, T), f32(T, N), f32(T, N), f32(2 * HEADS, T), f32(T, HEADS), f32(T, HEADS),
        f32(24, 2 * N),
        f32(SEQ, 1, N), *[buf(2 * SEQ, PART, N) for _ in range(8)], f32(2 * SEQ, N),
        *[buf(4, 8, 32, N) for _ in range(4)], *[buf(8, 32, N) for _ in range(4)],
        buf(3, SEQ, 32, N), buf(3, SEQ, 32, N),
        f32(8, 128), f32(SEQ, 8, 128), f32(DP, 8, 128), f32(8, 128),
        pltpu.SemaphoreType.DMA((21,)), pltpu.SemaphoreType.DMA((30,)),
        pltpu.SemaphoreType.DMA((8,)), pltpu.SemaphoreType.DMA((PAIRS,)), pltpu.SemaphoreType.DMA((3,)),
        pltpu.SemaphoreType.DMA((4,)), pltpu.SemaphoreType.REGULAR((2,)),
    ]
    state_grad, step_grad, small = pl.pallas_call(
        kernel,
        out_shape=(
            jax.ShapeDtypeStruct((SEQ, PIECE, 2 * N), BF),
            jax.ShapeDtypeStruct((HEADS, WIDTH), BF),
            jax.ShapeDtypeStruct((8, 128), F32),
        ),
        in_specs=[hbm, hbm, hbm, hbm, vmem],
        out_specs=(vmem, vmem, vmem),
        scratch_shapes=scratch,
        compiler_params=pltpu.CompilerParams(
            collective_id=0, has_side_effects=True, vmem_limit_bytes=52 * 1024 * 1024),
    )(teacher_rows, teacher_next, state_proj, step_proj.T,
      jnp.stack([rate_log, step_bias, skip_gain]))
    heads = jax.ShapeDtypeStruct((1, HEADS), F32)
    state_grad, step_grad, loss, *sums = pl.pallas_call(
        widen,
        out_shape=(
            jax.ShapeDtypeStruct((WIDTH, 2 * N), F32),
            jax.ShapeDtypeStruct((HEADS, WIDTH), F32),
            jax.ShapeDtypeStruct((1, 1), F32), heads, heads, heads,
        ),
        in_specs=[vmem] * 3,
        out_specs=(hbm,) * 6,
        scratch_shapes=[f32(4, 512, 2 * N), f32(HEADS, WIDTH), f32(1, 1), f32(3, 1, HEADS),
                        pltpu.SemaphoreType.DMA((9,))],
        compiler_params=pltpu.CompilerParams(vmem_limit_bytes=16 * 1024 * 1024),
    )(state_grad, step_grad, small)
    return (loss[0, 0], state_grad, step_grad.T, *(v[0] for v in sums))


def solution(mesh):
    placed = (P("seq", "dp"), P("seq", "dp"), P(), P(), P(), P(), P())
    return jax.shard_map(
        shards,
        mesh=mesh,
        in_specs=placed,
        out_specs=(P(), P("dp", None), P("dp", None), P(), P(), P()),
        check_vma=False,
    )
```
